32 devices in a mesh: seq: 4 (over y, core), fsdp: 8 (over z, x).
Axes of the slice: x: 2, y: 2, z: 4, core: 2. Of those that a mesh axis runs over, the one named last changes fastest.
Arguments:
- tokens: bfloat16 [8, 512, 2048], P('fsdp', 'seq'), may hold values from -6 to 6
- block_ids: int32 [8, 512], P('fsdp'), may hold values from 0 to 3, never falling along the last dimension, each value on 1 to 256 neighbouring positions
- gain_attn: bfloat16 [2048], P('fsdp'), may hold values from 0.5 to 1.5
- w_query: bfloat16 [2048, 2048], P('fsdp'), may hold values from -0.5 to 0.5
- w_key: bfloat16 [2048, 512], P('fsdp'), may hold values from -0.5 to 0.5
- w_value: bfloat16 [2048, 512], P('fsdp'), may hold values from -0.125 to 0.125
- w_out: bfloat16 [2048, 2048], P('fsdp'), may hold values from -1.5 to 1.5
- gain_mlp: bfloat16 [2048], P('fsdp'), may hold values from 0.5 to 1.5
- w_gate: bfloat16 [2048, 8192], P('fsdp'), may hold values from -0.125 to 0.125
- w_up: bfloat16 [2048, 8192], P('fsdp'), may hold values from -0.125 to 0.125
- w_down: bfloat16 [2048, 8192], P('fsdp'), may hold values from -0.5 to 0.5
- cotangent: bfloat16 [8, 512, 2048], P('fsdp', 'seq'), may hold values from -6 to 6
Outputs:
- mixed: bfloat16 [8, 512, 2048], P('fsdp', 'seq')
- grad_tokens: bfloat16 [8, 512, 2048], P('fsdp', 'seq')
- grad_gain_attn: float32 [2048], P('fsdp')
- grad_query: float32 [2048, 2048], P('fsdp')
- grad_key: float32 [2048, 512], P('fsdp')
- grad_value: float32 [2048, 512], P('fsdp')
- grad_out: float32 [2048, 2048], P('fsdp')
- grad_gain_mlp: float32 [2048], P('fsdp')
- grad_gate: float32 [2048, 8192], P('fsdp')
- grad_up: float32 [2048, 8192], P('fsdp')
- grad_down: float32 [2048, 8192], P('fsdp')
The draws below stay inside these ranges and needn't reach their ends.
Inputs may be any that keep to these rules, and one draw needn't show every extreme that they name: In each row of block_ids the block numbers never fall; each block holds 1 to 256 positions.
All inputs are finite; a program needn't handle non-finite values.
Results may differ from the reference program's by a relative error of at most 0.02.
Values may be sent and summed in bfloat16 or wider, within the bound.
A program may use at most 768 MiB of HBM per device.

```python
import math
import jax
import jax.numpy as jnp
import numpy as np
from jax import lax

D = 2048
H = 32
KVH = 8
HD = 64
FF = 8192
BLOCK = 256
SEQ_LEN = 512
SEQS = 8


def shard_levels(rng, shape, cuts, smallest, top_value):
    level = 1.0
    for position, parts in cuts:
        draws = jax.random.uniform(jax.random.fold_in(jax.random.fold_in(rng, 6), position), (parts,), jnp.float32, smallest / len(cuts), top_value / len(cuts))
        level = level * jnp.repeat(jnp.exp(draws), shape[position] // parts).reshape((-1,) + (1,) * (len(shape) - 1 - position))
    return level


def length_profile(number_of, total, bound, slope):
    portions = [(1 << 20) // math.isqrt(grade ** slope) + 1 for grade in range(2, number_of + 1)]
    surplus, given = total - bound - (number_of - 1), [1] * (number_of - 1)
    while surplus > 0:
        candidates = [i for i in range(number_of - 1) if given[i] < bound]
        whole, budget = sum([portions[i] for i in candidates]), surplus
        for i in candidates:
            more = min(bound - given[i], max(1, budget * portions[i] // whole), surplus)
            given[i] = given[i] + more
            surplus = surplus - more
    return np.array([bound] + given)


def uneven_parts(key, count, total, reach, skew):
    if count == 2:
        one = jax.random.randint(key, (), max(1, total - reach), min(reach, total - 1) + 1)
        return jnp.stack([one, total - one])
    lengths = jnp.asarray(length_profile(count, total, reach, skew), jnp.int32)
    couples = (count - 1) // 2
    donor, receiver = lengths[1:1 + 2 * couples:2], lengths[2:2 + 2 * couples:2]
    margin = jnp.minimum(donor - 1, reach - receiver)
    moved = jax.random.randint(jax.random.fold_in(key, 1), (couples,), 0, 1 << 20) % (margin + 1)
    lengths = lengths.at[1:1 + 2 * couples:2].set(donor - moved).at[2:2 + 2 * couples:2].set(receiver + moved)
    return lengths[jax.random.permutation(jax.random.fold_in(key, 2), count)]


def bell_draw(stream_key, extent, spread, limit, cuts=(), held_as=jnp.bfloat16):
    values = jax.random.normal(stream_key, extent, jnp.float32) * spread
    if len(cuts) > 0:
        values = shard_levels(stream_key, extent, cuts, -0.22, 0.18) * values
    return jnp.clip(values, min=-limit, max=limit).astype(held_as)


def setup_inputs(seed: int = 0) -> dict:
    key_list = jax.random.split(jax.random.key(seed), 13)
    return {
        "tokens": bell_draw(key_list[0], (SEQS, SEQ_LEN, D), 1.0, 6.0, ((0, 8), (1, 4))),
        "block_ids": jax.vmap(lambda own: jnp.searchsorted(jnp.cumsum(uneven_parts(own, 2 * SEQ_LEN // BLOCK, SEQ_LEN, BLOCK, 0)), jnp.arange(SEQ_LEN), side="right"))(jax.random.split(key_list[1], SEQS)).reshape((SEQS, SEQ_LEN)).astype(jnp.int32),
        "gain_attn": jnp.clip(1.0 + 0.1 * jax.random.normal(key_list[2], (D,), jnp.float32), 0.5, 1.5).astype(jnp.bfloat16),
        "w_query": bell_draw(key_list[3], (D, H * HD), (D // 16) ** -0.5, 0.5, ((0, 8),)),
        "w_key": bell_draw(key_list[4], (D, KVH * HD), (D // 16) ** -0.5, 0.5, ((0, 8),)),
        "w_value": bell_draw(key_list[5], (D, KVH * HD), D ** -0.5, 0.125, ((0, 8),)),
        "w_out": bell_draw(key_list[6], (D, H * HD), (H * HD // 128) ** -0.5, 1.5, ((0, 8),)),
        "gain_mlp": jnp.clip(1.0 + 0.1 * jax.random.normal(key_list[7], (D,), jnp.float32), 0.5, 1.5).astype(jnp.bfloat16),
        "w_gate": bell_draw(key_list[8], (D, FF), D ** -0.5, 0.125, ((0, 8),)),
        "w_up": bell_draw(key_list[9], (D, FF), D ** -0.5, 0.125, ((0, 8),)),
        "w_down": bell_draw(key_list[10], (D, FF), (FF // 64) ** -0.5, 0.5, ((0, 8),)),
        "cotangent": bell_draw(key_list[11], (SEQS, SEQ_LEN, D), 1.0, 6.0, ((0, 8), (1, 4))),
    }


EPSILON = 1e-05
RESIDUAL = 0.22

@jax.custom_vjp
def low(v):
    return lax.optimization_barrier(v.astype(jnp.bfloat16)).astype(jnp.float32)

@jax.custom_vjp
def low_back(v):
    return v

def low_keep(v):
    return (low(v), None)

def low_pass(kept, grad):
    return (grad,)

def back_keep(v):
    return (v, None)

def back_low(kept, grad):
    return (low(grad),)
low.defvjp(low_keep, low_pass)
low_back.defvjp(back_keep, back_low)

def matmul(left, right):
    return jnp.dot(left, right, precision=lax.Precision.HIGHEST)

def normed(values, gain):
    factor = lax.rsqrt(lax.optimization_barrier(jnp.mean(values * values, axis=-1, keepdims=True)) + EPSILON)
    return values * factor * gain

def attend_sequence(packed):
    query, keys, values, positions = packed
    length = query.shape[0]
    group = H // KVH
    span = min(512, length)
    query_blocks = query.reshape(length // span, span, KVH, group, HD)
    id_blocks = positions.reshape(length // span, span)
    key_heads = keys.reshape(length, KVH, HD)
    value_heads = values.reshape(length, KVH, HD)

    def one_block(pair):
        query_block, query_ids = pair
        scores = jnp.einsum('qkgd,tkd->kgqt', query_block, key_heads, precision=lax.Precision.HIGHEST) / HD
        scores = low_back(scores)
        allowed = positions[None, None, None, :] <= query_ids[None, None, :, None]
        scores = jnp.where(allowed, scores, -1e+30)
        shifted = jnp.exp(scores - lax.optimization_barrier(jnp.max(scores, axis=-1, keepdims=True)))
        probs = shifted / lax.optimization_barrier(jnp.sum(shifted, axis=-1, keepdims=True))
        result = jnp.einsum('kgqt,tkd->qkgd', low(probs), value_heads, precision=lax.Precision.HIGHEST)
        return result.reshape(span, H * HD)
    return lax.map(jax.checkpoint(one_block), (query_blocks, id_blocks)).reshape(length, H * HD)

def forward(tokens, gain_attn, w_query, w_key, w_value, w_out, gain_mlp, w_gate, w_up, w_down, block_ids):
    seqs, length, width = tokens.shape
    flat = tokens.reshape(seqs * length, width)
    first = low(normed(flat, gain_attn))
    query = low(low_back(matmul(first, w_query)))
    keys = low(low_back(matmul(first, w_key)))
    values = low(low_back(matmul(first, w_value)))
    attended = lax.map(jax.checkpoint(attend_sequence), (query.reshape(seqs, length, H * HD), keys.reshape(seqs, length, KVH * HD), values.reshape(seqs, length, KVH * HD), block_ids))
    attended = low(low_back(attended.reshape(seqs * length, H * HD)))
    branch = low_back(matmul(attended, w_out.T))
    middle = flat + RESIDUAL * branch
    second = low(normed(middle, gain_mlp))
    gate = low_back(matmul(second, w_gate))
    upward = low_back(matmul(second, w_up))
    hidden = low(jax.nn.silu(gate) * upward)
    down = low_back(matmul(hidden, w_down.T))
    return (middle + RESIDUAL * down).reshape(seqs, length, width)

def reference(tokens, block_ids, gain_attn, w_query, w_key, w_value, w_out, gain_mlp, w_gate, w_up, w_down, cotangent):
    floats = tuple((item.astype(jnp.float32) for item in (tokens, gain_attn, w_query, w_key, w_value, w_out, gain_mlp, w_gate, w_up, w_down)))

    def with_ids(*arrays):
        return forward(*arrays, block_ids)
    output, pullback = jax.vjp(with_ids, *floats)
    grads = pullback(cotangent.astype(jnp.float32))
    return (output.astype(jnp.bfloat16), grads[0].astype(jnp.bfloat16), grads[1], grads[2], grads[3], grads[4], grads[5], grads[6], grads[7], grads[8], grads[9])
```

```python
import functools

import jax
import jax.numpy as jnp
from jax import lax
from jax.experimental import pallas as pl
from jax.experimental.pallas import tpu as pltpu
from jax.sharding import PartitionSpec as P

H = 32
KVH = 8
HD = 64
EPSILON = 1e-05
RESIDUAL = 0.22
GROUP = 16
MESH = pl.DeviceIdType.MESH
PIECES = ((0, 48), (48, 48), (96, 32))
ORDERS = ((1, 2, 3), (2, 3, 1), (3, 1, 2))


def dot(left, right):
    return jnp.dot(left, right, preferred_element_type=jnp.float32)


def dot_cols(left, right):
    return lax.dot_general(
        left, right, (((1,), (1,)), ((), ())), preferred_element_type=jnp.float32
    )


def dot_rows(left, right):
    return lax.dot_general(
        left, right, (((0,), (0,)), ((), ())), preferred_element_type=jnp.float32
    )


def rms_factor(values):
    return lax.rsqrt(jnp.mean(values * values, axis=1, keepdims=True) + EPSILON)


def norm_back(grad_normed, values, factor, gain):
    weighted = grad_normed * gain
    centre = jnp.mean(weighted * values, axis=1, keepdims=True)
    return factor * weighted - values * (factor * factor * factor) * centre


class Layout:
    def __init__(self, seq_count, fsdp_count):
        self.seq = seq_count
        self.fsdp = fsdp_count
        self.share = GROUP // seq_count
        self.seq_bits = seq_count.bit_length() - 1

    def member(self):
        return lax.axis_index("seq") + self.seq * (lax.axis_index("fsdp") % self.share)

    def device(self, mask):
        low, high = mask % self.seq, mask // self.seq
        return {
            "seq": jnp.bitwise_xor(lax.axis_index("seq"), low),
            "fsdp": jnp.bitwise_xor(lax.axis_index("fsdp"), high),
        }


def span_mask(dims):
    return sum(1 << d for d in dims)


def greet(layout):
    barrier = pltpu.get_barrier_semaphore()
    for bit in range(4):
        pl.semaphore_signal(
            barrier, inc=1, device_id=layout.device(1 << bit), device_id_type=MESH
        )
    pl.semaphore_wait(barrier, 4)


def gather_kernel(layout, rows, x_ref, o_ref, send, recv, core_send, core_recv, own_sem):
    greet(layout)
    me = layout.member()

    def place(mask, piece):
        start, size = PIECES[piece]
        block = jnp.bitwise_xor(me, mask)
        return o_ref.at[pl.ds(pl.multiple_of(block * rows + start, 16), size)]

    def own(piece):
        start, size = PIECES[piece]
        return x_ref.at[pl.ds(start, size)]

    sent, relayed = [], []

    def push(mask, piece, slot, dim):
        copy = pltpu.make_async_remote_copy(
            src_ref=own(piece) if mask == 0 else place(mask, piece),
            dst_ref=place(mask, piece),
            send_sem=send.at[piece, slot],
            recv_sem=recv.at[piece, slot],
            device_id=layout.device(1 << dim),
            device_id_type=MESH,
        )
        copy.start()
        sent.append(copy)
        return copy

    def relay(mask, piece, slot):
        copy = pltpu.make_async_remote_copy(
            src_ref=own(piece) if mask == 0 else place(mask, piece),
            dst_ref=place(mask, piece),
            send_sem=core_send.at[piece, slot],
            recv_sem=core_recv.at[piece, slot],
            device_id=layout.device(1),
            device_id_type=MESH,
        )
        copy.start()
        sent.append(copy)
        relayed.append(copy)

    first, second, third = {}, {}, {}
    for piece, (a, b, c) in enumerate(ORDERS):
        first[piece] = push(0, piece, 0, a)
    for piece, (a, b, c) in enumerate(ORDERS):
        second[piece] = [push(0, piece, 1, b)]
    for piece, (a, b, c) in enumerate(ORDERS):
        third[piece] = [push(0, piece, 3, c)]
    local = pltpu.make_async_copy(x_ref, o_ref.at[pl.ds(pl.multiple_of(me * rows, 16), rows)], own_sem)
    local.start()
    for piece in range(3):
        relay(0, piece, 0)
    for piece, (a, b, c) in enumerate(ORDERS):
        first[piece].wait_recv()
        mask = span_mask((a,))
        second[piece].append(push(mask, piece, 2, b))
        third[piece].append(push(mask, piece, 4, c))
        relay(mask, piece, 1)
    for piece, (a, b, c) in enumerate(ORDERS):
        second[piece][0].wait_recv()
        mask = span_mask((b,))
        third[piece].append(push(mask, piece, 5, c))
        relay(mask, piece, 2)
    for piece, (a, b, c) in enumerate(ORDERS):
        second[piece][1].wait_recv()
        mask = span_mask((a, b))
        third[piece].append(push(mask, piece, 6, c))
        relay(mask, piece, 3)
    for turn, dims in enumerate(((2,), (0, 2), (1, 2), (0, 1, 2))):
        for piece, order in enumerate(ORDERS):
            third[piece][turn].wait_recv()
            relay(span_mask([order[d] for d in dims]), piece, 4 + turn)
    for copy in sent:
        copy.wait_send()
    for copy in relayed:
        copy.wait_recv()
    local.wait()


def token_gather(layout, block):
    rows, width = block.shape
    return pl.pallas_call(
        functools.partial(gather_kernel, layout, rows),
        out_shape=jax.ShapeDtypeStruct((GROUP * rows, width), block.dtype),
        in_specs=[pl.BlockSpec(memory_space=pl.ANY)],
        out_specs=pl.BlockSpec(memory_space=pl.ANY),
        scratch_shapes=[
            pltpu.SemaphoreType.DMA((3, 7)),
            pltpu.SemaphoreType.DMA((3, 7)),
            pltpu.SemaphoreType.DMA((3, 8)),
            pltpu.SemaphoreType.DMA((3, 8)),
            pltpu.SemaphoreType.DMA,
        ],
        compiler_params=pltpu.CompilerParams(collective_id=1, has_side_effects=True),
        name="token_gather",
    )(block)


def scatter_kernel(
    layout, rows, p_ref, o_ref, core_in, acc, arrive, core_send, core_recv, send, recv
):
    greet(layout)
    me = layout.member()
    masks = (14, 12, 10, 6, 8, 4, 2, 0)

    def rows_of(mask):
        return pl.ds(pl.multiple_of(jnp.bitwise_xor(me, mask) * rows, 16), rows)

    core = []
    for mask in masks:
        copy = pltpu.make_async_remote_copy(
            src_ref=p_ref.at[rows_of(mask ^ 1)],
            dst_ref=core_in.at[mask // 2],
            send_sem=core_send.at[mask // 2],
            recv_sem=core_recv.at[mask // 2],
            device_id=layout.device(1),
            device_id_type=MESH,
        )
        copy.start()
        core.append(copy)

    def push(piece, mask, dim, slot):
        start, size = PIECES[piece]
        copy = pltpu.make_async_remote_copy(
            src_ref=acc.at[mask // 2, pl.ds(start, size)],
            dst_ref=arrive.at[slot, pl.ds(start, size)],
            send_sem=send.at[piece, slot],
            recv_sem=recv.at[piece, slot],
            device_id=layout.device(1 << dim),
            device_id_type=MESH,
        )
        copy.start()
        return copy

    one, two, three = {}, {}, {}
    for mask, copy in zip(masks, core):
        copy.wait_recv()
        acc[mask // 2] = (
            p_ref[rows_of(mask)].astype(jnp.float32) + core_in[mask // 2].astype(jnp.float32)
        ).astype(jnp.bfloat16)
        for piece, (a, b, c) in enumerate(ORDERS):
            if mask & (1 << a):
                rest = mask ^ (1 << a)
                slot = (1 if rest & (1 << b) else 0) + (2 if rest & (1 << c) else 0)
                one[piece, slot] = push(piece, mask, a, slot)

    def add(piece, slot, mask):
        start, size = PIECES[piece]
        own = acc[mask // 2, pl.ds(start, size)].astype(jnp.float32)
        return own + arrive[slot, pl.ds(start, size)].astype(jnp.float32)

    def keep(piece, slot, mask):
        start, size = PIECES[piece]
        acc[mask // 2, pl.ds(start, size)] = add(piece, slot, mask).astype(jnp.bfloat16)

    for piece, (a, b, c) in enumerate(ORDERS):
        for slot, mask in ((3, span_mask((b, c))), (1, span_mask((b,)))):
            one[piece, slot].wait_recv()
            keep(piece, slot, mask)
            two[piece, slot] = push(piece, mask, b, 4 + slot // 2)
    for piece, (a, b, c) in enumerate(ORDERS):
        mask = span_mask((c,))
        one[piece, 2].wait_recv()
        keep(piece, 2, mask)
        two[piece, 3].wait_recv()
        keep(piece, 5, mask)
        three[piece] = push(piece, mask, c, 6)
    for piece, (a, b, c) in enumerate(ORDERS):
        start, size = PIECES[piece]
        one[piece, 0].wait_recv()
        two[piece, 1].wait_recv()
        partial = add(piece, 0, 0) + arrive[4, pl.ds(start, size)].astype(jnp.float32)
        three[piece].wait_recv()
        o_ref[pl.ds(start, size)] = partial + arrive[6, pl.ds(start, size)].astype(jnp.float32)
    for copy in core + list(one.values()) + list(two.values()) + list(three.values()):
        copy.wait_send()


def token_scatter(layout, partial):
    rows, width = partial.shape[0] // GROUP, partial.shape[1]
    return pl.pallas_call(
        functools.partial(scatter_kernel, layout, rows),
        out_shape=jax.ShapeDtypeStruct((rows, width), jnp.float32),
        in_specs=[pl.BlockSpec(memory_space=pltpu.VMEM)],
        out_specs=pl.BlockSpec(memory_space=pltpu.VMEM),
        scratch_shapes=[
            pltpu.VMEM((8, rows, width), jnp.bfloat16),
            pltpu.VMEM((8, rows, width), jnp.bfloat16),
            pltpu.VMEM((7, rows, width), jnp.bfloat16),
            pltpu.SemaphoreType.DMA((8,)),
            pltpu.SemaphoreType.DMA((8,)),
            pltpu.SemaphoreType.DMA((3, 7)),
            pltpu.SemaphoreType.DMA((3, 7)),
        ],
        compiler_params=pltpu.CompilerParams(
            collective_id=2, has_side_effects=True, vmem_limit_bytes=48 * 1024 * 1024
        ),
        name="token_scatter",
    )(partial)


def softmax(query, keys, query_ids, key_ids):
    scores = dot_cols(query, keys) * (1.0 / HD)
    scores = jnp.where(key_ids <= query_ids, scores, -1e30)
    shifted = jnp.exp(scores - jnp.max(scores, axis=1, keepdims=True))
    return shifted / jnp.sum(shifted, axis=1, keepdims=True)


def attend_kernel(heads, q_ref, kv_ref, row_ref, col_ref, o_ref):
    base = heads * HD
    keys = kv_ref[:, base : base + HD]
    values = kv_ref[:, base + HD : base + 2 * HD]
    outs = []
    for head in range(heads):
        query = q_ref[:, head * HD : (head + 1) * HD]
        probs = softmax(query, keys, col_ref[0], row_ref[0])
        outs.append(dot(probs.astype(jnp.bfloat16), values))
    o_ref[...] = jnp.concatenate(outs, axis=1).astype(jnp.bfloat16)


def attend_back_kernel(heads, q_ref, kv_ref, row_ref, col_ref, g_ref, o_ref, grad_kv):
    step = pl.program_id(1)
    span, length = q_ref.shape[0], kv_ref.shape[0]
    base = heads * HD
    keys = kv_ref[:, base : base + HD]
    values = kv_ref[:, base + HD : base + 2 * HD]
    grads, grad_keys, grad_values = [], 0.0, 0.0
    for head in range(heads):
        query = q_ref[:, head * HD : (head + 1) * HD]
        grad = g_ref[:, head * HD : (head + 1) * HD]
        probs = softmax(query, keys, col_ref[0], row_ref[0])
        grad_probs = dot_cols(grad, values)
        centre = jnp.sum(probs * grad_probs, axis=1, keepdims=True)
        grad_scores = (probs * (grad_probs - centre)).astype(jnp.bfloat16)
        grads.append(dot(grad_scores, keys) * (1.0 / HD))
        grad_keys = grad_keys + dot_rows(grad_scores, query) * (1.0 / HD)
        grad_values = grad_values + dot_rows(probs.astype(jnp.bfloat16), grad)
    both = jnp.concatenate([grad_keys, grad_values], axis=1)

    @pl.when(step == 0)
    def _():
        grad_kv[...] = both

    @pl.when(step > 0)
    def _():
        grad_kv[...] += both

    start = pl.multiple_of(step * span, span)
    o_ref[pl.ds(start, span), :base] = jnp.concatenate(grads, axis=1).astype(jnp.bfloat16)

    @pl.when(step == pl.num_programs(1) - 1)
    def _():
        o_ref[:, base:] = grad_kv[...].astype(jnp.bfloat16)


def attention_specs(qkv, ids, heads):
    count, length = ids.shape
    span = min(512, length)
    blocks = length // span
    width = qkv.shape[1]
    specs = [
        pl.BlockSpec((span, width), lambda i, j: (i * blocks + j, 0)),
        pl.BlockSpec((length, width), lambda i, j: (i, 0)),
        pl.BlockSpec((1, 1, length), lambda i, j: (i, 0, 0)),
        pl.BlockSpec((1, span, 1), lambda i, j: (i, j, 0)),
    ]
    args = (qkv, qkv, ids[:, None, :], ids[:, :, None])
    return (count, blocks), span, length, specs, args


def attend(qkv, ids, heads):
    grid, span, length, specs, args = attention_specs(qkv, ids, heads)
    return pl.pallas_call(
        functools.partial(attend_kernel, heads),
        grid=grid,
        in_specs=specs,
        out_specs=pl.BlockSpec((span, heads * HD), lambda i, j: (i * grid[1] + j, 0)),
        out_shape=jax.ShapeDtypeStruct((qkv.shape[0], heads * HD), jnp.bfloat16),
        compiler_params=pltpu.CompilerParams(vmem_limit_bytes=48 * 1024 * 1024),
        name="attend",
    )(*args)


def attend_back(qkv, ids, grad, heads):
    grid, span, length, specs, args = attention_specs(qkv, ids, heads)
    width = qkv.shape[1]
    return pl.pallas_call(
        functools.partial(attend_back_kernel, heads),
        grid=grid,
        in_specs=specs
        + [pl.BlockSpec((span, heads * HD), lambda i, j: (i * grid[1] + j, 0))],
        out_specs=pl.BlockSpec((length, width), lambda i, j: (i, 0)),
        out_shape=jax.ShapeDtypeStruct(qkv.shape, jnp.bfloat16),
        scratch_shapes=[pltpu.VMEM((length, 2 * HD), jnp.float32)],
        compiler_params=pltpu.CompilerParams(vmem_limit_bytes=48 * 1024 * 1024),
        name="attend_back",
    )(*args, grad)


def swap(array, axis, size, mask):
    return lax.ppermute(array, axis, [(i, i ^ mask) for i in range(size)])


def gather_seq(layout, array):
    me = lax.axis_index("seq")
    stack = array[None]
    for bit in reversed(range(layout.seq_bits)):
        other = swap(stack, "seq", layout.seq, 1 << bit)
        upper = (me >> bit) % 2 == 1
        pair = jnp.stack([jnp.where(upper, other, stack), jnp.where(upper, stack, other)], axis=1)
        stack = pair.reshape((-1,) + array.shape)
    return stack


def slices(array, start, size):
    return lax.dynamic_slice_in_dim(array, start, size, axis=1)


def body(
    tokens,
    block_ids,
    gain_attn,
    w_query,
    w_key,
    w_value,
    w_out,
    gain_mlp,
    w_gate,
    w_up,
    w_down,
    cotangent,
):
    layout = Layout(lax.axis_size("seq"), lax.axis_size("fsdp"))
    fsdp, share = layout.fsdp, layout.share
    seq_me, fsdp_me = lax.axis_index("seq"), lax.axis_index("fsdp")
    rows, width = tokens.shape[1], tokens.shape[2]
    depth = w_gate.shape[0]
    hidden_cols = w_gate.shape[1] // GROUP
    heads = H // GROUP
    query_cols = heads * HD
    kv_share = GROUP // KVH
    column_group = seq_me * share + fsdp_me % share

    def attn_part(target):
        kv = (target // kv_share) * HD
        return jnp.concatenate(
            [
                slices(w_query, target * query_cols, query_cols),
                slices(w_key, kv, HD),
                slices(w_value, kv, HD),
                slices(w_out, target * query_cols, query_cols),
                jnp.broadcast_to(gain_attn[:, None], (depth, 64)),
                jnp.broadcast_to(gain_mlp[:, None], (depth, 64)),
            ],
            axis=1,
        )

    def in_part(target):
        start = target * hidden_cols
        return jnp.concatenate(
            [slices(w_gate, start, hidden_cols), slices(w_up, start, hidden_cols)], axis=1
        )

    def down_part(target):
        return slices(w_down, target * hidden_cols, hidden_cols)

    def collect(part, after=None):
        whole = None
        for mask in range(fsdp):
            target = seq_me * share + jnp.bitwise_xor(fsdp_me, mask) % share
            piece = part(target)
            if mask:
                if after is not None:
                    piece, _ = lax.optimization_barrier((piece, after))
                piece = swap(piece, "fsdp", fsdp, mask)
            if whole is None:
                whole = jnp.zeros((fsdp * piece.shape[0], piece.shape[1]), piece.dtype)
            whole = lax.dynamic_update_slice_in_dim(
                whole, piece, jnp.bitwise_xor(fsdp_me, mask) * depth, axis=0
            )
        return whole

    attn_all = collect(attn_part)
    x_all = token_gather(layout, tokens[0])
    in_all = collect(in_part, attn_all)
    down_all = collect(down_part, attn_all)
    w_in = attn_all[:, : query_cols + 2 * HD]
    w_back = attn_all[:, query_cols + 2 * HD : 2 * query_cols + 2 * HD]
    attn_gain = attn_all[:, 2 * query_cols + 2 * HD].astype(jnp.float32)[None]
    mlp_gain = attn_all[:, 2 * query_cols + 2 * HD + 64].astype(jnp.float32)[None]

    id_rows = [block_ids]
    for bit in range(share.bit_length() - 1):
        id_rows = id_rows + [swap(r, "fsdp", fsdp, 1 << bit) for r in id_rows]
    ids = jnp.zeros((share, block_ids.shape[1]), block_ids.dtype)
    for mask, row in enumerate(id_rows):
        ids = lax.dynamic_update_slice_in_dim(
            ids, row, jnp.bitwise_xor(fsdp_me % share, mask), axis=0
        )

    inputs_all = x_all.astype(jnp.float32)
    normed_one = (inputs_all * rms_factor(inputs_all) * attn_gain).astype(jnp.bfloat16)
    qkv = dot(normed_one, w_in).astype(jnp.bfloat16)
    attended = attend(qkv, ids, heads)
    branch = token_scatter(layout, dot_cols(attended, w_back).astype(jnp.bfloat16))
    inputs = tokens[0].astype(jnp.float32)
    middle = inputs + RESIDUAL * branch
    factor_two = rms_factor(middle)
    normed_two = token_gather(
        layout, (middle * factor_two * mlp_gain).astype(jnp.bfloat16)
    )
    gate_up = dot(normed_two, in_all)
    gate, upward = gate_up[:, :hidden_cols], gate_up[:, hidden_cols:]
    sigma = jax.nn.sigmoid(gate)
    hidden = (gate * sigma * upward).astype(jnp.bfloat16)
    grad_all = token_gather(layout, cotangent[0])
    grad_down_in = (RESIDUAL * grad_all.astype(jnp.float32)).astype(jnp.bfloat16)
    grad_hidden = dot(grad_down_in, down_all)
    grad_upward = (grad_hidden * gate * sigma).astype(jnp.bfloat16)
    grad_gate_in = (grad_hidden * upward * sigma * (1.0 + gate * (1.0 - sigma))).astype(
        jnp.bfloat16
    )
    grad_in = jnp.concatenate([grad_gate_in, grad_upward], axis=1)
    grad_normed_two = token_scatter(layout, dot_cols(grad_in, in_all).astype(jnp.bfloat16))
    down = token_scatter(layout, dot_cols(hidden, down_all).astype(jnp.bfloat16))
    mixed = (middle + RESIDUAL * down).astype(jnp.bfloat16)

    def spread(partials):
        held = {}
        for mask in range(fsdp):
            piece = lax.dynamic_slice_in_dim(
                partials, jnp.bitwise_xor(fsdp_me, mask) * depth, depth, axis=0
            )
            held[mask] = swap(piece, "fsdp", fsdp, mask) if mask else piece
        sums = []
        for low in range(share):
            total = 0.0
            for high in range(0, fsdp, share):
                total = total + held[low + high].astype(jnp.float32)
            sums.append(total.astype(jnp.bfloat16))
        ordered = []
        mine = fsdp_me % share
        for column in range(share):
            pick = sums[0]
            for mask in range(1, share):
                pick = jnp.where(jnp.bitwise_xor(mine, mask) == column, sums[mask], pick)
            ordered.append(pick)
        return gather_seq(layout, jnp.stack(ordered))

    down_parts = spread(dot_rows(grad_down_in, hidden).astype(jnp.bfloat16))
    in_parts = spread(dot_rows(normed_two, grad_in).astype(jnp.bfloat16))

    grad_output = cotangent[0].astype(jnp.float32)
    gain_two_term = jnp.sum(grad_normed_two * middle * factor_two, axis=0)
    grad_middle = grad_output + norm_back(grad_normed_two, middle, factor_two, mlp_gain)
    grad_branch = token_gather(layout, (RESIDUAL * grad_middle).astype(jnp.bfloat16))
    grad_attended = dot(grad_branch, w_back).astype(jnp.bfloat16)
    grad_qkv = attend_back(qkv, ids, grad_attended, heads)
    grad_normed_one = token_scatter(layout, dot_cols(grad_qkv, w_in).astype(jnp.bfloat16))
    attn_parts = spread(
        jnp.concatenate(
            [dot_rows(normed_one, grad_qkv), dot_rows(grad_branch, attended)], axis=1
        ).astype(jnp.bfloat16)
    )
    factor_one = rms_factor(inputs)
    gain_one_term = jnp.sum(grad_normed_one * inputs * factor_one, axis=0)
    grad_inputs = grad_middle + norm_back(grad_normed_one, inputs, factor_one, attn_gain)

    gains = jnp.stack([gain_one_term, gain_two_term])
    gains = lax.psum(gains, ("seq", "fsdp"))
    gains = lax.dynamic_slice_in_dim(gains, fsdp_me * depth, depth, axis=1)

    def join(parts, start, size):
        return jnp.concatenate(
            [
                parts[i][j, :, start : start + size]
                for i in range(layout.seq)
                for j in range(share)
            ],
            axis=1,
        ).astype(jnp.float32)

    def join_shared(parts, start, size):
        columns = [
            parts[i][j, :, start : start + size].astype(jnp.float32)
            for i in range(layout.seq)
            for j in range(share)
        ]
        return jnp.concatenate(
            [
                sum(columns[i : i + kv_share][1:], columns[i])
                for i in range(0, GROUP, kv_share)
            ],
            axis=1,
        )

    return (
        mixed[None],
        grad_inputs.astype(jnp.bfloat16)[None],
        gains[0],
        join(attn_parts, 0, query_cols),
        join_shared(attn_parts, query_cols, HD),
        join_shared(attn_parts, query_cols + HD, HD),
        join(attn_parts, query_cols + 2 * HD, query_cols),
        gains[1],
        join(in_parts, 0, hidden_cols),
        join(in_parts, hidden_cols, hidden_cols),
        join(down_parts, 0, hidden_cols),
    )


def solution(mesh):
    tokens, rows = P("fsdp", "seq", None), P("fsdp", None)
    return jax.shard_map(
        body,
        mesh=mesh,
        in_specs=(tokens, rows, P("fsdp"), rows, rows, rows, rows, P("fsdp"), rows, rows, rows, tokens),
        out_specs=(tokens, tokens, P("fsdp"), rows, rows, rows, rows, P("fsdp"), rows, rows, rows),
        check_vma=False,
    )
```

```python
import functools

import jax
import jax.numpy as jnp
from jax import lax
from jax.experimental import pallas as pl
from jax.experimental.pallas import tpu as pltpu
from jax.sharding import PartitionSpec as P

H = 32
KVH = 8
HD = 64
EPSILON = 1e-05
RESIDUAL = 0.22
GROUP = 16
MESH = pl.DeviceIdType.MESH
PIECES = ((0, 48), (48, 48), (96, 32))
ORDERS = ((1, 2, 3), (2, 3, 1), (3, 1, 2))
PAIRS = (7, 6, 5, 3, 4, 2, 1, 0)


def dot(left, right):
    return jnp.dot(left, right, preferred_element_type=jnp.float32)


def dot_cols(left, right):
    return lax.dot_general(
        left, right, (((1,), (1,)), ((), ())), preferred_element_type=jnp.float32
    )


def dot_rows(left, right):
    return lax.dot_general(
        left, right, (((0,), (0,)), ((), ())), preferred_element_type=jnp.float32
    )


def rms_factor(values):
    return lax.rsqrt(jnp.mean(values * values, axis=1, keepdims=True) + EPSILON)


def norm_back(grad_normed, values, factor, gain):
    weighted = grad_normed * gain
    centre = jnp.mean(weighted * values, axis=1, keepdims=True)
    return factor * weighted - values * (factor * factor * factor) * centre


class Layout:
    def __init__(self, seq_count, fsdp_count):
        self.seq = seq_count
        self.fsdp = fsdp_count
        self.share = GROUP // seq_count
        self.seq_bits = seq_count.bit_length() - 1

    def member(self):
        return lax.axis_index("seq") + self.seq * (lax.axis_index("fsdp") % self.share)

    def offset(self, low, high):
        return {
            "seq": jnp.bitwise_xor(lax.axis_index("seq"), low),
            "fsdp": jnp.bitwise_xor(lax.axis_index("fsdp"), high),
        }

    def device(self, mask):
        return self.offset(mask % self.seq, mask // self.seq)


def span_mask(dims):
    return sum(1 << d for d in dims)


def greet(layout):
    barrier = pltpu.get_barrier_semaphore()
    for bit in range(4):
        pl.semaphore_signal(
            barrier, inc=1, device_id=layout.device(1 << bit), device_id_type=MESH
        )
    pl.semaphore_wait(barrier, 4)


def gather_kernel(layout, rows, x_ref, o_ref, send, recv, core_send, core_recv, own_sem):
    greet(layout)
    me = layout.member()

    def place(mask, piece):
        start, size = PIECES[piece]
        block = jnp.bitwise_xor(me, mask)
        return o_ref.at[pl.ds(pl.multiple_of(block * rows + start, 16), size)]

    def own(piece):
        start, size = PIECES[piece]
        return x_ref.at[pl.ds(start, size)]

    sent, relayed = [], []

    def push(mask, piece, slot, dim):
        copy = pltpu.make_async_remote_copy(
            src_ref=own(piece) if mask == 0 else place(mask, piece),
            dst_ref=place(mask, piece),
            send_sem=send.at[piece, slot],
            recv_sem=recv.at[piece, slot],
            device_id=layout.device(1 << dim),
            device_id_type=MESH,
        )
        copy.start()
        sent.append(copy)
        return copy

    def relay(mask, piece, slot):
        copy = pltpu.make_async_remote_copy(
            src_ref=own(piece) if mask == 0 else place(mask, piece),
            dst_ref=place(mask, piece),
            send_sem=core_send.at[piece, slot],
            recv_sem=core_recv.at[piece, slot],
            device_id=layout.device(1),
            device_id_type=MESH,
        )
        copy.start()
        sent.append(copy)
        relayed.append(copy)

    first, second, third = {}, {}, {}
    for piece, (a, b, c) in enumerate(ORDERS):
        first[piece] = push(0, piece, 0, a)
    for piece, (a, b, c) in enumerate(ORDERS):
        second[piece] = [push(0, piece, 1, b)]
    for piece, (a, b, c) in enumerate(ORDERS):
        third[piece] = [push(0, piece, 3, c)]
    local = pltpu.make_async_copy(x_ref, o_ref.at[pl.ds(pl.multiple_of(me * rows, 16), rows)], own_sem)
    local.start()
    for piece in range(3):
        relay(0, piece, 0)
    for piece, (a, b, c) in enumerate(ORDERS):
        first[piece].wait_recv()
        mask = span_mask((a,))
        second[piece].append(push(mask, piece, 2, b))
        third[piece].append(push(mask, piece, 4, c))
        relay(mask, piece, 1)
    for piece, (a, b, c) in enumerate(ORDERS):
        second[piece][0].wait_recv()
        mask = span_mask((b,))
        third[piece].append(push(mask, piece, 5, c))
        relay(mask, piece, 2)
    for piece, (a, b, c) in enumerate(ORDERS):
        second[piece][1].wait_recv()
        mask = span_mask((a, b))
        third[piece].append(push(mask, piece, 6, c))
        relay(mask, piece, 3)
    for turn, dims in enumerate(((2,), (0, 2), (1, 2), (0, 1, 2))):
        for piece, order in enumerate(ORDERS):
            third[piece][turn].wait_recv()
            relay(span_mask([order[d] for d in dims]), piece, 4 + turn)
    for copy in sent:
        copy.wait_send()
    for copy in relayed:
        copy.wait_recv()
    local.wait()


def token_gather(layout, block):
    rows, width = block.shape
    return pl.pallas_call(
        functools.partial(gather_kernel, layout, rows),
        out_shape=jax.ShapeDtypeStruct((GROUP * rows, width), block.dtype),
        in_specs=[pl.BlockSpec(memory_space=pl.ANY)],
        out_specs=pl.BlockSpec(memory_space=pl.ANY),
        scratch_shapes=[
            pltpu.SemaphoreType.DMA((3, 7)),
            pltpu.SemaphoreType.DMA((3, 7)),
            pltpu.SemaphoreType.DMA((3, 8)),
            pltpu.SemaphoreType.DMA((3, 8)),
            pltpu.SemaphoreType.DMA,
        ],
        compiler_params=pltpu.CompilerParams(collective_id=1, has_side_effects=True),
        name="token_gather",
    )(block)


def scatter_kernel(
    layout, rows, p_ref, o_ref, core_in, acc, arrive, core_send, core_recv, send, recv
):
    greet(layout)
    me = layout.member()
    masks = (14, 12, 10, 6, 8, 4, 2, 0)

    def rows_of(mask):
        return pl.ds(pl.multiple_of(jnp.bitwise_xor(me, mask) * rows, 16), rows)

    core = []
    for mask in masks:
        copy = pltpu.make_async_remote_copy(
            src_ref=p_ref.at[rows_of(mask ^ 1)],
            dst_ref=core_in.at[mask // 2],
            send_sem=core_send.at[mask // 2],
            recv_sem=core_recv.at[mask // 2],
            device_id=layout.device(1),
            device_id_type=MESH,
        )
        copy.start()
        core.append(copy)

    def push(piece, mask, dim, slot):
        start, size = PIECES[piece]
        copy = pltpu.make_async_remote_copy(
            src_ref=acc.at[mask // 2, pl.ds(start, size)],
            dst_ref=arrive.at[slot, pl.ds(start, size)],
            send_sem=send.at[piece, slot],
            recv_sem=recv.at[piece, slot],
            device_id=layout.device(1 << dim),
            device_id_type=MESH,
        )
        copy.start()
        return copy

    one, two, three = {}, {}, {}
    for mask, copy in zip(masks, core):
        copy.wait_recv()
        acc[mask // 2] = (
            p_ref[rows_of(mask)].astype(jnp.float32) + core_in[mask // 2].astype(jnp.float32)
        ).astype(jnp.bfloat16)
        for piece, (a, b, c) in enumerate(ORDERS):
            if mask & (1 << a):
                rest = mask ^ (1 << a)
                slot = (1 if rest & (1 << b) else 0) + (2 if rest & (1 << c) else 0)
                one[piece, slot] = push(piece, mask, a, slot)

    def add(piece, slot, mask):
        start, size = PIECES[piece]
        own = acc[mask // 2, pl.ds(start, size)].astype(jnp.float32)
        return own + arrive[slot, pl.ds(start, size)].astype(jnp.float32)

    def keep(piece, slot, mask):
        start, size = PIECES[piece]
        acc[mask // 2, pl.ds(start, size)] = add(piece, slot, mask).astype(jnp.bfloat16)

    for piece, (a, b, c) in enumerate(ORDERS):
        for slot, mask in ((3, span_mask((b, c))), (1, span_mask((b,)))):
            one[piece, slot].wait_recv()
            keep(piece, slot, mask)
            two[piece, slot] = push(piece, mask, b, 4 + slot // 2)
    for piece, (a, b, c) in enumerate(ORDERS):
        mask = span_mask((c,))
        one[piece, 2].wait_recv()
        keep(piece, 2, mask)
        two[piece, 3].wait_recv()
        keep(piece, 5, mask)
        three[piece] = push(piece, mask, c, 6)
    for piece, (a, b, c) in enumerate(ORDERS):
        start, size = PIECES[piece]
        one[piece, 0].wait_recv()
        two[piece, 1].wait_recv()
        partial = add(piece, 0, 0) + arrive[4, pl.ds(start, size)].astype(jnp.float32)
        three[piece].wait_recv()
        o_ref[pl.ds(start, size)] = partial + arrive[6, pl.ds(start, size)].astype(jnp.float32)
    for copy in core + list(one.values()) + list(two.values()) + list(three.values()):
        copy.wait_send()


def token_scatter(layout, partial):
    rows, width = partial.shape[0] // GROUP, partial.shape[1]
    return pl.pallas_call(
        functools.partial(scatter_kernel, layout, rows),
        out_shape=jax.ShapeDtypeStruct((rows, width), jnp.float32),
        in_specs=[pl.BlockSpec(memory_space=pltpu.VMEM)],
        out_specs=pl.BlockSpec(memory_space=pltpu.VMEM),
        scratch_shapes=[
            pltpu.VMEM((8, rows, width), jnp.bfloat16),
            pltpu.VMEM((8, rows, width), jnp.bfloat16),
            pltpu.VMEM((7, rows, width), jnp.bfloat16),
            pltpu.SemaphoreType.DMA((8,)),
            pltpu.SemaphoreType.DMA((8,)),
            pltpu.SemaphoreType.DMA((3, 7)),
            pltpu.SemaphoreType.DMA((3, 7)),
        ],
        compiler_params=pltpu.CompilerParams(
            collective_id=2, has_side_effects=True, vmem_limit_bytes=48 * 1024 * 1024
        ),
        name="token_scatter",
    )(partial)


def softmax(query, keys, query_ids, key_ids):
    scores = dot_cols(query, keys) * (1.0 / HD)
    scores = jnp.where(key_ids <= query_ids, scores, -1e30)
    shifted = jnp.exp(scores - jnp.max(scores, axis=1, keepdims=True))
    return shifted / jnp.sum(shifted, axis=1, keepdims=True)


def rows_at(start, size):
    return pl.ds(pl.multiple_of(start, 16), size)


def greet_all(layout):
    pairs = [(1 << bit, 0) for bit in range(layout.seq_bits)]
    pairs += [(0, mask) for mask in range(1, layout.fsdp)]
    barrier = pltpu.get_barrier_semaphore()
    for low, high in pairs:
        pl.semaphore_signal(
            barrier, inc=1, device_id=layout.offset(low, high), device_id_type=MESH
        )
    pl.semaphore_wait(barrier, len(pairs))


def gather_steps(layout, rows, own_ref, dst_ref, sems):
    send, recv, relay_recv, own_sem = sems
    me = layout.member()
    sent, relayed = [], []

    def place(mask, piece):
        start, size = PIECES[piece]
        block = jnp.bitwise_xor(me, mask)
        return dst_ref.at[rows_at(block * rows + start, size)]

    def source(mask, piece):
        start, size = PIECES[piece]
        return own_ref.at[pl.ds(start, size)] if mask == 0 else place(mask, piece)

    def push(mask, piece, slot, dim):
        copy = pltpu.make_async_remote_copy(
            src_ref=source(mask, piece),
            dst_ref=place(mask, piece),
            send_sem=send,
            recv_sem=recv.at[piece, slot],
            device_id=layout.device(1 << dim),
            device_id_type=MESH,
        )
        copy.start()
        sent.append(copy)
        return copy

    def relay(mask, piece, slot):
        copy = pltpu.make_async_remote_copy(
            src_ref=source(mask, piece),
            dst_ref=place(mask, piece),
            send_sem=send,
            recv_sem=relay_recv.at[piece, slot],
            device_id=layout.device(1),
            device_id_type=MESH,
        )
        copy.start()
        relayed.append(copy)

    first, second, third = {}, {}, {}
    for piece, (a, b, c) in enumerate(ORDERS):
        first[piece] = push(0, piece, 0, a)
    for piece, (a, b, c) in enumerate(ORDERS):
        second[piece] = [push(0, piece, 1, b)]
    for piece, (a, b, c) in enumerate(ORDERS):
        third[piece] = [push(0, piece, 3, c)]
    local = pltpu.make_async_copy(own_ref, dst_ref.at[rows_at(me * rows, rows)], own_sem)
    local.start()
    for piece in range(len(ORDERS)):
        relay(0, piece, 0)
    yield
    for piece, (a, b, c) in enumerate(ORDERS):
        first[piece].wait_recv()
        mask = span_mask((a,))
        second[piece].append(push(mask, piece, 2, b))
        third[piece].append(push(mask, piece, 4, c))
        relay(mask, piece, 1)
    yield
    for piece, (a, b, c) in enumerate(ORDERS):
        second[piece][0].wait_recv()
        mask = span_mask((b,))
        third[piece].append(push(mask, piece, 5, c))
        relay(mask, piece, 2)
    yield
    for piece, (a, b, c) in enumerate(ORDERS):
        second[piece][1].wait_recv()
        mask = span_mask((a, b))
        third[piece].append(push(mask, piece, 6, c))
        relay(mask, piece, 3)
    yield
    for turn, dims in enumerate(((2,), (0, 2), (1, 2), (0, 1, 2))):
        for piece, order in enumerate(ORDERS):
            third[piece][turn].wait_recv()
            relay(span_mask([order[d] for d in dims]), piece, 4 + turn)
    yield
    for copy in relayed:
        copy.wait_recv()
    local.wait()
    whole = dst_ref.at[pl.ds(0, 15 * rows)]
    pltpu.make_async_remote_copy(
        src_ref=whole,
        dst_ref=whole,
        send_sem=send,
        recv_sem=recv.at[0, 0],
        device_id=layout.device(1),
        device_id_type=MESH,
    ).wait_send()
    yield


def gather_sems():
    count = len(ORDERS)
    return [
        pltpu.SemaphoreType.DMA,
        pltpu.SemaphoreType.DMA((count, 7)),
        pltpu.SemaphoreType.DMA((count, 8)),
        pltpu.SemaphoreType.DMA,
    ]


def finish(steps):
    for _ in steps:
        pass


def scatter_steps(layout, rows, produce, total, buffers, sems):
    stage, core_in, arrive = buffers
    core_send, core_recv, send, recv = sems
    me = layout.member()
    core = me % 2
    own = pl.multiple_of(core * rows, 16)
    other = pl.multiple_of((1 - core) * rows, 16)
    copies = {}

    def chunked(start, size, body):
        @pl.loop(0, size // 16)
        def _(i):
            body(pl.multiple_of(i * 16 + start, 16))

    def push(piece, pair, dim, slot):
        start, size = PIECES[piece]
        copy = pltpu.make_async_remote_copy(
            src_ref=stage.at[pair, rows_at(own + start, size)],
            dst_ref=arrive.at[slot, pl.ds(start, size)],
            send_sem=send.at[piece, slot],
            recv_sem=recv.at[piece, slot],
            device_id=layout.device(1 << dim),
            device_id_type=MESH,
        )
        copy.start()
        return copy

    one, two, three = {}, {}, {}

    def settle(pair):
        copies[pair].wait_recv()

        def body(r):
            stage[pair, rows_at(own + r, 16)] = (
                stage[pair, rows_at(own + r, 16)].astype(jnp.float32)
                + core_in[pair, rows_at(r, 16)].astype(jnp.float32)
            ).astype(jnp.bfloat16)

        chunked(0, rows, body)
        mask = pair * 2
        for piece, (a, b, c) in enumerate(ORDERS):
            if mask & (1 << a):
                slot = (1 if mask & (1 << b) else 0) + (2 if mask & (1 << c) else 0)
                one[piece, slot] = push(piece, pair, a, slot)

    before = None
    for pair in PAIRS:
        produce(jnp.bitwise_xor(me // 2, pair), stage.at[pair])
        copies[pair] = pltpu.make_async_remote_copy(
            src_ref=stage.at[pair, rows_at(other, rows)],
            dst_ref=core_in.at[pair],
            send_sem=core_send.at[pair],
            recv_sem=core_recv.at[pair],
            device_id=layout.device(1),
            device_id_type=MESH,
        )
        copies[pair].start()
        if before is not None:
            settle(before)
        before = pair
    settle(before)
    yield

    def keep(piece, pair, slots):
        start, size = PIECES[piece]

        def body(r):
            value = stage[pair, rows_at(own + r, 16)].astype(jnp.float32)
            for slot in slots:
                value = value + arrive[slot, rows_at(r, 16)].astype(jnp.float32)
            stage[pair, rows_at(own + r, 16)] = value.astype(jnp.bfloat16)

        chunked(start, size, body)

    for piece, (a, b, c) in enumerate(ORDERS):
        for slot, dims in ((3, (b, c)), (1, (b,))):
            pair = span_mask(dims) // 2
            one[piece, slot].wait_recv()
            keep(piece, pair, (slot,))
            two[piece, slot] = push(piece, pair, b, 4 + slot // 2)
    yield
    for piece, (a, b, c) in enumerate(ORDERS):
        pair = span_mask((c,)) // 2
        one[piece, 2].wait_recv()
        two[piece, 3].wait_recv()
        keep(piece, pair, (2, 5))
        three[piece] = push(piece, pair, c, 6)
    yield
    for piece, (a, b, c) in enumerate(ORDERS):
        start, size = PIECES[piece]
        one[piece, 0].wait_recv()
        two[piece, 1].wait_recv()
        three[piece].wait_recv()

        def body(r):
            value = stage[0, rows_at(own + r, 16)].astype(jnp.float32)
            for slot in (0, 4, 6):
                value = value + arrive[slot, rows_at(r, 16)].astype(jnp.float32)
            total[rows_at(r, 16)] = value

        chunked(start, size, body)
    for group in (copies, one, two, three):
        for copy in group.values():
            copy.wait_send()
    yield


def scatter_scratch(rows, width):
    return [
        pltpu.VMEM((8, 2 * rows, width), jnp.bfloat16),
        pltpu.VMEM((8, rows, width), jnp.bfloat16),
        pltpu.VMEM((7, rows, width), jnp.bfloat16),
    ]


def scatter_sems():
    count = len(ORDERS)
    return [
        pltpu.SemaphoreType.DMA((8,)),
        pltpu.SemaphoreType.DMA((8,)),
        pltpu.SemaphoreType.DMA((count, 7)),
        pltpu.SemaphoreType.DMA((count, 7)),
    ]


def loop_rows(count, size, body):
    @pl.loop(0, count // size)
    def _(i):
        body(pl.ds(pl.multiple_of(i * size, size), size))


class Sizes:
    def __init__(self, layout, tokens, block_ids, w_query, w_gate):
        self.rows, self.width = tokens.shape[1], tokens.shape[2]
        self.length = block_ids.shape[1]
        self.depth = w_query.shape[0]
        self.hidden = w_gate.shape[1] // GROUP
        self.heads = H // GROUP
        self.query = self.heads * HD
        self.attn = 2 * self.query + 2 * HD
        self.all_rows = GROUP * self.rows
        self.span = min(512, self.length)
        self.kv_share = GROUP // KVH


def kv_half(layout, target, chunk):
    second = (target // (GROUP // KVH)) % 2 == 1
    return jnp.where(second, chunk[:, HD:], chunk[:, :HD])


def attention_scores(sizes, qkv, ids, seq, start, head):
    base = sizes.query
    keys_rows = rows_at(seq * sizes.length, sizes.length)
    query_rows = rows_at(seq * sizes.length + start, sizes.span)
    query = qkv[query_rows, head * HD : (head + 1) * HD]
    keys = qkv[keys_rows, base : base + HD]
    values = qkv[keys_rows, base + HD : base + 2 * HD]
    key_ids = ids[seq, 0:1, :]
    query_ids = jnp.transpose(ids[seq, :, pl.ds(start, sizes.span)])[:, :1]
    return query, keys, values, softmax(query, keys, query_ids, key_ids)


def front_kernel(
    layout,
    sizes,
    tok_ref,
    cot_ref,
    ids_ref,
    gains_ref,
    wq_ref,
    wk_ref,
    wv_ref,
    wo_ref,
    wg_ref,
    wu_ref,
    wd_ref,
    h1_out,
    h2_out,
    g_out,
    in_out,
    down_out,
    wa,
    qkv,
    attended,
    middle,
    gains,
    ids,
    x_all,
    tok,
    h2,
    wq,
    wk,
    wv,
    wo,
    pack,
    stage,
    core_in,
    arrive,
    x_send,
    x_recv,
    x_relay,
    x_own,
    h_send,
    h_recv,
    h_relay,
    h_own,
    g_send,
    g_recv,
    g_relay,
    g_own,
    core_send,
    core_recv,
    s_send,
    s_recv,
    attn_send,
    attn_recv,
    gain_send,
    gain_recv,
    id_send,
    id_recv,
    mlp_send,
    mlp_recv,
    load_sem,
):
    share, fsdp, depth = layout.share, layout.fsdp, sizes.depth
    seq_me, fsdp_me = lax.axis_index("seq"), lax.axis_index("fsdp")
    query = sizes.query
    rows, hidden = sizes.rows, sizes.hidden

    loads = []

    def load(src, dst):
        copy = pltpu.make_async_copy(src, dst, load_sem.at[len(loads)])
        copy.start()
        loads.append(copy)
        return copy

    def columns(ref, start, size):
        return ref.at[:, pl.ds(pl.multiple_of(start, 128), size)]

    load(tok_ref, tok)
    load(columns(wq_ref, seq_me * share * query, share * query), wq)
    load(columns(wo_ref, seq_me * share * query, share * query), wo)
    chunk = seq_me * share // (2 * sizes.kv_share) * 128
    load(columns(wk_ref, chunk, 128), wk)
    load(columns(wv_ref, chunk, 128), wv)
    own_rows = pl.ds(pl.multiple_of(fsdp_me * depth, 128), depth)
    load(gains_ref, gains.at[:, own_rows])
    load(ids_ref, ids.at[fsdp_me % share])
    greet_all(layout)
    x_steps = gather_steps(layout, rows, tok_ref, x_all, (x_send, x_recv, x_relay, x_own))
    next(x_steps)
    small = []
    for mask in range(1, fsdp):
        copy = pltpu.make_async_remote_copy(
            src_ref=gains_ref,
            dst_ref=gains.at[:, own_rows],
            send_sem=gain_send.at[mask],
            recv_sem=gain_recv.at[mask],
            device_id=layout.offset(0, mask),
            device_id_type=MESH,
        )
        copy.start()
        small.append(copy)
    for mask in range(1, share):
        copy = pltpu.make_async_remote_copy(
            src_ref=ids_ref,
            dst_ref=ids.at[fsdp_me % share],
            send_sem=id_send.at[mask],
            recv_sem=id_recv.at[mask],
            device_id=layout.offset(0, mask),
            device_id_type=MESH,
        )
        copy.start()
        small.append(copy)
    for copy in loads:
        copy.wait()
    for j in range(share):
        target = seq_me * share + j
        pack[j] = jnp.concatenate(
            [
                wq[:, j * query : (j + 1) * query],
                kv_half(layout, target, wk[...]),
                kv_half(layout, target, wv[...]),
                wo[:, j * query : (j + 1) * query],
            ],
            axis=1,
        )
    attn = []
    for mask in reversed(range(1, fsdp)):
        copy = pltpu.make_async_remote_copy(
            src_ref=pack.at[jnp.bitwise_xor(fsdp_me, mask) % share],
            dst_ref=wa.at[own_rows],
            send_sem=attn_send.at[mask],
            recv_sem=attn_recv.at[mask],
            device_id=layout.offset(0, mask),
            device_id_type=MESH,
        )
        copy.start()
        attn.append(copy)
    wa[own_rows] = pack[fsdp_me % share]
    finish(x_steps)
    for copy in small:
        copy.wait()

    gain_one = gains[0:1].astype(jnp.float32)

    def norm(r):
        values = x_all[r].astype(jnp.float32)
        x_all[r] = (values * rms_factor(values) * gain_one).astype(jnp.bfloat16)

    loop_rows(sizes.all_rows, 64, norm)
    h1_copy = pltpu.make_async_copy(x_all, h1_out, load_sem.at[0])
    h1_copy.start()
    for copy in attn:
        copy.wait()

    mlp = []

    def send_mlp(ref, out, place, index):
        def at(j):
            return columns(ref, (seq_me * share + j) * hidden, hidden)

        home = out.at[own_rows, pl.ds(place, hidden)]
        for mask in reversed(range(1, fsdp)):
            copy = pltpu.make_async_remote_copy(
                src_ref=at(jnp.bitwise_xor(fsdp_me, mask) % share),
                dst_ref=home,
                send_sem=mlp_send.at[index, mask],
                recv_sem=mlp_recv.at[index, mask],
                device_id=layout.offset(0, mask),
                device_id_type=MESH,
            )
            copy.start()
            mlp.append(copy)
        copy = pltpu.make_async_copy(at(fsdp_me % share), home, load_sem.at[1 + index])
        copy.start()
        mlp.append(copy)

    send_mlp(wg_ref, in_out, 0, 0)
    send_mlp(wu_ref, in_out, hidden, 1)
    send_mlp(wd_ref, down_out, 0, 2)

    def project(r):
        qkv[r] = dot(x_all[r], wa[:, : query + 2 * HD]).astype(jnp.bfloat16)

    loop_rows(sizes.all_rows, 256, project)

    blocks = sizes.length // sizes.span

    @pl.loop(0, share * blocks)
    def _(i):
        seq = i // blocks
        start = pl.multiple_of((i % blocks) * sizes.span, sizes.span)
        outs = []
        for head in range(sizes.heads):
            _, _, values, probs = attention_scores(sizes, qkv, ids, seq, start, head)
            outs.append(dot(probs.astype(jnp.bfloat16), values))
        attended[rows_at(seq * sizes.length + start, sizes.span)] = jnp.concatenate(
            outs, axis=1
        ).astype(jnp.bfloat16)

    def out_rows(pair, ref):
        block = attended[rows_at(pair * 2 * rows, 2 * rows)]

        @pl.loop(0, sizes.width // 512)
        def _(i):
            piece = pl.ds(pl.multiple_of(i * 512, 512), 512)
            ref[:, piece] = dot_cols(block, wa[piece, query + 2 * HD :]).astype(jnp.bfloat16)

    finish(
        scatter_steps(
            layout, rows, out_rows, middle, (stage, core_in, arrive),
            (core_send, core_recv, s_send, s_recv),
        )
    )
    gain_two = gains[8:9].astype(jnp.float32)

    def second(r):
        values = tok[r].astype(jnp.float32) + RESIDUAL * middle[r]
        middle[r] = values
        h2[r] = (values * rms_factor(values) * gain_two).astype(jnp.bfloat16)

    loop_rows(rows, 32, second)
    h_steps = gather_steps(layout, rows, h2, h2_out, (h_send, h_recv, h_relay, h_own))
    finish(h_steps)
    g_steps = gather_steps(layout, rows, cot_ref, g_out, (g_send, g_recv, g_relay, g_own))
    finish(g_steps)
    for copy in mlp:
        copy.wait()
    h1_copy.wait()


def front(layout, sizes, *args):
    width, count = sizes.width, sizes.all_rows
    hbm, vmem = pl.BlockSpec(memory_space=pl.ANY), pl.BlockSpec(memory_space=pltpu.VMEM)
    share, depth, fsdp = layout.share, sizes.depth, layout.fsdp
    bf16 = jnp.bfloat16
    shapes = [
        ((count, width), bf16, hbm),
        ((count, width), bf16, hbm),
        ((count, width), bf16, hbm),
        ((width, 2 * sizes.hidden), bf16, hbm),
        ((width, sizes.hidden), bf16, hbm),
        ((width, sizes.attn), bf16, vmem),
        ((count, sizes.query + 2 * HD), bf16, vmem),
        ((count, sizes.query), bf16, vmem),
        ((sizes.rows, width), jnp.float32, vmem),
        ((16, width), bf16, vmem),
        ((share, 8, sizes.length), jnp.int32, vmem),
    ]
    dma = pltpu.SemaphoreType.DMA
    return pl.pallas_call(
        functools.partial(front_kernel, layout, sizes),
        out_shape=[jax.ShapeDtypeStruct(shape, dtype) for shape, dtype, _ in shapes],
        in_specs=[hbm] * len(args),
        out_specs=[spec for _, _, spec in shapes],
        scratch_shapes=[
            pltpu.VMEM((count, width), bf16),
            pltpu.VMEM((sizes.rows, width), bf16),
            pltpu.VMEM((sizes.rows, width), bf16),
            pltpu.VMEM((depth, share * sizes.query), bf16),
            pltpu.VMEM((depth, 128), bf16),
            pltpu.VMEM((depth, 128), bf16),
            pltpu.VMEM((depth, share * sizes.query), bf16),
            pltpu.VMEM((share, depth, sizes.attn), bf16),
        ]
        + scatter_scratch(sizes.rows, width)
        + gather_sems() * 3
        + scatter_sems()
        + [dma((fsdp,)), dma((fsdp,)), dma((fsdp,)), dma((fsdp,))]
        + [dma((share,)), dma((share,)), dma((3, fsdp)), dma((3, fsdp)), dma((8,))],
        compiler_params=pltpu.CompilerParams(
            collective_id=3, has_side_effects=True, vmem_limit_bytes=56 * 1024 * 1024
        ),
        name="front",
    )(*args)


def attend_kernel(heads, q_ref, kv_ref, row_ref, col_ref, o_ref):
    base = heads * HD
    keys = kv_ref[:, base : base + HD]
    values = kv_ref[:, base + HD : base + 2 * HD]
    outs = []
    for head in range(heads):
        query = q_ref[:, head * HD : (head + 1) * HD]
        probs = softmax(query, keys, col_ref[0], row_ref[0])
        outs.append(dot(probs.astype(jnp.bfloat16), values))
    o_ref[...] = jnp.concatenate(outs, axis=1).astype(jnp.bfloat16)


def attend_back_kernel(heads, q_ref, kv_ref, row_ref, col_ref, g_ref, o_ref, grad_kv):
    step = pl.program_id(1)
    span, length = q_ref.shape[0], kv_ref.shape[0]
    base = heads * HD
    keys = kv_ref[:, base : base + HD]
    values = kv_ref[:, base + HD : base + 2 * HD]
    grads, grad_keys, grad_values = [], 0.0, 0.0
    for head in range(heads):
        query = q_ref[:, head * HD : (head + 1) * HD]
        grad = g_ref[:, head * HD : (head + 1) * HD]
        probs = softmax(query, keys, col_ref[0], row_ref[0])
        grad_probs = dot_cols(grad, values)
        centre = jnp.sum(probs * grad_probs, axis=1, keepdims=True)
        grad_scores = (probs * (grad_probs - centre)).astype(jnp.bfloat16)
        grads.append(dot(grad_scores, keys) * (1.0 / HD))
        grad_keys = grad_keys + dot_rows(grad_scores, query) * (1.0 / HD)
        grad_values = grad_values + dot_rows(probs.astype(jnp.bfloat16), grad)
    both = jnp.concatenate([grad_keys, grad_values], axis=1)

    @pl.when(step == 0)
    def _():
        grad_kv[...] = both

    @pl.when(step > 0)
    def _():
        grad_kv[...] += both

    start = pl.multiple_of(step * span, span)
    o_ref[pl.ds(start, span), :base] = jnp.concatenate(grads, axis=1).astype(jnp.bfloat16)

    @pl.when(step == pl.num_programs(1) - 1)
    def _():
        o_ref[:, base:] = grad_kv[...].astype(jnp.bfloat16)


def attention_specs(qkv, ids, heads):
    count, length = ids.shape
    span = min(512, length)
    blocks = length // span
    width = qkv.shape[1]
    specs = [
        pl.BlockSpec((span, width), lambda i, j: (i * blocks + j, 0)),
        pl.BlockSpec((length, width), lambda i, j: (i, 0)),
        pl.BlockSpec((1, 1, length), lambda i, j: (i, 0, 0)),
        pl.BlockSpec((1, span, 1), lambda i, j: (i, j, 0)),
    ]
    args = (qkv, qkv, ids[:, None, :], ids[:, :, None])
    return (count, blocks), span, length, specs, args


def attend(qkv, ids, heads):
    grid, span, length, specs, args = attention_specs(qkv, ids, heads)
    return pl.pallas_call(
        functools.partial(attend_kernel, heads),
        grid=grid,
        in_specs=specs,
        out_specs=pl.BlockSpec((span, heads * HD), lambda i, j: (i * grid[1] + j, 0)),
        out_shape=jax.ShapeDtypeStruct((qkv.shape[0], heads * HD), jnp.bfloat16),
        compiler_params=pltpu.CompilerParams(vmem_limit_bytes=48 * 1024 * 1024),
        name="attend",
    )(*args)


def attend_back(qkv, ids, grad, heads):
    grid, span, length, specs, args = attention_specs(qkv, ids, heads)
    width = qkv.shape[1]
    return pl.pallas_call(
        functools.partial(attend_back_kernel, heads),
        grid=grid,
        in_specs=specs
        + [pl.BlockSpec((span, heads * HD), lambda i, j: (i * grid[1] + j, 0))],
        out_specs=pl.BlockSpec((length, width), lambda i, j: (i, 0)),
        out_shape=jax.ShapeDtypeStruct(qkv.shape, jnp.bfloat16),
        scratch_shapes=[pltpu.VMEM((length, 2 * HD), jnp.float32)],
        compiler_params=pltpu.CompilerParams(vmem_limit_bytes=48 * 1024 * 1024),
        name="attend_back",
    )(*args, grad)


def swap(array, axis, size, mask):
    return lax.ppermute(array, axis, [(i, i ^ mask) for i in range(size)])


def gather_seq(layout, array):
    me = lax.axis_index("seq")
    stack = array[None]
    for bit in reversed(range(layout.seq_bits)):
        other = swap(stack, "seq", layout.seq, 1 << bit)
        upper = (me >> bit) % 2 == 1
        pair = jnp.stack([jnp.where(upper, other, stack), jnp.where(upper, stack, other)], axis=1)
        stack = pair.reshape((-1,) + array.shape)
    return stack


def slices(array, start, size):
    return lax.dynamic_slice_in_dim(array, start, size, axis=1)


def body(
    tokens,
    block_ids,
    gain_attn,
    w_query,
    w_key,
    w_value,
    w_out,
    gain_mlp,
    w_gate,
    w_up,
    w_down,
    cotangent,
):
    layout = Layout(lax.axis_size("seq"), lax.axis_size("fsdp"))
    fsdp, share = layout.fsdp, layout.share
    seq_me, fsdp_me = lax.axis_index("seq"), lax.axis_index("fsdp")
    rows, width = tokens.shape[1], tokens.shape[2]
    depth = w_gate.shape[0]
    hidden_cols = w_gate.shape[1] // GROUP
    heads = H // GROUP
    query_cols = heads * HD
    kv_share = GROUP // KVH
    sizes = Sizes(layout, tokens, block_ids, w_query, w_gate)
    gains_own = jnp.concatenate(
        [jnp.broadcast_to(gain[None], (8, depth)) for gain in (gain_attn, gain_mlp)], axis=0
    )
    ids_own = jnp.broadcast_to(block_ids, (8, block_ids.shape[1]))
    (
        normed_one,
        normed_two,
        grad_all,
        in_all,
        down_all,
        attn_all,
        qkv,
        attended,
        middle,
        gains_all,
        ids_all,
    ) = front(
        layout,
        sizes,
        tokens[0],
        cotangent[0],
        ids_own,
        gains_own,
        w_query,
        w_key,
        w_value,
        w_out,
        w_gate,
        w_up,
        w_down,
    )
    w_in = attn_all[:, : query_cols + 2 * HD]
    w_back = attn_all[:, query_cols + 2 * HD :]
    attn_gain = gains_all[0:1].astype(jnp.float32)
    mlp_gain = gains_all[8:9].astype(jnp.float32)
    ids = ids_all[:, 0]
    inputs = tokens[0].astype(jnp.float32)
    factor_two = rms_factor(middle)
    gate_up = dot(normed_two, in_all)
    gate, upward = gate_up[:, :hidden_cols], gate_up[:, hidden_cols:]
    sigma = jax.nn.sigmoid(gate)
    hidden = (gate * sigma * upward).astype(jnp.bfloat16)
    grad_down_in = (RESIDUAL * grad_all.astype(jnp.float32)).astype(jnp.bfloat16)
    grad_hidden = dot(grad_down_in, down_all)
    grad_upward = (grad_hidden * gate * sigma).astype(jnp.bfloat16)
    grad_gate_in = (grad_hidden * upward * sigma * (1.0 + gate * (1.0 - sigma))).astype(
        jnp.bfloat16
    )
    grad_in = jnp.concatenate([grad_gate_in, grad_upward], axis=1)
    grad_normed_two = token_scatter(layout, dot_cols(grad_in, in_all).astype(jnp.bfloat16))
    down = token_scatter(layout, dot_cols(hidden, down_all).astype(jnp.bfloat16))
    mixed = (middle + RESIDUAL * down).astype(jnp.bfloat16)

    def spread(partials):
        held = {}
        for mask in range(fsdp):
            piece = lax.dynamic_slice_in_dim(
                partials, jnp.bitwise_xor(fsdp_me, mask) * depth, depth, axis=0
            )
            held[mask] = swap(piece, "fsdp", fsdp, mask) if mask else piece
        sums = []
        for low in range(share):
            total = 0.0
            for high in range(0, fsdp, share):
                total = total + held[low + high].astype(jnp.float32)
            sums.append(total.astype(jnp.bfloat16))
        ordered = []
        mine = fsdp_me % share
        for column in range(share):
            pick = sums[0]
            for mask in range(1, share):
                pick = jnp.where(jnp.bitwise_xor(mine, mask) == column, sums[mask], pick)
            ordered.append(pick)
        return gather_seq(layout, jnp.stack(ordered))

    down_parts = spread(dot_rows(grad_down_in, hidden).astype(jnp.bfloat16))
    in_parts = spread(dot_rows(normed_two, grad_in).astype(jnp.bfloat16))

    grad_output = cotangent[0].astype(jnp.float32)
    gain_two_term = jnp.sum(grad_normed_two * middle * factor_two, axis=0)
    grad_middle = grad_output + norm_back(grad_normed_two, middle, factor_two, mlp_gain)
    grad_branch = token_gather(layout, (RESIDUAL * grad_middle).astype(jnp.bfloat16))
    grad_attended = dot(grad_branch, w_back).astype(jnp.bfloat16)
    grad_qkv = attend_back(qkv, ids, grad_attended, heads)
    grad_normed_one = token_scatter(layout, dot_cols(grad_qkv, w_in).astype(jnp.bfloat16))
    attn_parts = spread(
        jnp.concatenate(
            [dot_rows(normed_one, grad_qkv), dot_rows(grad_branch, attended)], axis=1
        ).astype(jnp.bfloat16)
    )
    factor_one = rms_factor(inputs)
    gain_one_term = jnp.sum(grad_normed_one * inputs * factor_one, axis=0)
    grad_inputs = grad_middle + norm_back(grad_normed_one, inputs, factor_one, attn_gain)

    gains = jnp.stack([gain_one_term, gain_two_term])
    gains = lax.psum(gains, ("seq", "fsdp"))
    gains = lax.dynamic_slice_in_dim(gains, fsdp_me * depth, depth, axis=1)

    def join(parts, start, size):
        return jnp.concatenate(
            [
                parts[i][j, :, start : start + size]
                for i in range(layout.seq)
                for j in range(share)
            ],
            axis=1,
        ).astype(jnp.float32)

    def join_shared(parts, start, size):
        columns = [
            parts[i][j, :, start : start + size].astype(jnp.float32)
            for i in range(layout.seq)
            for j in range(share)
        ]
        return jnp.concatenate(
            [
                sum(columns[i : i + kv_share][1:], columns[i])
                for i in range(0, GROUP, kv_share)
            ],
            axis=1,
        )

    return (
        mixed[None],
        grad_inputs.astype(jnp.bfloat16)[None],
        gains[0],
        join(attn_parts, 0, query_cols),
        join_shared(attn_parts, query_cols, HD),
        join_shared(attn_parts, query_cols + HD, HD),
        join(attn_parts, query_cols + 2 * HD, query_cols),
        gains[1],
        join(in_parts, 0, hidden_cols),
        join(in_parts, hidden_cols, hidden_cols),
        join(down_parts, 0, hidden_cols),
    )


def solution(mesh):
    tokens, rows = P("fsdp", "seq", None), P("fsdp", None)
    return jax.shard_map(
        body,
        mesh=mesh,
        in_specs=(tokens, rows, P("fsdp"), rows, rows, rows, rows, P("fsdp"), rows, rows, rows, tokens),
        out_specs=(tokens, tokens, P("fsdp"), rows, rows, rows, rows, P("fsdp"), rows, rows, rows),
        check_vma=False,
    )
```

```python
import functools

import jax
import jax.numpy as jnp
from jax import lax
from jax.experimental import pallas as pl
from jax.experimental.pallas import tpu as pltpu
from jax.sharding import PartitionSpec as P

H = 32
KVH = 8
HD = 64
EPSILON = 1e-05
RESIDUAL = 0.22
GROUP = 16
MESH = pl.DeviceIdType.MESH
PIECES = ((0, 48), (48, 48), (96, 32))
ORDERS = ((1, 2, 3), (2, 3, 1), (3, 1, 2))
PAIRS = (7, 6, 5, 3, 4, 2, 1, 0)


def dot(left, right):
    return jnp.dot(left, right, preferred_element_type=jnp.float32)


def dot_cols(left, right):
    return lax.dot_general(
        left, right, (((1,), (1,)), ((), ())), preferred_element_type=jnp.float32
    )


def dot_rows(left, right):
    return lax.dot_general(
        left, right, (((0,), (0,)), ((), ())), preferred_element_type=jnp.float32
    )


def rms_factor(values):
    return lax.rsqrt(jnp.mean(values * values, axis=1, keepdims=True) + EPSILON)


def norm_back(grad_normed, values, factor, gain):
    weighted = grad_normed * gain
    centre = jnp.mean(weighted * values, axis=1, keepdims=True)
    return factor * weighted - values * (factor * factor * factor) * centre


class Layout:
    def __init__(self, seq_count, fsdp_count):
        self.seq = seq_count
        self.fsdp = fsdp_count
        self.share = GROUP // seq_count
        self.seq_bits = seq_count.bit_length() - 1

    def member(self):
        return lax.axis_index("seq") + self.seq * (lax.axis_index("fsdp") % self.share)

    def offset(self, low, high):
        return {
            "seq": jnp.bitwise_xor(lax.axis_index("seq"), low),
            "fsdp": jnp.bitwise_xor(lax.axis_index("fsdp"), high),
        }

    def device(self, mask):
        return self.offset(mask % self.seq, mask // self.seq)


def span_mask(dims):
    return sum(1 << d for d in dims)


def softmax(query, keys, query_ids, key_ids):
    scores = dot_cols(query, keys) * (1.0 / HD)
    scores = jnp.where(key_ids <= query_ids, scores, -1e30)
    shifted = jnp.exp(scores - jnp.max(scores, axis=1, keepdims=True))
    return shifted / jnp.sum(shifted, axis=1, keepdims=True)


def rows_at(start, size):
    return pl.ds(pl.multiple_of(start, 16), size)


def greet_all(layout):
    pairs = [(1 << bit, 0) for bit in range(layout.seq_bits)]
    pairs += [(0, mask) for mask in range(1, layout.fsdp)]
    barrier = pltpu.get_barrier_semaphore()
    for low, high in pairs:
        pl.semaphore_signal(
            barrier, inc=1, device_id=layout.offset(low, high), device_id_type=MESH
        )
    pl.semaphore_wait(barrier, len(pairs))


def gather_steps(layout, rows, own_ref, dst_ref, sems):
    send, recv, relay_recv, own_sem = sems
    me = layout.member()
    sent, relayed = [], []

    def place(mask, piece):
        start, size = PIECES[piece]
        block = jnp.bitwise_xor(me, mask)
        return dst_ref.at[rows_at(block * rows + start, size)]

    def source(mask, piece):
        start, size = PIECES[piece]
        return own_ref.at[pl.ds(start, size)] if mask == 0 else place(mask, piece)

    def push(mask, piece, slot, dim):
        copy = pltpu.make_async_remote_copy(
            src_ref=source(mask, piece),
            dst_ref=place(mask, piece),
            send_sem=send,
            recv_sem=recv.at[piece, slot],
            device_id=layout.device(1 << dim),
            device_id_type=MESH,
        )
        copy.start()
        sent.append(copy)
        return copy

    def relay(mask, piece, slot):
        copy = pltpu.make_async_remote_copy(
            src_ref=source(mask, piece),
            dst_ref=place(mask, piece),
            send_sem=send,
            recv_sem=relay_recv.at[piece, slot],
            device_id=layout.device(1),
            device_id_type=MESH,
        )
        copy.start()
        relayed.append(copy)

    first, second, third = {}, {}, {}
    for piece, (a, b, c) in enumerate(ORDERS):
        first[piece] = push(0, piece, 0, a)
    for piece, (a, b, c) in enumerate(ORDERS):
        second[piece] = [push(0, piece, 1, b)]
    for piece, (a, b, c) in enumerate(ORDERS):
        third[piece] = [push(0, piece, 3, c)]
    local = pltpu.make_async_copy(own_ref, dst_ref.at[rows_at(me * rows, rows)], own_sem)
    local.start()
    for piece in range(len(ORDERS)):
        relay(0, piece, 0)
    yield
    for piece, (a, b, c) in enumerate(ORDERS):
        first[piece].wait_recv()
        mask = span_mask((a,))
        second[piece].append(push(mask, piece, 2, b))
        third[piece].append(push(mask, piece, 4, c))
        relay(mask, piece, 1)
    yield
    for piece, (a, b, c) in enumerate(ORDERS):
        second[piece][0].wait_recv()
        mask = span_mask((b,))
        third[piece].append(push(mask, piece, 5, c))
        relay(mask, piece, 2)
    yield
    for piece, (a, b, c) in enumerate(ORDERS):
        second[piece][1].wait_recv()
        mask = span_mask((a, b))
        third[piece].append(push(mask, piece, 6, c))
        relay(mask, piece, 3)
    yield
    for turn, dims in enumerate(((2,), (0, 2), (1, 2), (0, 1, 2))):
        for piece, order in enumerate(ORDERS):
            third[piece][turn].wait_recv()
            relay(span_mask([order[d] for d in dims]), piece, 4 + turn)
    yield
    for copy in relayed:
        copy.wait_recv()
    local.wait()
    whole = dst_ref.at[pl.ds(0, 15 * rows)]
    pltpu.make_async_remote_copy(
        src_ref=whole,
        dst_ref=whole,
        send_sem=send,
        recv_sem=recv.at[0, 0],
        device_id=layout.device(1),
        device_id_type=MESH,
    ).wait_send()
    yield


def gather_sems():
    count = len(ORDERS)
    return [
        pltpu.SemaphoreType.DMA,
        pltpu.SemaphoreType.DMA((count, 7)),
        pltpu.SemaphoreType.DMA((count, 8)),
        pltpu.SemaphoreType.DMA,
    ]


def finish(steps):
    for _ in steps:
        pass


def scatter_steps(layout, rows, produce, total, buffers, sems):
    stage, core_in, arrive = buffers
    core_send, core_recv, send, recv = sems
    me = layout.member()
    core = me % 2
    own = pl.multiple_of(core * rows, 16)
    other = pl.multiple_of((1 - core) * rows, 16)
    copies = {}

    def chunked(start, size, body):
        @pl.loop(0, size // 16)
        def _(i):
            body(pl.multiple_of(i * 16 + start, 16))

    def push(piece, pair, dim, slot):
        start, size = PIECES[piece]
        copy = pltpu.make_async_remote_copy(
            src_ref=stage.at[pair, rows_at(own + start, size)],
            dst_ref=arrive.at[slot, pl.ds(start, size)],
            send_sem=send.at[piece, slot],
            recv_sem=recv.at[piece, slot],
            device_id=layout.device(1 << dim),
            device_id_type=MESH,
        )
        copy.start()
        return copy

    one, two, three = {}, {}, {}

    def settle(pair):
        copies[pair].wait_recv()

        def body(r):
            stage[pair, rows_at(own + r, 16)] = (
                stage[pair, rows_at(own + r, 16)].astype(jnp.float32)
                + core_in[pair, rows_at(r, 16)].astype(jnp.float32)
            ).astype(jnp.bfloat16)

        chunked(0, rows, body)
        mask = pair * 2
        for piece, (a, b, c) in enumerate(ORDERS):
            if mask & (1 << a):
                slot = (1 if mask & (1 << b) else 0) + (2 if mask & (1 << c) else 0)
                one[piece, slot] = push(piece, pair, a, slot)

    before = None
    for pair in PAIRS:
        produce(jnp.bitwise_xor(me // 2, pair), stage.at[pair])
        copies[pair] = pltpu.make_async_remote_copy(
            src_ref=stage.at[pair, rows_at(other, rows)],
            dst_ref=core_in.at[pair],
            send_sem=core_send.at[pair],
            recv_sem=core_recv.at[pair],
            device_id=layout.device(1),
            device_id_type=MESH,
        )
        copies[pair].start()
        if before is not None:
            settle(before)
        before = pair
    settle(before)
    yield

    def keep(piece, pair, slots):
        start, size = PIECES[piece]

        def body(r):
            value = stage[pair, rows_at(own + r, 16)].astype(jnp.float32)
            for slot in slots:
                value = value + arrive[slot, rows_at(r, 16)].astype(jnp.float32)
            stage[pair, rows_at(own + r, 16)] = value.astype(jnp.bfloat16)

        chunked(start, size, body)

    for piece, (a, b, c) in enumerate(ORDERS):
        for slot, dims in ((3, (b, c)), (1, (b,))):
            pair = span_mask(dims) // 2
            one[piece, slot].wait_recv()
            keep(piece, pair, (slot,))
            two[piece, slot] = push(piece, pair, b, 4 + slot // 2)
    yield
    for piece, (a, b, c) in enumerate(ORDERS):
        pair = span_mask((c,)) // 2
        one[piece, 2].wait_recv()
        two[piece, 3].wait_recv()
        keep(piece, pair, (2, 5))
        three[piece] = push(piece, pair, c, 6)
    yield
    for piece, (a, b, c) in enumerate(ORDERS):
        start, size = PIECES[piece]
        one[piece, 0].wait_recv()
        two[piece, 1].wait_recv()
        three[piece].wait_recv()

        def body(r):
            value = stage[0, rows_at(own + r, 16)].astype(jnp.float32)
            for slot in (0, 4, 6):
                value = value + arrive[slot, rows_at(r, 16)].astype(jnp.float32)
            total[rows_at(r, 16)] = value

        chunked(start, size, body)
    for group in (copies, one, two, three):
        for copy in group.values():
            copy.wait_send()
    yield


def scatter_scratch(rows, width):
    return [
        pltpu.VMEM((8, 2 * rows, width), jnp.bfloat16),
        pltpu.VMEM((8, rows, width), jnp.bfloat16),
        pltpu.VMEM((7, rows, width), jnp.bfloat16),
    ]


def scatter_sems():
    count = len(ORDERS)
    return [
        pltpu.SemaphoreType.DMA((8,)),
        pltpu.SemaphoreType.DMA((8,)),
        pltpu.SemaphoreType.DMA((count, 7)),
        pltpu.SemaphoreType.DMA((count, 7)),
    ]


def loop_rows(count, size, body):
    @pl.loop(0, count // size)
    def _(i):
        body(pl.ds(pl.multiple_of(i * size, size), size))


class Sizes:
    def __init__(self, layout, tokens, block_ids, w_query, w_gate):
        self.rows, self.width = tokens.shape[1], tokens.shape[2]
        self.length = block_ids.shape[1]
        self.depth = w_query.shape[0]
        self.hidden = w_gate.shape[1] // GROUP
        self.heads = H // GROUP
        self.query = self.heads * HD
        self.attn = 2 * self.query + 2 * HD
        self.all_rows = GROUP * self.rows
        self.span = max(128, min(self.length, 512 * 512 // self.length))
        self.kv_share = GROUP // KVH


def kv_half(layout, target, chunk):
    second = (target // (GROUP // KVH)) % 2 == 1
    return jnp.where(second, chunk[:, HD:], chunk[:, :HD])


def attention_scores(sizes, qkv, ids, seq, start, head):
    base = sizes.query
    keys_rows = rows_at(seq * sizes.length, sizes.length)
    query_rows = rows_at(seq * sizes.length + start, sizes.span)
    query = qkv[query_rows, head * HD : (head + 1) * HD]
    keys = qkv[keys_rows, base : base + HD]
    values = qkv[keys_rows, base + HD : base + 2 * HD]
    key_ids = ids[seq, 0:1, :]
    query_ids = jnp.transpose(ids[seq, :, pl.ds(start, sizes.span)])[:, :1]
    return query, keys, values, softmax(query, keys, query_ids, key_ids)


def front_kernel(
    layout,
    sizes,
    tok_ref,
    cot_ref,
    ids_ref,
    gains_ref,
    wq_ref,
    wk_ref,
    wv_ref,
    wo_ref,
    wg_ref,
    wu_ref,
    wd_ref,
    h1_out,
    h2_out,
    g_out,
    in_out,
    down_out,
    wa,
    qkv,
    attended,
    middle,
    gains,
    ids,
    x_all,
    tok,
    h2,
    wq,
    wk,
    wv,
    wo,
    pack,
    stage,
    core_in,
    arrive,
    x_send,
    x_recv,
    x_relay,
    x_own,
    h_send,
    h_recv,
    h_relay,
    h_own,
    g_send,
    g_recv,
    g_relay,
    g_own,
    core_send,
    core_recv,
    s_send,
    s_recv,
    attn_send,
    attn_recv,
    gain_send,
    gain_recv,
    id_send,
    id_recv,
    mlp_send,
    mlp_recv,
    load_sem,
):
    share, fsdp, depth = layout.share, layout.fsdp, sizes.depth
    seq_me, fsdp_me = lax.axis_index("seq"), lax.axis_index("fsdp")
    query = sizes.query
    rows, hidden = sizes.rows, sizes.hidden

    loads = []

    def load(src, dst):
        copy = pltpu.make_async_copy(src, dst, load_sem.at[len(loads)])
        copy.start()
        loads.append(copy)
        return copy

    def columns(ref, start, size):
        return ref.at[:, pl.ds(pl.multiple_of(start, 128), size)]

    load(tok_ref, tok)
    load(columns(wq_ref, seq_me * share * query, share * query), wq)
    load(columns(wo_ref, seq_me * share * query, share * query), wo)
    chunk = seq_me * share // (2 * sizes.kv_share) * 128
    load(columns(wk_ref, chunk, 128), wk)
    load(columns(wv_ref, chunk, 128), wv)
    own_rows = pl.ds(pl.multiple_of(fsdp_me * depth, 128), depth)
    load(gains_ref, gains.at[:, own_rows])
    load(ids_ref, ids.at[fsdp_me % share])
    greet_all(layout)
    x_steps = gather_steps(layout, rows, tok_ref, x_all, (x_send, x_recv, x_relay, x_own))
    next(x_steps)
    small = []
    for mask in range(1, fsdp):
        copy = pltpu.make_async_remote_copy(
            src_ref=gains_ref,
            dst_ref=gains.at[:, own_rows],
            send_sem=gain_send.at[mask],
            recv_sem=gain_recv.at[mask],
            device_id=layout.offset(0, mask),
            device_id_type=MESH,
        )
        copy.start()
        small.append(copy)
    for mask in range(1, share):
        copy = pltpu.make_async_remote_copy(
            src_ref=ids_ref,
            dst_ref=ids.at[fsdp_me % share],
            send_sem=id_send.at[mask],
            recv_sem=id_recv.at[mask],
            device_id=layout.offset(0, mask),
            device_id_type=MESH,
        )
        copy.start()
        small.append(copy)
    for copy in loads:
        copy.wait()
    for j in range(share):
        target = seq_me * share + j
        pack[j] = jnp.concatenate(
            [
                wq[:, j * query : (j + 1) * query],
                kv_half(layout, target, wk[...]),
                kv_half(layout, target, wv[...]),
                wo[:, j * query : (j + 1) * query],
            ],
            axis=1,
        )
    attn = []
    for mask in reversed(range(1, fsdp)):
        copy = pltpu.make_async_remote_copy(
            src_ref=pack.at[jnp.bitwise_xor(fsdp_me, mask) % share],
            dst_ref=wa.at[own_rows],
            send_sem=attn_send.at[mask],
            recv_sem=attn_recv.at[mask],
            device_id=layout.offset(0, mask),
            device_id_type=MESH,
        )
        copy.start()
        attn.append(copy)
    wa[own_rows] = pack[fsdp_me % share]
    finish(x_steps)
    for copy in small:
        copy.wait()

    gain_one = gains[0:1].astype(jnp.float32)

    def norm(r):
        values = x_all[r].astype(jnp.float32)
        x_all[r] = (values * rms_factor(values) * gain_one).astype(jnp.bfloat16)

    loop_rows(sizes.all_rows, 64, norm)
    h1_copy = pltpu.make_async_copy(x_all, h1_out, load_sem.at[0])
    h1_copy.start()
    for copy in attn:
        copy.wait()

    mlp = []

    def send_mlp(ref, out, place, index):
        def at(j):
            return columns(ref, (seq_me * share + j) * hidden, hidden)

        home = out.at[own_rows, pl.ds(place, hidden)]
        for mask in reversed(range(1, fsdp)):
            copy = pltpu.make_async_remote_copy(
                src_ref=at(jnp.bitwise_xor(fsdp_me, mask) % share),
                dst_ref=home,
                send_sem=mlp_send.at[index, mask],
                recv_sem=mlp_recv.at[index, mask],
                device_id=layout.offset(0, mask),
                device_id_type=MESH,
            )
            copy.start()
            mlp.append(copy)
        copy = pltpu.make_async_copy(at(fsdp_me % share), home, load_sem.at[1 + index])
        copy.start()
        mlp.append(copy)

    send_mlp(wg_ref, in_out, 0, 0)
    send_mlp(wu_ref, in_out, hidden, 1)
    send_mlp(wd_ref, down_out, 0, 2)

    def project(r):
        qkv[r] = dot(x_all[r], wa[:, : query + 2 * HD]).astype(jnp.bfloat16)

    loop_rows(sizes.all_rows, 256, project)

    blocks = sizes.length // sizes.span

    @pl.loop(0, share * blocks)
    def _(i):
        seq = i // blocks
        start = pl.multiple_of((i % blocks) * sizes.span, sizes.span)
        outs = []
        for head in range(sizes.heads):
            _, _, values, probs = attention_scores(sizes, qkv, ids, seq, start, head)
            outs.append(dot(probs.astype(jnp.bfloat16), values))
        attended[rows_at(seq * sizes.length + start, sizes.span)] = jnp.concatenate(
            outs, axis=1
        ).astype(jnp.bfloat16)

    def out_rows(pair, ref):
        block = attended[rows_at(pair * 2 * rows, 2 * rows)]

        @pl.loop(0, sizes.width // 512)
        def _(i):
            piece = pl.ds(pl.multiple_of(i * 512, 512), 512)
            ref[:, piece] = dot_cols(block, wa[piece, query + 2 * HD :]).astype(jnp.bfloat16)

    finish(
        scatter_steps(
            layout, rows, out_rows, middle, (stage, core_in, arrive),
            (core_send, core_recv, s_send, s_recv),
        )
    )
    gain_two = gains[8:9].astype(jnp.float32)

    def second(r):
        values = tok[r].astype(jnp.float32) + RESIDUAL * middle[r]
        middle[r] = values
        h2[r] = (values * rms_factor(values) * gain_two).astype(jnp.bfloat16)

    loop_rows(rows, 32, second)
    h_steps = gather_steps(layout, rows, h2, h2_out, (h_send, h_recv, h_relay, h_own))
    finish(h_steps)
    g_steps = gather_steps(layout, rows, cot_ref, g_out, (g_send, g_recv, g_relay, g_own))
    finish(g_steps)
    for copy in mlp:
        copy.wait()
    h1_copy.wait()


def front(layout, sizes, *args):
    width, count = sizes.width, sizes.all_rows
    hbm, vmem = pl.BlockSpec(memory_space=pl.ANY), pl.BlockSpec(memory_space=pltpu.VMEM)
    share, depth, fsdp = layout.share, sizes.depth, layout.fsdp
    bf16 = jnp.bfloat16
    shapes = [
        ((count, width), bf16, hbm),
        ((count, width), bf16, hbm),
        ((count, width), bf16, hbm),
        ((width, 2 * sizes.hidden), bf16, hbm),
        ((width, sizes.hidden), bf16, hbm),
        ((width, sizes.attn), bf16, vmem),
        ((count, sizes.query + 2 * HD), bf16, vmem),
        ((count, sizes.query), bf16, vmem),
        ((sizes.rows, width), jnp.float32, vmem),
        ((16, width), bf16, vmem),
        ((share, 8, sizes.length), jnp.int32, vmem),
    ]
    dma = pltpu.SemaphoreType.DMA
    return pl.pallas_call(
        functools.partial(front_kernel, layout, sizes),
        out_shape=[jax.ShapeDtypeStruct(shape, dtype) for shape, dtype, _ in shapes],
        in_specs=[hbm] * len(args),
        out_specs=[spec for _, _, spec in shapes],
        scratch_shapes=[
            pltpu.VMEM((count, width), bf16),
            pltpu.VMEM((sizes.rows, width), bf16),
            pltpu.VMEM((sizes.rows, width), bf16),
            pltpu.VMEM((depth, share * sizes.query), bf16),
            pltpu.VMEM((depth, 128), bf16),
            pltpu.VMEM((depth, 128), bf16),
            pltpu.VMEM((depth, share * sizes.query), bf16),
            pltpu.VMEM((share, depth, sizes.attn), bf16),
        ]
        + scatter_scratch(sizes.rows, width)
        + gather_sems() * 3
        + scatter_sems()
        + [dma((fsdp,)), dma((fsdp,)), dma((fsdp,)), dma((fsdp,))]
        + [dma((share,)), dma((share,)), dma((3, fsdp)), dma((3, fsdp)), dma((8,))],
        compiler_params=pltpu.CompilerParams(
            collective_id=3, has_side_effects=True, vmem_limit_bytes=56 * 1024 * 1024
        ),
        name="front",
    )(*args)


def seq_gather(layout, own_ref, out_ref, width, sems):
    send, recv, own_sem = sems
    me = lax.axis_index("seq")
    bits = [1 << bit for bit in reversed(range(layout.seq_bits))]

    def block(mask):
        start = jnp.bitwise_xor(me, mask) * width
        return out_ref.at[:, pl.ds(pl.multiple_of(start, 128), width)]

    copies = {}

    def push(mask, bit):
        copy = pltpu.make_async_remote_copy(
            src_ref=own_ref if mask == 0 else block(mask),
            dst_ref=block(mask),
            send_sem=send.at[mask ^ bit],
            recv_sem=recv.at[mask ^ bit],
            device_id=layout.offset(bit, 0),
            device_id_type=MESH,
        )
        copy.start()
        copies[mask ^ bit] = copy

    for bit in bits:
        push(0, bit)
    local = pltpu.make_async_copy(own_ref, block(0), own_sem)
    local.start()
    yield
    held = [0]
    for bit in bits:
        for mask in held[1:]:
            push(mask, bit)
        new = [mask ^ bit for mask in held]
        if bit != bits[-1]:
            for mask in new:
                copies[mask].wait_recv()
        held = held + new
    yield
    for mask in held[len(held) // 2 :]:
        copies[mask].wait_recv()
    for copy in copies.values():
        copy.wait_send()
    local.wait()
    yield


def back_kernel(
    layout,
    sizes,
    tok_ref,
    cot_ref,
    h1_ref,
    h2_ref,
    g_ref,
    in_ref,
    down_ref,
    wa_ref,
    qkv_ref,
    att_ref,
    mid_ref,
    gains_ref,
    ids_ref,
    mixed,
    grad_tok,
    gain_sum,
    gate_out,
    up_out,
    down_out,
    attn_out,
    in_recv,
    down_recv,
    attn_recv,
    g_all,
    h_all,
    w_in,
    w_down,
    wa,
    qkv,
    attended,
    hid,
    grad_in,
    middle,
    total,
    grad_mid,
    tok,
    cot,
    grad_loc,
    down_stage,
    gains,
    ids,
    grad_kv,
    terms,
    gain_in,
    gain_seq,
    stage,
    core_in,
    arrive,
    a_send,
    a_recv,
    a_relay,
    a_own,
    core_send,
    core_recv,
    s_send,
    s_recv,
    credit,
    grad_send,
    grad_recv,
    join_send,
    join_recv,
    join_own,
    gain_send,
    gain_recv,
    gs_send,
    gs_recv,
    load_sem,
    pick_sem,
):
    share, fsdp, depth = layout.share, layout.fsdp, sizes.depth
    seq_me, fsdp_me = lax.axis_index("seq"), lax.axis_index("fsdp")
    query, hidden, rows = sizes.query, sizes.hidden, sizes.rows
    base = query + 2 * HD
    count = sizes.all_rows
    scatter = (stage, core_in, arrive)
    scatter_sem = (core_send, core_recv, s_send, s_recv)

    loads = {}
    for name, src, dst in (
        ("in", in_ref, w_in),
        ("h", h2_ref, h_all),
        ("g", g_ref, g_all),
        ("down", down_ref, w_down),
        ("mid", mid_ref, middle),
        ("tok", tok_ref, tok),
        ("cot", cot_ref, cot),
        ("gains", gains_ref, gains),
        ("wa", wa_ref, wa),
        ("qkv", qkv_ref, qkv),
        ("att", att_ref, attended),
        ("ids", ids_ref, ids),
    ):
        loads[name] = pltpu.make_async_copy(src, dst, load_sem.at[len(loads)])
        loads[name].start()
    greet_all(layout)
    for name in ("in", "h", "g", "down"):
        loads[name].wait()

    def hidden_rows(r):
        h = h_all[r]
        gate = dot(h, w_in[:, :hidden])
        upward = dot(h, w_in[:, hidden:])
        grad = (RESIDUAL * g_all[r].astype(jnp.float32)).astype(jnp.bfloat16)
        g_all[r] = grad
        grad_hidden = dot(grad, w_down[...])
        sigma = jax.nn.sigmoid(gate)
        hid[r] = (gate * sigma * upward).astype(jnp.bfloat16)
        grad_in[r, hidden:] = (grad_hidden * gate * sigma).astype(jnp.bfloat16)
        grad_in[r, :hidden] = (
            grad_hidden * upward * sigma * (1.0 + gate * (1.0 - sigma))
        ).astype(jnp.bfloat16)

    loop_rows(count, 256, hidden_rows)

    sends = []
    far = list(reversed(range(1, fsdp))) + [0]

    def owner_columns(mask):
        start = jnp.bitwise_xor(fsdp_me, mask) * depth
        return pl.ds(pl.multiple_of(start, 128), depth)

    def send_grad(mask, src, dst, index):
        if mask == 0:
            return
        copy = pltpu.make_async_remote_copy(
            src_ref=src,
            dst_ref=dst.at[mask],
            send_sem=grad_send.at[index, mask],
            recv_sem=grad_recv.at[index, mask],
            device_id=layout.offset(0, mask),
            device_id_type=MESH,
        )
        copy.start()
        sends.append((index, mask, copy))

    def block(mask):
        return pl.ds(mask * depth, depth)

    def grad_down(mask):
        down_stage[block(mask)] = dot_rows(g_all[:, owner_columns(mask)], hid[...]).astype(
            jnp.bfloat16
        )
        send_grad(mask, down_stage.at[block(mask)], down_recv, 0)

    for mask in far:
        grad_down(mask)

    def hidden_back(pair, ref):
        left = grad_in[rows_at(pair * 2 * rows, 2 * rows)]

        @pl.loop(0, sizes.width // 512)
        def _(i):
            piece = pl.ds(pl.multiple_of(i * 512, 512), 512)
            ref[:, piece] = dot_cols(left, w_in[piece]).astype(jnp.bfloat16)

    steps = scatter_steps(layout, rows, hidden_back, total, scatter, scatter_sem)
    next(steps)

    def grad_up(mask):
        w_in[block(mask)] = dot_rows(h_all[:, owner_columns(mask)], grad_in[...]).astype(
            jnp.bfloat16
        )
        send_grad(mask, w_in.at[block(mask)], in_recv, 1)

    for turn in range(3):
        for mask in far[turn * 3 : turn * 3 + 3]:
            grad_up(mask)
        next(steps)
    finish(steps)
    h1_copy = pltpu.make_async_copy(h1_ref, h_all, load_sem.at[len(loads)])
    h1_copy.start()
    for name in ("mid", "tok", "cot", "gains", "wa", "qkv", "att", "ids"):
        loads[name].wait()
    gain_one = gains[0:1].astype(jnp.float32)
    gain_two = gains[8:9].astype(jnp.float32)
    terms[...] = jnp.zeros_like(terms)

    def norm_two(r):
        values, normed = middle[r], total[r]
        factor = rms_factor(values)
        terms[1:2] += jnp.sum(normed * values * factor, axis=0, keepdims=True)
        grad = cot[r].astype(jnp.float32) + norm_back(normed, values, factor, gain_two)
        grad_mid[r] = grad
        grad_loc[r] = (RESIDUAL * grad).astype(jnp.bfloat16)

    loop_rows(rows, 32, norm_two)
    finish(gather_steps(layout, rows, grad_loc, g_all, (a_send, a_recv, a_relay, a_own)))

    def down_rows(pair, ref):
        left = hid[rows_at(pair * 2 * rows, 2 * rows)]

        @pl.loop(0, sizes.width // 512)
        def _(i):
            piece = pl.ds(pl.multiple_of(i * 512, 512), 512)
            ref[:, piece] = dot_cols(left, w_down[piece]).astype(jnp.bfloat16)

    steps = scatter_steps(layout, rows, down_rows, total, scatter, scatter_sem)
    next(steps)

    blocks = sizes.length // sizes.span

    def attend_back_block(i):
        seq = i // blocks
        part = i % blocks
        start = pl.multiple_of(part * sizes.span, sizes.span)
        here = rows_at(seq * sizes.length + start, sizes.span)
        grad_out = dot(g_all[here], wa[:, base:]).astype(jnp.bfloat16)
        grads, grad_keys, grad_values = [], 0.0, 0.0
        for head in range(sizes.heads):
            left, keys, values, probs = attention_scores(sizes, qkv, ids, seq, start, head)
            grad = grad_out[:, head * HD : (head + 1) * HD]
            grad_probs = dot_cols(grad, values)
            centre = jnp.sum(probs * grad_probs, axis=1, keepdims=True)
            grad_scores = (probs * (grad_probs - centre)).astype(jnp.bfloat16)
            grads.append(dot(grad_scores, keys) * (1.0 / HD))
            grad_keys = grad_keys + dot_rows(grad_scores, left) * (1.0 / HD)
            grad_values = grad_values + dot_rows(probs.astype(jnp.bfloat16), grad)
        both = jnp.concatenate([grad_keys, grad_values], axis=1)

        @pl.when(part == 0)
        def _():
            grad_kv[...] = both

        @pl.when(part > 0)
        def _():
            grad_kv[...] += both

        qkv[here, :query] = jnp.concatenate(grads, axis=1).astype(jnp.bfloat16)

        @pl.when(part == blocks - 1)
        def _():
            qkv[rows_at(seq * sizes.length, sizes.length), query:] = grad_kv[...].astype(
                jnp.bfloat16
            )

    turns = share * blocks

    @pl.loop(0, turns // 2)
    def _(i):
        attend_back_block(i)

    next(steps)

    @pl.loop(turns // 2, turns)
    def _(i):
        attend_back_block(i)

    finish(steps)
    for bit in range(4):
        pl.semaphore_signal(
            credit, inc=1, device_id=layout.device(1 << bit), device_id_type=MESH
        )

    def mix(r):
        mixed[r] = (middle[r] + RESIDUAL * total[r]).astype(jnp.bfloat16)

    loop_rows(rows, 32, mix)
    pl.semaphore_wait(credit, 4)

    def qkv_back(pair, ref):
        left = qkv[rows_at(pair * 2 * rows, 2 * rows)]

        @pl.loop(0, sizes.width // 512)
        def _(i):
            piece = pl.ds(pl.multiple_of(i * 512, 512), 512)
            ref[:, piece] = dot_cols(left, wa[piece, :base]).astype(jnp.bfloat16)

    steps = scatter_steps(layout, rows, qkv_back, total, scatter, scatter_sem)
    next(steps)
    h1_copy.wait()

    def grad_attn(mask):
        cols = owner_columns(mask)
        w_down[block(mask), :base] = dot_rows(h_all[:, cols], qkv[...]).astype(jnp.bfloat16)
        w_down[block(mask), base : sizes.attn] = dot_rows(g_all[:, cols], attended[...]).astype(
            jnp.bfloat16
        )
        send_grad(mask, w_down.at[block(mask), pl.ds(0, sizes.attn)], attn_recv, 2)

    for turn in range(3):
        for mask in far[turn * 3 : turn * 3 + 3]:
            grad_attn(mask)
        next(steps)
    finish(steps)

    def norm_one(r):
        values, normed = tok[r].astype(jnp.float32), total[r]
        factor = rms_factor(values)
        terms[0:1] += jnp.sum(normed * values * factor, axis=0, keepdims=True)
        grad = grad_mid[r] + norm_back(normed, values, factor, gain_one)
        grad_tok[r] = grad.astype(jnp.bfloat16)

    loop_rows(rows, 32, norm_one)
    gain_copies = []
    for mask in range(1, fsdp):
        copy = pltpu.make_async_remote_copy(
            src_ref=terms.at[:, owner_columns(mask)],
            dst_ref=gain_in.at[mask],
            send_sem=gain_send.at[mask],
            recv_sem=gain_recv.at[mask],
            device_id=layout.offset(0, mask),
            device_id_type=MESH,
        )
        copy.start()
        gain_copies.append(copy)

    picks = []

    def fetch(index, src, width, place):
        for number, mask, copy in sends:
            if number == index:
                copy.wait_recv()
                pick = pltpu.make_async_copy(
                    src.at[mask],
                    h_all.at[block(mask), pl.ds(place, width)],
                    pick_sem.at[index, mask],
                )
                pick.start()
                picks.append((index, pick))

    def combine(index, own_ref, own_at, width, place, slot):
        for number, pick in picks:
            if number == index:
                pick.wait()
        mine = fsdp_me % share
        for low in range(share):
            value = 0.0
            for mask in range(low, fsdp, share):
                if mask:
                    piece = h_all[block(mask), place : place + width]
                else:
                    piece = own_ref[block(0), own_at : own_at + width]
                value = value + piece.astype(jnp.float32)
            start = pl.multiple_of(jnp.bitwise_xor(mine, low) * width, 128)
            stage[slot, :, pl.ds(start, width)] = value.astype(jnp.bfloat16)

    def join(index, width, out):
        sems = (join_send.at[index], join_recv.at[index], join_own.at[index])
        return seq_gather(
            layout, stage.at[index, :, pl.ds(0, share * width)], out, share * width, sems
        )

    fetch(0, down_recv, hidden, 2 * hidden)
    combine(0, down_stage, 0, hidden, 2 * hidden, 0)
    joins = [join(0, hidden, down_out)]
    next(joins[0])
    fetch(1, in_recv, 2 * hidden, 0)
    for pick_index in (1, 2):
        combine(1, w_in, (pick_index - 1) * hidden, hidden, (pick_index - 1) * hidden, pick_index)
        picks.clear()
        joins.append(join(pick_index, hidden, gate_out if pick_index == 1 else up_out))
        next(joins[-1])
    fetch(2, attn_recv, sizes.attn, 3 * hidden)
    combine(2, w_down, 0, sizes.attn, 3 * hidden, 3)
    joins.append(join(3, sizes.attn, attn_out))
    next(joins[-1])

    value = terms[:, owner_columns(0)]
    for copy in gain_copies:
        copy.wait()
    for mask in range(1, fsdp):
        value = value + gain_in[mask]
    for bit in range(layout.seq_bits):
        gain_seq[2 * bit] = value
        copy = pltpu.make_async_remote_copy(
            src_ref=gain_seq.at[2 * bit],
            dst_ref=gain_seq.at[2 * bit + 1],
            send_sem=gs_send.at[bit],
            recv_sem=gs_recv.at[bit],
            device_id=layout.offset(1 << bit, 0),
            device_id_type=MESH,
        )
        copy.start()
        copy.wait()
        value = value + gain_seq[2 * bit + 1]
    gain_sum[...] = value
    for steps in joins:
        next(steps)
    for steps in joins:
        finish(steps)
    for _, _, copy in sends:
        copy.wait_send()


def back(layout, sizes, *args):
    width, count = sizes.width, sizes.all_rows
    hbm, vmem = pl.BlockSpec(memory_space=pl.ANY), pl.BlockSpec(memory_space=pltpu.VMEM)
    share, depth, fsdp = layout.share, sizes.depth, layout.fsdp
    rows, hidden, base = sizes.rows, sizes.hidden, sizes.query + 2 * HD
    bf16, f32 = jnp.bfloat16, jnp.float32
    shapes = [
        ((rows, width), bf16, vmem),
        ((rows, width), bf16, vmem),
        ((8, depth), f32, vmem),
        ((depth, GROUP * hidden), bf16, hbm),
        ((depth, GROUP * hidden), bf16, hbm),
        ((depth, GROUP * hidden), bf16, hbm),
        ((depth, GROUP * sizes.attn), bf16, hbm),
        ((fsdp, depth, 2 * hidden), bf16, hbm),
        ((fsdp, depth, hidden), bf16, hbm),
        ((fsdp, depth, sizes.attn), bf16, hbm),
    ]
    dma = pltpu.SemaphoreType.DMA
    seq = layout.seq
    return pl.pallas_call(
        functools.partial(back_kernel, layout, sizes),
        out_shape=[jax.ShapeDtypeStruct(shape, dtype) for shape, dtype, _ in shapes],
        in_specs=[hbm] * len(args),
        out_specs=[spec for _, _, spec in shapes],
        scratch_shapes=[
            pltpu.VMEM((count, width), bf16),
            pltpu.VMEM((count, width), bf16),
            pltpu.VMEM((width, 2 * hidden), bf16),
            pltpu.VMEM((width, hidden), bf16),
            pltpu.VMEM((width, sizes.attn), bf16),
            pltpu.VMEM((count, base), bf16),
            pltpu.VMEM((count, sizes.query), bf16),
            pltpu.VMEM((count, hidden), bf16),
            pltpu.VMEM((count, 2 * hidden), bf16),
            pltpu.VMEM((rows, width), f32),
            pltpu.VMEM((rows, width), f32),
            pltpu.VMEM((rows, width), f32),
            pltpu.VMEM((rows, width), bf16),
            pltpu.VMEM((rows, width), bf16),
            pltpu.VMEM((rows, width), bf16),
            pltpu.VMEM((width, hidden), bf16),
            pltpu.VMEM((16, width), bf16),
            pltpu.VMEM((share, 8, sizes.length), jnp.int32),
            pltpu.VMEM((sizes.length, 2 * HD), f32),
            pltpu.VMEM((8, width), f32),
            pltpu.VMEM((fsdp, 8, depth), f32),
            pltpu.VMEM((2 * layout.seq_bits, 8, depth), f32),
        ]
        + scatter_scratch(rows, width)
        + gather_sems()
        + scatter_sems()
        + [pltpu.SemaphoreType.REGULAR]
        + [dma((3, fsdp)), dma((3, fsdp)), dma((4, seq)), dma((4, seq)), dma((4,))]
        + [dma((fsdp,)), dma((fsdp,)), dma((layout.seq_bits,)), dma((layout.seq_bits,))]
        + [dma((16,)), dma((3, fsdp))],
        compiler_params=pltpu.CompilerParams(
            collective_id=4, has_side_effects=True, vmem_limit_bytes=62 * 1024 * 1024
        ),
        name="back",
    )(*args)


def body(
    tokens,
    block_ids,
    gain_attn,
    w_query,
    w_key,
    w_value,
    w_out,
    gain_mlp,
    w_gate,
    w_up,
    w_down,
    cotangent,
):
    layout = Layout(lax.axis_size("seq"), lax.axis_size("fsdp"))
    depth = w_gate.shape[0]
    sizes = Sizes(layout, tokens, block_ids, w_query, w_gate)
    gains_own = jnp.concatenate(
        [jnp.broadcast_to(gain[None], (8, depth)) for gain in (gain_attn, gain_mlp)], axis=0
    )
    ids_own = jnp.broadcast_to(block_ids, (8, block_ids.shape[1]))
    (
        normed_one,
        normed_two,
        grad_all,
        in_all,
        down_all,
        attn_all,
        qkv,
        attended,
        middle,
        gains_all,
        ids_all,
    ) = front(
        layout,
        sizes,
        tokens[0],
        cotangent[0],
        ids_own,
        gains_own,
        w_query,
        w_key,
        w_value,
        w_out,
        w_gate,
        w_up,
        w_down,
    )
    mixed, grad_tokens, gain_sum, grad_gate, grad_up, grad_down, grad_attn, _, _, _ = back(
        layout,
        sizes,
        tokens[0],
        cotangent[0],
        normed_one,
        normed_two,
        grad_all,
        in_all,
        down_all,
        attn_all,
        qkv,
        attended,
        middle,
        gains_all,
        ids_all,
    )
    parts = grad_attn.reshape(depth, GROUP, sizes.attn)
    query, base = sizes.query, sizes.query + 2 * HD

    def flat(columns):
        return columns.astype(jnp.float32).reshape(depth, -1)

    def shared(columns):
        pairs = columns.astype(jnp.float32).reshape(depth, KVH, sizes.kv_share, HD)
        return jnp.sum(pairs, axis=2).reshape(depth, -1)

    return (
        mixed[None],
        grad_tokens[None],
        gain_sum[0],
        flat(parts[:, :, :query]),
        shared(parts[:, :, query : query + HD]),
        shared(parts[:, :, query + HD : base]),
        flat(parts[:, :, base:]),
        gain_sum[1],
        flat(grad_gate),
        flat(grad_up),
        flat(grad_down),
    )


def solution(mesh):
    tokens, rows = P("fsdp", "seq", None), P("fsdp", None)
    return jax.shard_map(
        body,
        mesh=mesh,
        in_specs=(tokens, rows, P("fsdp"), rows, rows, rows, rows, P("fsdp"), rows, rows, rows, tokens),
        out_specs=(tokens, tokens, P("fsdp"), rows, rows, rows, rows, P("fsdp"), rows, rows, rows),
        check_vma=False,
    )
```

```python
import functools

import jax
import jax.numpy as jnp
from jax import lax
from jax.experimental import pallas as pl
from jax.experimental.pallas import tpu as pltpu
from jax.sharding import PartitionSpec as P

H = 32
KVH = 8
HD = 64
EPSILON = 1e-05
RESIDUAL = 0.22
GROUP = 16
MESH = pl.DeviceIdType.MESH
FIRST_PLAN = ((0, 48, (3, 2, 1)), (48, 48, (3, 1, 2)), (96, 32, (3, 2, 1)))
COTANGENT_PLAN = ((0, 48, (3, 2, 1)), (48, 48, (3, 1, 2)), (96, 32, (3, 2, 1)))
BRANCH_PLAN = ((0, 48, (1, 2, 3)), (48, 48, (2, 1, 3)), (96, 32, (1, 2, 3)))
SECOND_PLAN = ((0, 48, (3, 2, 1)), (48, 48, (3, 1, 2)), (96, 32, (3, 2, 1)))
HIDDEN_PLAN = ((0, 48, (1, 2, 3)), (48, 48, (2, 1, 3)), (96, 32, (1, 2, 3)))
MIDDLE_PLAN = ((0, 48, (3, 2, 1)), (48, 48, (3, 1, 2)), (96, 32, (3, 2, 1)))
DOWN_PLAN = ((0, 48, (1, 2, 3)), (48, 48, (2, 3, 1)), (96, 32, (3, 1, 2)))
LAST_PLAN = ((0, 48, (1, 2, 3)), (48, 48, (2, 3, 1)), (96, 32, (3, 1, 2)))
PLAN_PIECES = 4
PAIRS = (7, 6, 5, 3, 4, 2, 1, 0)


def dot(left, right):
    return jnp.dot(left, right, preferred_element_type=jnp.float32)


def dot_cols(left, right):
    return lax.dot_general(
        left, right, (((1,), (1,)), ((), ())), preferred_element_type=jnp.float32
    )


def dot_rows(left, right):
    return lax.dot_general(
        left, right, (((0,), (0,)), ((), ())), preferred_element_type=jnp.float32
    )


def rms_factor(values):
    return lax.rsqrt(jnp.mean(values * values, axis=1, keepdims=True) + EPSILON)


def norm_back(grad_normed, values, factor, gain):
    weighted = grad_normed * gain
    centre = jnp.mean(weighted * values, axis=1, keepdims=True)
    return factor * weighted - values * (factor * factor * factor) * centre


class Layout:
    def __init__(self, seq_count, fsdp_count):
        self.seq = seq_count
        self.fsdp = fsdp_count
        self.share = GROUP // seq_count
        self.seq_bits = seq_count.bit_length() - 1

    def member(self):
        return lax.axis_index("seq") + self.seq * (lax.axis_index("fsdp") % self.share)

    def offset(self, low, high):
        return {
            "seq": jnp.bitwise_xor(lax.axis_index("seq"), low),
            "fsdp": jnp.bitwise_xor(lax.axis_index("fsdp"), high),
        }

    def device(self, mask):
        return self.offset(mask % self.seq, mask // self.seq)


def span_mask(dims):
    return sum(1 << d for d in dims)


def softmax(query, keys, query_ids, key_ids):
    scores = dot_cols(query, keys) * (1.0 / HD)
    scores = jnp.where(key_ids <= query_ids, scores, -1e30)
    shifted = jnp.exp(scores - jnp.max(scores, axis=1, keepdims=True))
    return shifted / jnp.sum(shifted, axis=1, keepdims=True)


def rows_at(start, size):
    return pl.ds(pl.multiple_of(start, 16), size)


def greet_all(layout):
    pairs = [(1 << bit, 0) for bit in range(layout.seq_bits)]
    pairs += [(0, mask) for mask in range(1, layout.fsdp)]
    barrier = pltpu.get_barrier_semaphore()
    for low, high in pairs:
        pl.semaphore_signal(
            barrier, inc=1, device_id=layout.offset(low, high), device_id_type=MESH
        )
    pl.semaphore_wait(barrier, len(pairs))


def gather_steps(layout, rows, plan, own_ref, dst_ref, sems):
    send, recv, relay_recv, own_sem = sems
    me = layout.member()
    sent, relayed = [], []

    def place(mask, piece):
        start, size, _ = plan[piece]
        block = jnp.bitwise_xor(me, mask)
        return dst_ref.at[rows_at(block * rows + start, size)]

    def source(mask, piece):
        start, size, _ = plan[piece]
        return own_ref.at[pl.ds(start, size)] if mask == 0 else place(mask, piece)

    def push(mask, piece, slot, dim):
        copy = pltpu.make_async_remote_copy(
            src_ref=source(mask, piece),
            dst_ref=place(mask, piece),
            send_sem=send,
            recv_sem=recv.at[piece, slot],
            device_id=layout.device(1 << dim),
            device_id_type=MESH,
        )
        copy.start()
        sent.append(copy)
        return copy

    def relay(mask, piece, slot):
        copy = pltpu.make_async_remote_copy(
            src_ref=source(mask, piece),
            dst_ref=place(mask, piece),
            send_sem=send,
            recv_sem=relay_recv.at[piece, slot],
            device_id=layout.device(1),
            device_id_type=MESH,
        )
        copy.start()
        relayed.append(copy)

    first, second, third = {}, {}, {}
    for piece, (_, _, (a, b, c)) in enumerate(plan):
        first[piece] = push(0, piece, 0, a)
    for piece, (_, _, (a, b, c)) in enumerate(plan):
        second[piece] = [push(0, piece, 1, b)]
    for piece, (_, _, (a, b, c)) in enumerate(plan):
        third[piece] = [push(0, piece, 3, c)]
    local = pltpu.make_async_copy(own_ref, dst_ref.at[rows_at(me * rows, rows)], own_sem)
    local.start()
    for piece in range(len(plan)):
        relay(0, piece, 0)
    yield
    for piece, (_, _, (a, b, c)) in enumerate(plan):
        first[piece].wait_recv()
        mask = span_mask((a,))
        second[piece].append(push(mask, piece, 2, b))
        third[piece].append(push(mask, piece, 4, c))
        relay(mask, piece, 1)
    yield
    for piece, (_, _, (a, b, c)) in enumerate(plan):
        second[piece][0].wait_recv()
        mask = span_mask((b,))
        third[piece].append(push(mask, piece, 5, c))
        relay(mask, piece, 2)
    yield
    for piece, (_, _, (a, b, c)) in enumerate(plan):
        second[piece][1].wait_recv()
        mask = span_mask((a, b))
        third[piece].append(push(mask, piece, 6, c))
        relay(mask, piece, 3)
    yield
    for turn, dims in enumerate(((2,), (0, 2), (1, 2), (0, 1, 2))):
        for piece, (_, _, order) in enumerate(plan):
            third[piece][turn].wait_recv()
            relay(span_mask([order[d] for d in dims]), piece, 4 + turn)
    yield
    for copy in relayed:
        copy.wait_recv()
    local.wait()
    whole = dst_ref.at[pl.ds(0, 15 * rows)]
    pltpu.make_async_remote_copy(
        src_ref=whole,
        dst_ref=whole,
        send_sem=send,
        recv_sem=recv.at[0, 0],
        device_id=layout.device(1),
        device_id_type=MESH,
    ).wait_send()
    yield


def gather_sems():
    count = PLAN_PIECES
    return [
        pltpu.SemaphoreType.DMA,
        pltpu.SemaphoreType.DMA((count, 7)),
        pltpu.SemaphoreType.DMA((count, 8)),
        pltpu.SemaphoreType.DMA,
    ]


def finish(steps):
    for _ in steps:
        pass


def scatter_steps(layout, rows, plan, produce, total, buffers, tail, sems):
    stage, core_in, arrive = buffers
    last_out, last_in = tail
    core_send, core_recv, send, recv, last_send, last_recv = sems
    me = layout.member()
    core = me % 2
    own = pl.multiple_of(core * rows, 16)
    other = pl.multiple_of((1 - core) * rows, 16)
    copies = {}

    def chunked(start, size, body):
        @pl.loop(0, size // 16)
        def _(i):
            body(pl.multiple_of(i * 16 + start, 16))

    def push(piece, pair, dim, slot):
        start, size, _ = plan[piece]
        copy = pltpu.make_async_remote_copy(
            src_ref=stage.at[pair, rows_at(own + start, size)],
            dst_ref=arrive.at[slot, pl.ds(start, size)],
            send_sem=send.at[piece, slot],
            recv_sem=recv.at[piece, slot],
            device_id=layout.device(1 << dim),
            device_id_type=MESH,
        )
        copy.start()
        return copy

    one, two, three = {}, {}, {}

    def settle(pair):
        copies[pair].wait_recv()

        def body(r):
            stage[pair, rows_at(own + r, 16)] = (
                stage[pair, rows_at(own + r, 16)].astype(jnp.float32)
                + core_in[pair, rows_at(r, 16)].astype(jnp.float32)
            ).astype(jnp.bfloat16)

        chunked(0, rows, body)
        mask = pair * 2
        for piece, (_, _, (a, b, c)) in enumerate(plan):
            if mask & (1 << a):
                slot = (1 if mask & (1 << b) else 0) + (2 if mask & (1 << c) else 0)
                one[piece, slot] = push(piece, pair, a, slot)

    before = None
    for pair in PAIRS:
        produce(jnp.bitwise_xor(me // 2, pair), stage.at[pair])
        copies[pair] = pltpu.make_async_remote_copy(
            src_ref=stage.at[pair, rows_at(other, rows)],
            dst_ref=core_in.at[pair],
            send_sem=core_send.at[pair],
            recv_sem=core_recv.at[pair],
            device_id=layout.device(1),
            device_id_type=MESH,
        )
        copies[pair].start()
        if before is not None:
            settle(before)
        before = pair
    settle(before)
    yield

    def keep(piece, pair, slots):
        start, size, _ = plan[piece]

        def body(r):
            value = stage[pair, rows_at(own + r, 16)].astype(jnp.float32)
            for slot in slots:
                value = value + arrive[slot, rows_at(r, 16)].astype(jnp.float32)
            stage[pair, rows_at(own + r, 16)] = value.astype(jnp.bfloat16)

        chunked(start, size, body)

    for piece, (_, _, (a, b, c)) in enumerate(plan):
        for slot, dims in ((3, (b, c)), (1, (b,))):
            pair = span_mask(dims) // 2
            one[piece, slot].wait_recv()
            keep(piece, pair, (slot,))
            two[piece, slot] = push(piece, pair, b, 4 + slot // 2)
    yield
    for piece, (start, size, (a, b, c)) in enumerate(plan):
        pair = span_mask((c,)) // 2
        one[piece, 2].wait_recv()
        two[piece, 3].wait_recv()

        def onward(r):
            value = stage[pair, rows_at(own + r, 16)].astype(jnp.float32)
            for slot in (2, 5):
                value = value + arrive[slot, rows_at(r, 16)].astype(jnp.float32)
            last_out[rows_at(r, 16)] = value.astype(jnp.bfloat16)

        chunked(start, size, onward)
        three[piece] = pltpu.make_async_remote_copy(
            src_ref=last_out.at[pl.ds(start, size)],
            dst_ref=last_in.at[pl.ds(start, size)],
            send_sem=last_send.at[piece],
            recv_sem=last_recv.at[piece],
            device_id=layout.device(1 << c),
            device_id_type=MESH,
        )
        three[piece].start()
    for piece, (start, size, (a, b, c)) in enumerate(plan):
        one[piece, 0].wait_recv()
        two[piece, 1].wait_recv()

        def gathered(r):
            value = stage[0, rows_at(own + r, 16)].astype(jnp.float32)
            for slot in (0, 4):
                value = value + arrive[slot, rows_at(r, 16)].astype(jnp.float32)
            total[rows_at(r, 16)] = value

        chunked(start, size, gathered)
    for group in (copies, one, two):
        for copy in group.values():
            copy.wait_send()
    yield
    for piece, (start, size, _) in enumerate(plan):
        three[piece].wait_recv()

        def finished(r):
            total[rows_at(r, 16)] += last_in[rows_at(r, 16)].astype(jnp.float32)

        chunked(start, size, finished)
    for copy in three.values():
        copy.wait_send()
    yield


def scatter_scratch(rows, width):
    return [
        pltpu.VMEM((8, 2 * rows, width), jnp.bfloat16),
        pltpu.VMEM((8, rows, width), jnp.bfloat16),
        pltpu.VMEM((6, rows, width), jnp.bfloat16),
        pltpu.VMEM((rows, width), jnp.bfloat16),
        pltpu.VMEM((rows, width), jnp.bfloat16),
    ]


def scatter_sems():
    count = PLAN_PIECES
    return [
        pltpu.SemaphoreType.DMA((8,)),
        pltpu.SemaphoreType.DMA((8,)),
        pltpu.SemaphoreType.DMA((count, 6)),
        pltpu.SemaphoreType.DMA((count, 6)),
        pltpu.SemaphoreType.DMA((count,)),
        pltpu.SemaphoreType.DMA((count,)),
    ]


def loop_rows(count, size, body):
    @pl.loop(0, count // size)
    def _(i):
        body(pl.ds(pl.multiple_of(i * size, size), size))


class Sizes:
    def __init__(self, layout, tokens, block_ids, w_query, w_gate):
        self.rows, self.width = tokens.shape[1], tokens.shape[2]
        self.length = block_ids.shape[1]
        self.depth = w_query.shape[0]
        self.hidden = w_gate.shape[1] // GROUP
        self.heads = H // GROUP
        self.query = self.heads * HD
        self.attn = 2 * self.query + 2 * HD
        self.all_rows = GROUP * self.rows
        self.span = max(128, min(self.length, 512 * 512 // self.length))
        self.kv_share = GROUP // KVH

    def kv_columns(self, layout):
        return max(1, layout.share // self.kv_share) * HD

    def attn_joined(self, layout):
        return 2 * layout.share * self.query + 2 * self.kv_columns(layout)


def kv_half(layout, target, chunk):
    second = (target // (GROUP // KVH)) % 2 == 1
    return jnp.where(second, chunk[:, HD:], chunk[:, :HD])


def attention_scores(sizes, qkv, ids, seq, start, head):
    base = sizes.query
    keys_rows = rows_at(seq * sizes.length, sizes.length)
    query_rows = rows_at(seq * sizes.length + start, sizes.span)
    query = qkv[query_rows, head * HD : (head + 1) * HD]
    keys = qkv[keys_rows, base : base + HD]
    values = qkv[keys_rows, base + HD : base + 2 * HD]
    key_ids = ids[seq, 0:1, :]
    query_ids = jnp.transpose(ids[seq, :, pl.ds(start, sizes.span)])[:, :1]
    return query, keys, values, softmax(query, keys, query_ids, key_ids)


def front_kernel(
    layout,
    sizes,
    tok_ref,
    cot_ref,
    ids_ref,
    gains_ref,
    wq_ref,
    wk_ref,
    wv_ref,
    wo_ref,
    wg_ref,
    wu_ref,
    wd_ref,
    h1_out,
    h2_out,
    g_out,
    in_out,
    down_out,
    wa,
    qkv,
    attended,
    middle,
    gains,
    ids,
    x_all,
    tok,
    h2,
    wq,
    wk,
    wv,
    wo,
    pack,
    stage,
    core_in,
    arrive,
    last_out,
    last_in,
    x_send,
    x_recv,
    x_relay,
    x_own,
    h_send,
    h_recv,
    h_relay,
    h_own,
    g_send,
    g_recv,
    g_relay,
    g_own,
    core_send,
    core_recv,
    s_send,
    s_recv,
    last_send,
    last_recv,
    attn_send,
    attn_recv,
    gain_send,
    gain_recv,
    id_send,
    id_recv,
    mlp_send,
    mlp_recv,
    load_sem,
):
    share, fsdp, depth = layout.share, layout.fsdp, sizes.depth
    seq_me, fsdp_me = lax.axis_index("seq"), lax.axis_index("fsdp")
    query = sizes.query
    rows, hidden = sizes.rows, sizes.hidden

    loads = []

    def load(src, dst):
        copy = pltpu.make_async_copy(src, dst, load_sem.at[len(loads)])
        copy.start()
        loads.append(copy)
        return copy

    def columns(ref, start, size):
        return ref.at[:, pl.ds(pl.multiple_of(start, 128), size)]

    load(tok_ref, tok)
    own_rows = pl.ds(pl.multiple_of(fsdp_me * depth, 128), depth)
    load(gains_ref, gains.at[:, own_rows])
    load(columns(wq_ref, seq_me * share * query, share * query), wq)
    load(columns(wo_ref, seq_me * share * query, share * query), wo)
    chunk = seq_me * share // (2 * sizes.kv_share) * 128
    load(columns(wk_ref, chunk, 128), wk)
    load(columns(wv_ref, chunk, 128), wv)
    load(ids_ref, ids.at[fsdp_me % share])
    greet_all(layout)
    small = []
    for mask in range(1, fsdp):
        copy = pltpu.make_async_remote_copy(
            src_ref=gains_ref,
            dst_ref=gains.at[:, own_rows],
            send_sem=gain_send.at[mask],
            recv_sem=gain_recv.at[mask],
            device_id=layout.offset(0, mask),
            device_id_type=MESH,
        )
        copy.start()
        small.append(copy)
    for copy in loads:
        copy.wait()
    for j in range(share):
        target = seq_me * share + j
        pack[j] = jnp.concatenate(
            [
                wq[:, j * query : (j + 1) * query],
                kv_half(layout, target, wk[...]),
                kv_half(layout, target, wv[...]),
                wo[:, j * query : (j + 1) * query],
            ],
            axis=1,
        )
    attn = []
    for mask in reversed(range(1, fsdp)):
        copy = pltpu.make_async_remote_copy(
            src_ref=pack.at[jnp.bitwise_xor(fsdp_me, mask) % share],
            dst_ref=wa.at[own_rows],
            send_sem=attn_send.at[mask],
            recv_sem=attn_recv.at[mask],
            device_id=layout.offset(0, mask),
            device_id_type=MESH,
        )
        copy.start()
        attn.append(copy)
    wa[own_rows] = pack[fsdp_me % share]
    for copy in small:
        copy.wait()
    gain_one = gains[0:1].astype(jnp.float32)

    def norm(r):
        values = tok[r].astype(jnp.float32)
        h2[r] = (values * rms_factor(values) * gain_one).astype(jnp.bfloat16)

    loop_rows(rows, 32, norm)
    x_steps = gather_steps(layout, rows, FIRST_PLAN, h2, x_all, (x_send, x_recv, x_relay, x_own))
    next(x_steps)
    id_copies = []
    for mask in range(1, share):
        copy = pltpu.make_async_remote_copy(
            src_ref=ids_ref,
            dst_ref=ids.at[fsdp_me % share],
            send_sem=id_send.at[mask],
            recv_sem=id_recv.at[mask],
            device_id=layout.offset(0, mask),
            device_id_type=MESH,
        )
        copy.start()
        id_copies.append(copy)
    g_steps = gather_steps(
        layout, rows, COTANGENT_PLAN, cot_ref, g_out, (g_send, g_recv, g_relay, g_own)
    )
    next(g_steps)
    next(x_steps)

    mlp = []

    def send_mlp(ref, out, place, index):
        def at(j):
            return columns(ref, (seq_me * share + j) * hidden, hidden)

        home = out.at[own_rows, pl.ds(place, hidden)]
        for mask in reversed(range(1, fsdp)):
            copy = pltpu.make_async_remote_copy(
                src_ref=at(jnp.bitwise_xor(fsdp_me, mask) % share),
                dst_ref=home,
                send_sem=mlp_send.at[index, mask],
                recv_sem=mlp_recv.at[index, mask],
                device_id=layout.offset(0, mask),
                device_id_type=MESH,
            )
            copy.start()
            mlp.append(copy)
        copy = pltpu.make_async_copy(at(fsdp_me % share), home, load_sem.at[1 + index])
        copy.start()
        mlp.append(copy)

    send_mlp(wg_ref, in_out, 0, 0)
    send_mlp(wu_ref, in_out, hidden, 1)
    finish(x_steps)
    h1_copy = pltpu.make_async_copy(x_all, h1_out, load_sem.at[0])
    h1_copy.start()
    next(g_steps)
    for copy in attn:
        copy.wait()

    def project(r):
        qkv[r] = dot(x_all[r], wa[:, : query + 2 * HD]).astype(jnp.bfloat16)

    loop_rows(sizes.all_rows, 256, project)
    next(g_steps)
    for copy in id_copies:
        copy.wait()

    blocks = sizes.length // sizes.span

    @pl.loop(0, share * blocks)
    def _(i):
        seq = i // blocks
        start = pl.multiple_of((i % blocks) * sizes.span, sizes.span)
        outs = []
        for head in range(sizes.heads):
            _, _, values, probs = attention_scores(sizes, qkv, ids, seq, start, head)
            outs.append(dot(probs.astype(jnp.bfloat16), values))
        attended[rows_at(seq * sizes.length + start, sizes.span)] = jnp.concatenate(
            outs, axis=1
        ).astype(jnp.bfloat16)

    def out_rows(pair, ref):
        block = attended[rows_at(pair * 2 * rows, 2 * rows)]

        @pl.loop(0, sizes.width // 512)
        def _(i):
            piece = pl.ds(pl.multiple_of(i * 512, 512), 512)
            ref[:, piece] = dot_cols(block, wa[piece, query + 2 * HD :]).astype(jnp.bfloat16)

    next(g_steps)
    next(g_steps)
    steps = scatter_steps(
        layout, rows, BRANCH_PLAN, out_rows, middle, (stage, core_in, arrive),
        (last_out, last_in), (core_send, core_recv, s_send, s_recv, last_send, last_recv),
    )
    next(steps)
    next(g_steps)
    finish(steps)
    gain_two = gains[8:9].astype(jnp.float32)

    def second(r):
        values = tok[r].astype(jnp.float32) + RESIDUAL * middle[r]
        middle[r] = values
        h2[r] = (values * rms_factor(values) * gain_two).astype(jnp.bfloat16)

    loop_rows(rows, 32, second)
    h_steps = gather_steps(
        layout, rows, SECOND_PLAN, h2, h2_out, (h_send, h_recv, h_relay, h_own)
    )
    next(h_steps)
    next(h_steps)
    send_mlp(wd_ref, down_out, 0, 2)
    finish(g_steps)
    finish(h_steps)
    for copy in mlp:
        copy.wait()
    h1_copy.wait()


def front(layout, sizes, *args):
    width, count = sizes.width, sizes.all_rows
    hbm, vmem = pl.BlockSpec(memory_space=pl.ANY), pl.BlockSpec(memory_space=pltpu.VMEM)
    share, depth, fsdp = layout.share, sizes.depth, layout.fsdp
    bf16 = jnp.bfloat16
    shapes = [
        ((count, width), bf16, hbm),
        ((count, width), bf16, hbm),
        ((count, width), bf16, hbm),
        ((width, 2 * sizes.hidden), bf16, hbm),
        ((width, sizes.hidden), bf16, hbm),
        ((width, sizes.attn), bf16, vmem),
        ((count, sizes.query + 2 * HD), bf16, vmem),
        ((count, sizes.query), bf16, vmem),
        ((sizes.rows, width), jnp.float32, vmem),
        ((16, width), bf16, vmem),
        ((share, 8, sizes.length), jnp.int32, vmem),
    ]
    dma = pltpu.SemaphoreType.DMA
    return pl.pallas_call(
        functools.partial(front_kernel, layout, sizes),
        out_shape=[jax.ShapeDtypeStruct(shape, dtype) for shape, dtype, _ in shapes],
        in_specs=[hbm] * len(args),
        out_specs=[spec for _, _, spec in shapes],
        scratch_shapes=[
            pltpu.VMEM((count, width), bf16),
            pltpu.VMEM((sizes.rows, width), bf16),
            pltpu.VMEM((sizes.rows, width), bf16),
            pltpu.VMEM((depth, share * sizes.query), bf16),
            pltpu.VMEM((depth, 128), bf16),
            pltpu.VMEM((depth, 128), bf16),
            pltpu.VMEM((depth, share * sizes.query), bf16),
            pltpu.VMEM((share, depth, sizes.attn), bf16),
        ]
        + scatter_scratch(sizes.rows, width)
        + gather_sems() * 3
        + scatter_sems()
        + [dma((fsdp,)), dma((fsdp,)), dma((fsdp,)), dma((fsdp,))]
        + [dma((share,)), dma((share,)), dma((3, fsdp)), dma((3, fsdp)), dma((8,))],
        compiler_params=pltpu.CompilerParams(
            collective_id=3, has_side_effects=True, vmem_limit_bytes=56 * 1024 * 1024
        ),
        name="front",
    )(*args)


def seq_gather(layout, out_ref, width, sems):
    send, recv = sems
    me = lax.axis_index("seq")
    bits = [1 << bit for bit in reversed(range(layout.seq_bits))]

    def block(mask):
        start = jnp.bitwise_xor(me, mask) * width
        return out_ref.at[:, pl.ds(pl.multiple_of(start, 128), width)]

    copies = {}

    def push(mask, bit):
        copy = pltpu.make_async_remote_copy(
            src_ref=block(mask),
            dst_ref=block(mask),
            send_sem=send.at[mask ^ bit],
            recv_sem=recv.at[mask ^ bit],
            device_id=layout.offset(bit, 0),
            device_id_type=MESH,
        )
        copy.start()
        copies[mask ^ bit] = copy

    for bit in bits:
        push(0, bit)
    yield
    held = [0]
    for bit in bits:
        for mask in held[1:]:
            push(mask, bit)
        new = [mask ^ bit for mask in held]
        if bit != bits[-1]:
            for mask in new:
                copies[mask].wait_recv()
        held = held + new
    yield
    for mask in held[len(held) // 2 :]:
        copies[mask].wait_recv()
    for copy in copies.values():
        copy.wait_send()
    yield


def back_kernel(
    layout,
    sizes,
    tok_ref,
    cot_ref,
    h1_ref,
    h2_ref,
    g_ref,
    in_ref,
    down_ref,
    wa_ref,
    qkv_ref,
    att_ref,
    mid_ref,
    gains_ref,
    ids_ref,
    mixed,
    grad_tok,
    gain_sum,
    gate_out,
    up_out,
    down_out,
    attn_out,
    gate_recv,
    up_recv,
    down_recv,
    attn_recv,
    g_all,
    h_all,
    w_in,
    w_down,
    wa,
    qkv,
    attended,
    hid,
    grad_in,
    middle,
    total,
    grad_mid,
    tok,
    down_stage,
    gains,
    ids,
    grad_kv,
    terms,
    gain_in,
    gain_seq,
    own_sum,
    stage,
    core_in,
    arrive,
    last_out,
    last_in,
    down_total,
    down_last_out,
    down_last_in,
    a_send,
    a_recv,
    a_relay,
    a_own,
    core_send,
    core_recv,
    s_send,
    s_recv,
    last_send,
    last_recv,
    down_last_send,
    down_last_recv,
    credit,
    grad_send,
    grad_recv,
    join_send,
    join_recv,
    own_sem,
    gain_send,
    gain_recv,
    gs_send,
    gs_recv,
    load_sem,
    pick_sem,
):
    share, fsdp, depth = layout.share, layout.fsdp, sizes.depth
    seq_me, fsdp_me = lax.axis_index("seq"), lax.axis_index("fsdp")
    query, hidden, rows = sizes.query, sizes.hidden, sizes.rows
    base = query + 2 * HD
    count = sizes.all_rows
    scatter = (stage, core_in, arrive)
    sems = (core_send, core_recv, s_send, s_recv)
    scatter_sem = sems + (last_send, last_recv)

    loads = {}
    for name, src, dst in (
        ("in", in_ref, w_in),
        ("h", h2_ref, h_all),
        ("g", g_ref, g_all),
        ("down", down_ref, w_down),
        ("mid", mid_ref, middle),
        ("tok", tok_ref, tok),
        ("cot", cot_ref, down_last_out),
        ("gains", gains_ref, gains),
        ("wa", wa_ref, wa),
        ("qkv", qkv_ref, qkv),
        ("att", att_ref, attended),
        ("ids", ids_ref, ids),
    ):
        loads[name] = pltpu.make_async_copy(src, dst, load_sem.at[len(loads)])
        loads[name].start()
    greet_all(layout)
    for name in ("in", "h", "g", "down"):
        loads[name].wait()

    def hidden_rows(r):
        h = h_all[r]
        gate = dot(h, w_in[:, :hidden])
        upward = dot(h, w_in[:, hidden:])
        grad = (RESIDUAL * g_all[r].astype(jnp.float32)).astype(jnp.bfloat16)
        g_all[r] = grad
        grad_hidden = dot(grad, w_down[...])
        sigma = jax.nn.sigmoid(gate)
        hid[r] = (gate * sigma * upward).astype(jnp.bfloat16)
        grad_in[r, hidden:] = (grad_hidden * gate * sigma).astype(jnp.bfloat16)
        grad_in[r, :hidden] = (
            grad_hidden * upward * sigma * (1.0 + gate * (1.0 - sigma))
        ).astype(jnp.bfloat16)

    loop_rows(count, 256, hidden_rows)

    sends = []
    far = list(reversed(range(1, fsdp))) + [0]

    def owner_columns(mask):
        start = jnp.bitwise_xor(fsdp_me, mask) * depth
        return pl.ds(pl.multiple_of(start, 128), depth)

    def send_grad(mask, src, dst, index):
        if mask == 0:
            return
        copy = pltpu.make_async_remote_copy(
            src_ref=src,
            dst_ref=dst.at[mask],
            send_sem=grad_send.at[index, mask],
            recv_sem=grad_recv.at[index, mask],
            device_id=layout.offset(0, mask),
            device_id_type=MESH,
        )
        copy.start()
        sends.append((index, mask, copy))

    def block(mask):
        return pl.ds(mask * depth, depth)

    def grad_down(mask):
        down_stage[block(mask)] = dot_rows(g_all[:, owner_columns(mask)], hid[...]).astype(
            jnp.bfloat16
        )
        send_grad(mask, down_stage.at[block(mask)], down_recv, 0)

    for mask in far:
        grad_down(mask)

    def hidden_back(pair, ref):
        left = grad_in[rows_at(pair * 2 * rows, 2 * rows)]

        @pl.loop(0, sizes.width // 512)
        def _(i):
            piece = pl.ds(pl.multiple_of(i * 512, 512), 512)
            ref[:, piece] = dot_cols(left, w_in[piece]).astype(jnp.bfloat16)

    steps = scatter_steps(layout, rows, HIDDEN_PLAN, hidden_back, total, scatter, (last_out, last_in), scatter_sem)
    next(steps)

    def grad_up(mask):
        w_in[block(mask)] = dot_rows(h_all[:, owner_columns(mask)], grad_in[...]).astype(
            jnp.bfloat16
        )

    for turn in range(3):
        for mask in far[turn * 3 : turn * 3 + 3]:
            grad_up(mask)
        next(steps)
    finish(steps)
    h1_copy = pltpu.make_async_copy(h1_ref, h_all, load_sem.at[len(loads)])
    h1_copy.start()
    for name in ("mid", "tok", "cot", "gains", "wa", "qkv", "att", "ids"):
        loads[name].wait()
    gain_one = gains[0:1].astype(jnp.float32)
    gain_two = gains[8:9].astype(jnp.float32)
    terms[...] = jnp.zeros_like(terms)

    def norm_two(r):
        values, normed = middle[r], total[r]
        factor = rms_factor(values)
        terms[1:2] += jnp.sum(normed * values * factor, axis=0, keepdims=True)
        grad = down_last_out[r].astype(jnp.float32) + norm_back(normed, values, factor, gain_two)
        grad_mid[r] = grad
        last_out[r] = (RESIDUAL * grad).astype(jnp.bfloat16)

    loop_rows(rows, 32, norm_two)
    a_steps = gather_steps(
        layout, rows, MIDDLE_PLAN, last_out, g_all, (a_send, a_recv, a_relay, a_own)
    )
    next(a_steps)
    next(a_steps)
    for mask in far:
        send_grad(mask, w_in.at[block(mask), pl.ds(0, hidden)], gate_recv, 1)
    for mask in far:
        send_grad(mask, w_in.at[block(mask), pl.ds(hidden, hidden)], up_recv, 2)
    finish(a_steps)

    def down_rows(pair, ref):
        left = hid[rows_at(pair * 2 * rows, 2 * rows)]

        @pl.loop(0, sizes.width // 512)
        def _(i):
            piece = pl.ds(pl.multiple_of(i * 512, 512), 512)
            ref[:, piece] = dot_cols(left, w_down[piece]).astype(jnp.bfloat16)

    steps_low = scatter_steps(
        layout, rows, DOWN_PLAN, down_rows, down_total, scatter, (down_last_out, down_last_in),
        sems + (down_last_send, down_last_recv),
    )
    next(steps_low)

    mine = fsdp_me % share

    def collect(index, src, width, own_piece, landing, combine, out, out_width):
        picks = []
        for number, mask, copy in sends:
            if number == index:
                copy.wait_recv()
                pick = pltpu.make_async_copy(
                    src.at[mask], landing.at[block(mask)], pick_sem.at[index, mask]
                )
                pick.start()
                picks.append(pick)
        yield
        for pick in picks:
            pick.wait()

        def terms_of(low, start, size):
            cols = pl.ds(start, size)
            value = own_piece[:, cols] if low == 0 else landing[block(low), cols]
            value = value.astype(jnp.float32)
            for mask in range(low + share, fsdp, share):
                value = value + landing[block(mask), cols].astype(jnp.float32)
            return value

        combine(terms_of, width)
        home = pl.multiple_of(seq_me * out_width, 128)
        local = pltpu.make_async_copy(
            own_sum.at[:, pl.ds(0, out_width)], out.at[:, pl.ds(home, out_width)], own_sem.at[index]
        )
        local.start()
        local.wait()
        yield from seq_gather(layout, out, out_width, (join_send.at[index], join_recv.at[index]))

    def place_columns(terms_of, width):
        for low in range(share):
            start = pl.multiple_of(jnp.bitwise_xor(mine, low) * width, 128)
            own_sum[:, pl.ds(start, width)] = terms_of(low, 0, width).astype(jnp.bfloat16)

    def place_attn(terms_of, width):
        for low in range(share):
            for source, target in ((0, 0), (base, share * query)):
                start = pl.multiple_of(target + jnp.bitwise_xor(mine, low) * query, 128)
                own_sum[:, pl.ds(start, query)] = terms_of(low, source, query).astype(
                    jnp.bfloat16
                )
        both = sizes.kv_columns(layout)
        at = 2 * share * query
        for source in (query, query + HD):
            heads = []
            for first in range(0, share, sizes.kv_share):
                value = terms_of(first, source, HD)
                for low in range(first + 1, min(share, first + sizes.kv_share)):
                    value = value + terms_of(low, source, HD)
                heads.append(value)
            value = heads[0]
            if len(heads) == 2:
                upper = mine // sizes.kv_share == 1
                value = jnp.concatenate(
                    [jnp.where(upper, heads[1], heads[0]), jnp.where(upper, heads[0], heads[1])],
                    axis=1,
                )
            own_sum[:, at : at + both] = value.astype(jnp.bfloat16)
            at += both

    joined = share * hidden
    steps_down = collect(
        0, down_recv, hidden, down_stage.at[block(0)], hid, place_columns, down_out, joined
    )
    next(steps_down)

    blocks = sizes.length // sizes.span

    def attend_back_block(i):
        seq = i // blocks
        part = i % blocks
        start = pl.multiple_of(part * sizes.span, sizes.span)
        here = rows_at(seq * sizes.length + start, sizes.span)
        grad_out = dot(g_all[here], wa[:, base:]).astype(jnp.bfloat16)
        grads, grad_keys, grad_values = [], 0.0, 0.0
        for head in range(sizes.heads):
            left, keys, values, probs = attention_scores(sizes, qkv, ids, seq, start, head)
            grad = grad_out[:, head * HD : (head + 1) * HD]
            grad_probs = dot_cols(grad, values)
            centre = jnp.sum(probs * grad_probs, axis=1, keepdims=True)
            grad_scores = (probs * (grad_probs - centre)).astype(jnp.bfloat16)
            grads.append(dot(grad_scores, keys) * (1.0 / HD))
            grad_keys = grad_keys + dot_rows(grad_scores, left) * (1.0 / HD)
            grad_values = grad_values + dot_rows(probs.astype(jnp.bfloat16), grad)
        both = jnp.concatenate([grad_keys, grad_values], axis=1)

        @pl.when(part == 0)
        def _():
            grad_kv[...] = both

        @pl.when(part > 0)
        def _():
            grad_kv[...] += both

        qkv[here, :query] = jnp.concatenate(grads, axis=1).astype(jnp.bfloat16)

        @pl.when(part == blocks - 1)
        def _():
            qkv[rows_at(seq * sizes.length, sizes.length), query:] = grad_kv[...].astype(
                jnp.bfloat16
            )

    turns = share * blocks

    @pl.loop(0, turns // 2)
    def _(i):
        attend_back_block(i)

    next(steps_down)
    next(steps_low)

    @pl.loop(turns // 2, turns)
    def _(i):
        attend_back_block(i)

    next(steps_low)
    for bit in range(4):
        pl.semaphore_signal(
            credit, inc=1, device_id=layout.device(1 << bit), device_id_type=MESH
        )

    next(steps_down)
    pl.semaphore_wait(credit, 4)

    def qkv_back(pair, ref):
        left = qkv[rows_at(pair * 2 * rows, 2 * rows)]

        @pl.loop(0, sizes.width // 512)
        def _(i):
            piece = pl.ds(pl.multiple_of(i * 512, 512), 512)
            ref[:, piece] = dot_cols(left, wa[piece, :base]).astype(jnp.bfloat16)

    h1_copy.wait()

    def grad_attn(mask):
        cols = owner_columns(mask)
        w_down[block(mask), :base] = dot_rows(h_all[:, cols], qkv[...]).astype(jnp.bfloat16)
        w_down[block(mask), base : sizes.attn] = dot_rows(g_all[:, cols], attended[...]).astype(
            jnp.bfloat16
        )
        send_grad(mask, w_down.at[block(mask), pl.ds(0, sizes.attn)], attn_recv, 3)

    for mask in far[: fsdp // 2]:
        grad_attn(mask)
    steps = scatter_steps(layout, rows, LAST_PLAN, qkv_back, total, scatter, (last_out, last_in), scatter_sem)
    next(steps)
    for mask in far[fsdp // 2 :]:
        grad_attn(mask)
    steps_gate = collect(
        1, gate_recv, hidden, w_in.at[block(0), pl.ds(0, hidden)], grad_in.at[:, pl.ds(0, hidden)],
        place_columns, gate_out, joined,
    )
    next(steps_gate)
    next(steps)
    next(steps_gate)
    next(steps)
    finish(steps)

    def norm_one(r):
        values, normed = tok[r].astype(jnp.float32), total[r]
        factor = rms_factor(values)
        terms[0:1] += jnp.sum(normed * values * factor, axis=0, keepdims=True)
        grad = grad_mid[r] + norm_back(normed, values, factor, gain_one)
        grad_tok[r] = grad.astype(jnp.bfloat16)

    loop_rows(rows, 32, norm_one)
    finish(steps_low)

    def mix(r):
        mixed[r] = (middle[r] + RESIDUAL * down_total[r]).astype(jnp.bfloat16)

    loop_rows(rows, 32, mix)
    gain_copies = []
    for mask in range(1, fsdp):
        copy = pltpu.make_async_remote_copy(
            src_ref=terms.at[:, owner_columns(mask)],
            dst_ref=gain_in.at[mask],
            send_sem=gain_send.at[mask],
            recv_sem=gain_recv.at[mask],
            device_id=layout.offset(0, mask),
            device_id_type=MESH,
        )
        copy.start()
        gain_copies.append(copy)

    steps_up = collect(
        2, up_recv, hidden, w_in.at[block(0), pl.ds(hidden, hidden)], grad_in.at[:, pl.ds(hidden, hidden)],
        place_columns, up_out, joined,
    )
    next(steps_up)
    next(steps_up)
    next(steps_gate)
    steps_attn = collect(
        3, attn_recv, sizes.attn, w_down.at[block(0), pl.ds(0, sizes.attn)], h_all.at[:, pl.ds(0, sizes.attn)],
        place_attn, attn_out, sizes.attn_joined(layout),
    )
    next(steps_attn)
    next(steps_attn)
    next(steps_up)

    value = terms[:, owner_columns(0)]
    for copy in gain_copies:
        copy.wait()
    for mask in range(1, fsdp):
        value = value + gain_in[mask]
    for bit in range(layout.seq_bits):
        gain_seq[2 * bit] = value
        copy = pltpu.make_async_remote_copy(
            src_ref=gain_seq.at[2 * bit],
            dst_ref=gain_seq.at[2 * bit + 1],
            send_sem=gs_send.at[bit],
            recv_sem=gs_recv.at[bit],
            device_id=layout.offset(1 << bit, 0),
            device_id_type=MESH,
        )
        copy.start()
        copy.wait()
        value = value + gain_seq[2 * bit + 1]
    gain_sum[...] = value
    for steps in (steps_attn, steps_down, steps_gate, steps_up):
        finish(steps)
    for _, _, copy in sends:
        copy.wait_send()


def back(layout, sizes, *args):
    width, count = sizes.width, sizes.all_rows
    hbm, vmem = pl.BlockSpec(memory_space=pl.ANY), pl.BlockSpec(memory_space=pltpu.VMEM)
    share, depth, fsdp = layout.share, sizes.depth, layout.fsdp
    rows, hidden, base = sizes.rows, sizes.hidden, sizes.query + 2 * HD
    bf16, f32 = jnp.bfloat16, jnp.float32
    shapes = [
        ((rows, width), bf16, vmem),
        ((rows, width), bf16, vmem),
        ((8, depth), f32, vmem),
        ((depth, GROUP * hidden), bf16, hbm),
        ((depth, GROUP * hidden), bf16, hbm),
        ((depth, GROUP * hidden), bf16, hbm),
        ((depth, layout.seq * sizes.attn_joined(layout)), bf16, hbm),
        ((fsdp, depth, hidden), bf16, hbm),
        ((fsdp, depth, hidden), bf16, hbm),
        ((fsdp, depth, hidden), bf16, hbm),
        ((fsdp, depth, sizes.attn), bf16, hbm),
    ]
    dma = pltpu.SemaphoreType.DMA
    seq = layout.seq
    return pl.pallas_call(
        functools.partial(back_kernel, layout, sizes),
        out_shape=[jax.ShapeDtypeStruct(shape, dtype) for shape, dtype, _ in shapes],
        in_specs=[hbm] * len(args),
        out_specs=[spec for _, _, spec in shapes],
        scratch_shapes=[
            pltpu.VMEM((count, width), bf16),
            pltpu.VMEM((count, width), bf16),
            pltpu.VMEM((width, 2 * hidden), bf16),
            pltpu.VMEM((width, hidden), bf16),
            pltpu.VMEM((width, sizes.attn), bf16),
            pltpu.VMEM((count, base), bf16),
            pltpu.VMEM((count, sizes.query), bf16),
            pltpu.VMEM((count, hidden), bf16),
            pltpu.VMEM((count, 2 * hidden), bf16),
            pltpu.VMEM((rows, width), f32),
            pltpu.VMEM((rows, width), f32),
            pltpu.VMEM((rows, width), f32),
            pltpu.VMEM((rows, width), bf16),
            pltpu.VMEM((width, hidden), bf16),
            pltpu.VMEM((16, width), bf16),
            pltpu.VMEM((share, 8, sizes.length), jnp.int32),
            pltpu.VMEM((sizes.length, 2 * HD), f32),
            pltpu.VMEM((8, width), f32),
            pltpu.VMEM((fsdp, 8, depth), f32),
            pltpu.VMEM((2 * layout.seq_bits, 8, depth), f32),
            pltpu.VMEM((depth, share * max(hidden, 2 * sizes.query + 2 * HD)), bf16),
        ]
        + scatter_scratch(rows, width)
        + [
            pltpu.VMEM((rows, width), f32),
            pltpu.VMEM((rows, width), bf16),
            pltpu.VMEM((rows, width), bf16),
        ]
        + gather_sems()
        + scatter_sems()
        + [dma((PLAN_PIECES,)), dma((PLAN_PIECES,))]
        + [pltpu.SemaphoreType.REGULAR]
        + [dma((4, fsdp)), dma((4, fsdp)), dma((4, seq)), dma((4, seq)), dma((4,))]
        + [dma((fsdp,)), dma((fsdp,)), dma((layout.seq_bits,)), dma((layout.seq_bits,))]
        + [dma((16,)), dma((4, fsdp))],
        compiler_params=pltpu.CompilerParams(
            collective_id=4, has_side_effects=True, vmem_limit_bytes=62 * 1024 * 1024
        ),
        name="back",
    )(*args)


def body(
    tokens,
    block_ids,
    gain_attn,
    w_query,
    w_key,
    w_value,
    w_out,
    gain_mlp,
    w_gate,
    w_up,
    w_down,
    cotangent,
):
    layout = Layout(lax.axis_size("seq"), lax.axis_size("fsdp"))
    depth = w_gate.shape[0]
    sizes = Sizes(layout, tokens, block_ids, w_query, w_gate)
    gains_own = jnp.concatenate(
        [jnp.broadcast_to(gain[None], (8, depth)) for gain in (gain_attn, gain_mlp)], axis=0
    )
    ids_own = jnp.broadcast_to(block_ids, (8, block_ids.shape[1]))
    (
        normed_one,
        normed_two,
        grad_all,
        in_all,
        down_all,
        attn_all,
        qkv,
        attended,
        middle,
        gains_all,
        ids_all,
    ) = front(
        layout,
        sizes,
        tokens[0],
        cotangent[0],
        ids_own,
        gains_own,
        w_query,
        w_key,
        w_value,
        w_out,
        w_gate,
        w_up,
        w_down,
    )
    mixed, grad_tokens, gain_sum, grad_gate, grad_up, grad_down, grad_attn, *_ = back(
        layout,
        sizes,
        tokens[0],
        cotangent[0],
        normed_one,
        normed_two,
        grad_all,
        in_all,
        down_all,
        attn_all,
        qkv,
        attended,
        middle,
        gains_all,
        ids_all,
    )
    parts = grad_attn.reshape(depth, layout.seq, sizes.attn_joined(layout))
    wide, narrow = layout.share * sizes.query, sizes.kv_columns(layout)

    def flat(columns):
        return columns.astype(jnp.float32).reshape(depth, -1)

    def heads(columns):
        columns = columns.astype(jnp.float32)
        if layout.seq * narrow > KVH * HD:
            columns = jnp.sum(columns.reshape(depth, KVH, -1, HD), axis=2)
        return columns.reshape(depth, -1)

    return (
        mixed[None],
        grad_tokens[None],
        gain_sum[0],
        flat(parts[:, :, :wide]),
        heads(parts[:, :, 2 * wide : 2 * wide + narrow]),
        heads(parts[:, :, 2 * wide + narrow :]),
        flat(parts[:, :, wide : 2 * wide]),
        gain_sum[1],
        flat(grad_gate),
        flat(grad_up),
        flat(grad_down),
    )


def solution(mesh):
    tokens, rows = P("fsdp", "seq", None), P("fsdp", None)
    return jax.shard_map(
        body,
        mesh=mesh,
        in_specs=(tokens, rows, P("fsdp"), rows, rows, rows, rows, P("fsdp"), rows, rows, rows, tokens),
        out_specs=(tokens, tokens, P("fsdp"), rows, rows, rows, rows, P("fsdp"), rows, rows, rows),
        check_vma=False,
    )
```

```python
import functools

import jax
import jax.numpy as jnp
from jax import lax
from jax.experimental import pallas as pl
from jax.experimental.pallas import tpu as pltpu
from jax.sharding import PartitionSpec as P

H = 32
KVH = 8
HD = 64
EPSILON = 1e-05
RESIDUAL = 0.22
MLP_GROUP = 16
ATTN_GROUP = 8
MESH = pl.DeviceIdType.MESH
EVEN = ((0, 64), (64, 64))
THIRDS = ((0, 48), (48, 48), (96, 32))


def plan_of(pieces, orders):
    return tuple((start, size, order) for (start, size), order in zip(pieces, orders))


MLP_GATHER = plan_of(THIRDS, ((3, 2, 1), (3, 1, 2), (3, 2, 1)))
MLP_SCATTER = plan_of(THIRDS, ((1, 2, 3), (2, 1, 3), (1, 2, 3)))


def attn_plan(group):
    if group.bits == 3:
        return plan_of(EVEN, ((1, 2), (2, 1)))
    return plan_of(THIRDS, ((1, 2, 3), (2, 3, 1), (3, 1, 2)))


PLAN_PIECES = 3


def dot(left, right):
    return jnp.dot(left, right, preferred_element_type=jnp.float32)


def dot_cols(left, right):
    return lax.dot_general(
        left, right, (((1,), (1,)), ((), ())), preferred_element_type=jnp.float32
    )


def dot_rows(left, right):
    return lax.dot_general(
        left, right, (((0,), (0,)), ((), ())), preferred_element_type=jnp.float32
    )


def rms_factor(values):
    return lax.rsqrt(jnp.mean(values * values, axis=1, keepdims=True) + EPSILON)


def norm_back(grad_normed, values, factor, gain):
    weighted = grad_normed * gain
    centre = jnp.mean(weighted * values, axis=1, keepdims=True)
    return factor * weighted - values * (factor * factor * factor) * centre


class Group:
    def __init__(self, seq, share):
        self.seq = seq
        self.share = share
        self.count = seq * share
        self.bits = self.count.bit_length() - 1

    def member(self):
        return lax.axis_index("seq") + self.seq * (lax.axis_index("fsdp") % self.share)

    def partner(self, bit):
        mask = 1 << bit
        return offset(mask % self.seq, mask // self.seq)


class Layout:
    def __init__(self, seq_count, fsdp_count):
        self.seq = seq_count
        self.fsdp = fsdp_count
        self.seq_bits = seq_count.bit_length() - 1
        self.mlp = Group(seq_count, max(1, MLP_GROUP // seq_count))
        self.attn = Group(seq_count, max(1, ATTN_GROUP // seq_count))


def offset(low, high):
    return {
        "seq": jnp.bitwise_xor(lax.axis_index("seq"), low),
        "fsdp": jnp.bitwise_xor(lax.axis_index("fsdp"), high),
    }


def place_of(order, index):
    return sum(1 << bit for position, bit in enumerate(order) if index >> position & 1)


def softmax(query, keys, query_ids, key_ids):
    scores = dot_cols(query, keys) * (1.0 / HD)
    scores = jnp.where(key_ids <= query_ids, scores, -1e30)
    shifted = jnp.exp(scores - jnp.max(scores, axis=1, keepdims=True))
    return shifted / jnp.sum(shifted, axis=1, keepdims=True)


def rows_at(start, size):
    return pl.ds(pl.multiple_of(start, 16), size)


def greet_all(layout):
    pairs = [(1 << bit, 0) for bit in range(layout.seq_bits)]
    pairs += [(0, mask) for mask in range(1, layout.fsdp)]
    barrier = pltpu.get_barrier_semaphore()
    for low, high in pairs:
        pl.semaphore_signal(
            barrier, inc=1, device_id=offset(low, high), device_id_type=MESH
        )
    pl.semaphore_wait(barrier, len(pairs))


def gather_steps(group, rows, plan, own_ref, dst_ref, sems):
    send, recv, relay_recv, own_sem = sems
    me = group.member()
    depth = group.bits - 1
    pushed, relayed = {}, []

    def place(mask, piece):
        start, size, _ = plan[piece]
        block = jnp.bitwise_xor(me, mask)
        return dst_ref.at[rows_at(block * rows + start, size)]

    def source(mask, piece):
        start, size, _ = plan[piece]
        return own_ref.at[pl.ds(start, size)] if mask == 0 else place(mask, piece)

    def copy_to(mask, piece, recv_sem, bit):
        copy = pltpu.make_async_remote_copy(
            src_ref=source(mask, piece),
            dst_ref=place(mask, piece),
            send_sem=send,
            recv_sem=recv_sem,
            device_id=group.partner(bit),
            device_id_type=MESH,
        )
        copy.start()
        return copy

    def forward(index, piece):
        order = plan[piece][2]
        mask = place_of(order, index)
        for position in range(index.bit_length(), depth):
            number = index | 1 << position
            pushed[piece, number] = copy_to(
                mask, piece, recv.at[piece, number], order[position]
            )
        relayed.append(copy_to(mask, piece, relay_recv.at[piece, index], 0))

    for piece in range(len(plan)):
        forward(0, piece)
    local = pltpu.make_async_copy(own_ref, dst_ref.at[rows_at(me * rows, rows)], own_sem)
    local.start()
    yield
    for index in range(1, 1 << depth):
        for piece in range(len(plan)):
            pushed[piece, index].wait_recv()
            forward(index, piece)
        if index < 4:
            yield
    yield
    for copy in relayed:
        copy.wait_recv()
    local.wait()
    whole = dst_ref.at[pl.ds(0, (group.count - 1) * rows)]
    pltpu.make_async_remote_copy(
        src_ref=whole,
        dst_ref=whole,
        send_sem=send,
        recv_sem=recv.at[0, 0],
        device_id=group.partner(0),
        device_id_type=MESH,
    ).wait_send()
    yield


def gather_sems():
    count = PLAN_PIECES
    return [
        pltpu.SemaphoreType.DMA,
        pltpu.SemaphoreType.DMA((count, 8)),
        pltpu.SemaphoreType.DMA((count, 8)),
        pltpu.SemaphoreType.DMA,
    ]


def finish(steps):
    for _ in steps:
        pass


def scatter_steps(group, rows, plan, produce, total, buffers, tail, sems):
    stage, core_in, arrive = buffers
    last_out, last_in = tail
    core_send, core_recv, send, recv, last_send, last_recv = sems
    me = group.member()
    core = me % 2
    own = pl.multiple_of(core * rows, 16)
    other = pl.multiple_of((1 - core) * rows, 16)
    depth = group.bits - 1
    top = 1 << depth
    copies, pushed = {}, {}

    def chunked(start, size, body):
        @pl.loop(0, size // 16)
        def _(i):
            body(pl.multiple_of(i * 16 + start, 16))

    def slot(position, index):
        return top - (top >> position) + (index >> position + 1)

    def push(piece, position, index):
        start, size, order = plan[piece]
        rest = index ^ 1 << position
        number = slot(position, rest)
        copy = pltpu.make_async_remote_copy(
            src_ref=stage.at[place_of(order, index) // 2, rows_at(own + start, size)],
            dst_ref=arrive.at[number, pl.ds(start, size)],
            send_sem=send.at[piece, number],
            recv_sem=recv.at[piece, number],
            device_id=group.partner(order[position]),
            device_id_type=MESH,
        )
        copy.start()
        pushed[piece, position, rest] = copy

    def summed(pair, r, slots):
        value = stage[pair, rows_at(own + r, 16)].astype(jnp.float32)
        for number in slots:
            value = value + arrive[number, rows_at(r, 16)].astype(jnp.float32)
        return value

    def settle(pair):
        copies[pair].wait_recv()

        def body(r):
            stage[pair, rows_at(own + r, 16)] = (
                stage[pair, rows_at(own + r, 16)].astype(jnp.float32)
                + core_in[pair, rows_at(r, 16)].astype(jnp.float32)
            ).astype(jnp.bfloat16)

        chunked(0, rows, body)
        for piece, (_, _, order) in enumerate(plan):
            for index in range(1, top, 2):
                if place_of(order, index) == 2 * pair:
                    push(piece, 0, index)

    before = None
    for pair in sorted(range(top), key=lambda pair: (-pair.bit_count(), -pair)):
        produce(jnp.bitwise_xor(me // 2, pair), stage.at[pair])
        copies[pair] = pltpu.make_async_remote_copy(
            src_ref=stage.at[pair, rows_at(other, rows)],
            dst_ref=core_in.at[pair],
            send_sem=core_send.at[pair],
            recv_sem=core_recv.at[pair],
            device_id=group.partner(0),
            device_id_type=MESH,
        )
        copies[pair].start()
        if before is not None:
            settle(before)
        before = pair
    settle(before)
    yield
    final = {}
    for position in range(1, depth):
        for index in reversed(range(1 << position, top, 2 << position)):
            for piece, (start, size, order) in enumerate(plan):
                pair = place_of(order, index) // 2
                slots = [slot(p, index) for p in range(position)]
                for p in range(position):
                    pushed[piece, p, index].wait_recv()
                if position < depth - 1:

                    def keep(r):
                        stage[pair, rows_at(own + r, 16)] = summed(pair, r, slots).astype(
                            jnp.bfloat16
                        )

                    chunked(start, size, keep)
                    push(piece, position, index)
                else:

                    def onward(r):
                        last_out[rows_at(r, 16)] = summed(pair, r, slots).astype(jnp.bfloat16)

                    chunked(start, size, onward)
                    final[piece] = pltpu.make_async_remote_copy(
                        src_ref=last_out.at[pl.ds(start, size)],
                        dst_ref=last_in.at[pl.ds(start, size)],
                        send_sem=last_send.at[piece],
                        recv_sem=last_recv.at[piece],
                        device_id=group.partner(order[position]),
                        device_id_type=MESH,
                    )
                    final[piece].start()
        if position < depth - 1:
            yield
    slots = [slot(p, 0) for p in range(depth - 1)]
    for piece, (start, size, _) in enumerate(plan):
        for p in range(depth - 1):
            pushed[piece, p, 0].wait_recv()

        def gathered(r):
            total[rows_at(r, 16)] = summed(0, r, slots)

        chunked(start, size, gathered)
    for some in (copies, pushed):
        for copy in some.values():
            copy.wait_send()
    yield
    for piece, (start, size, _) in enumerate(plan):
        final[piece].wait_recv()

        def finished(r):
            total[rows_at(r, 16)] += last_in[rows_at(r, 16)].astype(jnp.float32)

        chunked(start, size, finished)
    for copy in final.values():
        copy.wait_send()
    yield


def scatter_scratch(rows, width):
    return [
        pltpu.VMEM((8, 2 * rows, width), jnp.bfloat16),
        pltpu.VMEM((8, rows, width), jnp.bfloat16),
        pltpu.VMEM((6, rows, width), jnp.bfloat16),
        pltpu.VMEM((rows, width), jnp.bfloat16),
        pltpu.VMEM((rows, width), jnp.bfloat16),
    ]


def scatter_sems():
    count = PLAN_PIECES
    return [
        pltpu.SemaphoreType.DMA((8,)),
        pltpu.SemaphoreType.DMA((8,)),
        pltpu.SemaphoreType.DMA((count, 6)),
        pltpu.SemaphoreType.DMA((count, 6)),
        pltpu.SemaphoreType.DMA((count,)),
        pltpu.SemaphoreType.DMA((count,)),
    ]


def loop_rows(count, size, body):
    @pl.loop(0, count // size)
    def _(i):
        body(pl.ds(pl.multiple_of(i * size, size), size))


class Sizes:
    def __init__(self, layout, tokens, block_ids, w_query, w_gate):
        self.rows, self.width = tokens.shape[1], tokens.shape[2]
        self.length = block_ids.shape[1]
        self.depth = w_query.shape[0]
        self.hidden = w_gate.shape[1] // layout.mlp.count
        self.heads = H // layout.attn.count
        self.query = self.heads * HD
        self.attn = 2 * self.query + 2 * HD
        self.mlp_rows = layout.mlp.count * self.rows
        self.attn_rows = layout.attn.count * self.rows
        self.span = max(128, min(self.length, 256 * 512 // self.length))
        self.kv_share = max(1, layout.attn.count // KVH)
        self.kv_columns = max(1, layout.attn.share // self.kv_share) * HD
        self.attn_joined = 2 * layout.attn.share * self.query + 2 * self.kv_columns


def kv_half(sizes, target, chunk):
    second = (target // sizes.kv_share) % 2 == 1
    return jnp.where(second, chunk[:, HD:], chunk[:, :HD])


def attention_scores(sizes, qkv, ids, seq, start, head):
    base = sizes.query
    keys_rows = rows_at(seq * sizes.length, sizes.length)
    query_rows = rows_at(seq * sizes.length + start, sizes.span)
    query = qkv[query_rows, head * HD : (head + 1) * HD]
    keys = qkv[keys_rows, base : base + HD]
    values = qkv[keys_rows, base + HD : base + 2 * HD]
    key_ids = ids[seq, 0:1, :]
    query_ids = jnp.transpose(ids[seq, :, pl.ds(start, sizes.span)])[:, :1]
    return query, keys, values, softmax(query, keys, query_ids, key_ids)


def front_kernel(
    layout,
    sizes,
    tok_ref,
    cot_ref,
    ids_ref,
    gains_ref,
    wq_ref,
    wk_ref,
    wv_ref,
    wo_ref,
    wg_ref,
    wu_ref,
    wd_ref,
    h1_out,
    h2_out,
    g_out,
    in_out,
    down_out,
    wa,
    qkv,
    attended,
    middle,
    gains,
    ids,
    x_all,
    tok,
    h2,
    wq,
    wk,
    wv,
    wo,
    pack,
    stage,
    core_in,
    arrive,
    last_out,
    last_in,
    x_send,
    x_recv,
    x_relay,
    x_own,
    h_send,
    h_recv,
    h_relay,
    h_own,
    g_send,
    g_recv,
    g_relay,
    g_own,
    core_send,
    core_recv,
    s_send,
    s_recv,
    last_send,
    last_recv,
    attn_send,
    attn_recv,
    gain_send,
    gain_recv,
    id_send,
    id_recv,
    mlp_send,
    mlp_recv,
    load_sem,
):
    share, fsdp, depth = layout.attn.share, layout.fsdp, sizes.depth
    mlp_share = layout.mlp.share
    seq_me, fsdp_me = lax.axis_index("seq"), lax.axis_index("fsdp")
    query = sizes.query
    rows, hidden = sizes.rows, sizes.hidden

    loads = []

    def load(src, dst):
        copy = pltpu.make_async_copy(src, dst, load_sem.at[len(loads)])
        copy.start()
        loads.append(copy)
        return copy

    def columns(ref, start, size):
        return ref.at[:, pl.ds(pl.multiple_of(start, 128), size)]

    load(tok_ref, tok)
    own_rows = pl.ds(pl.multiple_of(fsdp_me * depth, 128), depth)
    load(gains_ref, gains.at[:, own_rows])
    load(columns(wq_ref, seq_me * share * query, share * query), wq)
    load(columns(wo_ref, seq_me * share * query, share * query), wo)
    chunk = seq_me * share // (2 * sizes.kv_share) * 128
    load(columns(wk_ref, chunk, 128), wk)
    load(columns(wv_ref, chunk, 128), wv)
    load(ids_ref, ids.at[fsdp_me % share])
    greet_all(layout)
    small = []
    for mask in range(1, fsdp):
        copy = pltpu.make_async_remote_copy(
            src_ref=gains_ref,
            dst_ref=gains.at[:, own_rows],
            send_sem=gain_send.at[mask],
            recv_sem=gain_recv.at[mask],
            device_id=offset(0, mask),
            device_id_type=MESH,
        )
        copy.start()
        small.append(copy)
    for copy in loads:
        copy.wait()
    for j in range(share):
        target = seq_me * share + j
        pack[j] = jnp.concatenate(
            [
                wq[:, j * query : (j + 1) * query],
                kv_half(sizes, target, wk[...]),
                kv_half(sizes, target, wv[...]),
                wo[:, j * query : (j + 1) * query],
            ],
            axis=1,
        )
    attn = []
    for mask in reversed(range(1, fsdp)):
        copy = pltpu.make_async_remote_copy(
            src_ref=pack.at[jnp.bitwise_xor(fsdp_me, mask) % share],
            dst_ref=wa.at[own_rows],
            send_sem=attn_send.at[mask],
            recv_sem=attn_recv.at[mask],
            device_id=offset(0, mask),
            device_id_type=MESH,
        )
        copy.start()
        attn.append(copy)
    wa[own_rows] = pack[fsdp_me % share]
    for copy in small:
        copy.wait()
    gain_one = gains[0:1].astype(jnp.float32)

    def norm(r):
        values = tok[r].astype(jnp.float32)
        h2[r] = (values * rms_factor(values) * gain_one).astype(jnp.bfloat16)

    loop_rows(rows, 32, norm)
    x_steps = gather_steps(layout.attn, rows, attn_plan(layout.attn), h2, x_all, (x_send, x_recv, x_relay, x_own))
    next(x_steps)
    id_copies = []
    for mask in range(1, share):
        copy = pltpu.make_async_remote_copy(
            src_ref=ids_ref,
            dst_ref=ids.at[fsdp_me % share],
            send_sem=id_send.at[mask],
            recv_sem=id_recv.at[mask],
            device_id=offset(0, mask),
            device_id_type=MESH,
        )
        copy.start()
        id_copies.append(copy)
    g_steps = gather_steps(
        layout.mlp, rows, MLP_GATHER, cot_ref, g_out, (g_send, g_recv, g_relay, g_own)
    )
    next(g_steps)
    next(x_steps)

    mlp = []

    def send_mlp(ref, out, place, index):
        def at(j):
            return columns(ref, (seq_me * mlp_share + j) * hidden, hidden)

        home = out.at[own_rows, pl.ds(place, hidden)]
        for mask in reversed(range(1, fsdp)):
            copy = pltpu.make_async_remote_copy(
                src_ref=at(jnp.bitwise_xor(fsdp_me, mask) % mlp_share),
                dst_ref=home,
                send_sem=mlp_send.at[index, mask],
                recv_sem=mlp_recv.at[index, mask],
                device_id=offset(0, mask),
                device_id_type=MESH,
            )
            copy.start()
            mlp.append(copy)
        copy = pltpu.make_async_copy(at(fsdp_me % mlp_share), home, load_sem.at[1 + index])
        copy.start()
        mlp.append(copy)

    send_mlp(wg_ref, in_out, 0, 0)
    send_mlp(wu_ref, in_out, hidden, 1)
    finish(x_steps)
    h1_copy = pltpu.make_async_copy(x_all, h1_out, load_sem.at[0])
    h1_copy.start()
    next(g_steps)
    for copy in attn:
        copy.wait()

    def project(r):
        qkv[r] = dot(x_all[r], wa[:, : query + 2 * HD]).astype(jnp.bfloat16)

    loop_rows(sizes.attn_rows, 256, project)
    next(g_steps)
    for copy in id_copies:
        copy.wait()

    blocks = sizes.length // sizes.span

    @pl.loop(0, share * blocks)
    def _(i):
        seq = i // blocks
        start = pl.multiple_of((i % blocks) * sizes.span, sizes.span)
        outs = []
        for head in range(sizes.heads):
            _, _, values, probs = attention_scores(sizes, qkv, ids, seq, start, head)
            outs.append(dot(probs.astype(jnp.bfloat16), values))
        attended[rows_at(seq * sizes.length + start, sizes.span)] = jnp.concatenate(
            outs, axis=1
        ).astype(jnp.bfloat16)

    def out_rows(pair, ref):
        block = attended[rows_at(pair * 2 * rows, 2 * rows)]

        @pl.loop(0, sizes.width // 512)
        def _(i):
            piece = pl.ds(pl.multiple_of(i * 512, 512), 512)
            ref[:, piece] = dot_cols(block, wa[piece, query + 2 * HD :]).astype(jnp.bfloat16)

    next(g_steps)
    next(g_steps)
    steps = scatter_steps(
        layout.attn, rows, attn_plan(layout.attn), out_rows, middle, (stage, core_in, arrive),
        (last_out, last_in), (core_send, core_recv, s_send, s_recv, last_send, last_recv),
    )
    next(steps)
    next(g_steps)
    finish(steps)
    gain_two = gains[8:9].astype(jnp.float32)

    def second(r):
        values = tok[r].astype(jnp.float32) + RESIDUAL * middle[r]
        middle[r] = values
        h2[r] = (values * rms_factor(values) * gain_two).astype(jnp.bfloat16)

    loop_rows(rows, 32, second)
    h_steps = gather_steps(
        layout.mlp, rows, MLP_GATHER, h2, h2_out, (h_send, h_recv, h_relay, h_own)
    )
    next(h_steps)
    next(h_steps)
    send_mlp(wd_ref, down_out, 0, 2)
    finish(g_steps)
    finish(h_steps)
    for copy in mlp:
        copy.wait()
    h1_copy.wait()


def front(layout, sizes, *args):
    width, count, few = sizes.width, sizes.mlp_rows, sizes.attn_rows
    hbm, vmem = pl.BlockSpec(memory_space=pl.ANY), pl.BlockSpec(memory_space=pltpu.VMEM)
    share, depth, fsdp = layout.attn.share, sizes.depth, layout.fsdp
    bf16 = jnp.bfloat16
    shapes = [
        ((few, width), bf16, hbm),
        ((count, width), bf16, hbm),
        ((count, width), bf16, hbm),
        ((width, 2 * sizes.hidden), bf16, hbm),
        ((width, sizes.hidden), bf16, hbm),
        ((width, sizes.attn), bf16, vmem),
        ((few, sizes.query + 2 * HD), bf16, vmem),
        ((few, sizes.query), bf16, vmem),
        ((sizes.rows, width), jnp.float32, vmem),
        ((16, width), bf16, vmem),
        ((share, 8, sizes.length), jnp.int32, vmem),
    ]
    dma = pltpu.SemaphoreType.DMA
    return pl.pallas_call(
        functools.partial(front_kernel, layout, sizes),
        out_shape=[jax.ShapeDtypeStruct(shape, dtype) for shape, dtype, _ in shapes],
        in_specs=[hbm] * len(args),
        out_specs=[spec for _, _, spec in shapes],
        scratch_shapes=[
            pltpu.VMEM((few, width), bf16),
            pltpu.VMEM((sizes.rows, width), bf16),
            pltpu.VMEM((sizes.rows, width), bf16),
            pltpu.VMEM((depth, share * sizes.query), bf16),
            pltpu.VMEM((depth, 128), bf16),
            pltpu.VMEM((depth, 128), bf16),
            pltpu.VMEM((depth, share * sizes.query), bf16),
            pltpu.VMEM((share, depth, sizes.attn), bf16),
        ]
        + scatter_scratch(sizes.rows, width)
        + gather_sems() * 3
        + scatter_sems()
        + [dma((fsdp,)), dma((fsdp,)), dma((fsdp,)), dma((fsdp,))]
        + [dma((share,)), dma((share,)), dma((3, fsdp)), dma((3, fsdp)), dma((8,))],
        compiler_params=pltpu.CompilerParams(
            collective_id=3, has_side_effects=True, vmem_limit_bytes=56 * 1024 * 1024
        ),
        name="front",
    )(*args)


def seq_gather(layout, out_ref, width, sems):
    send, recv = sems
    me = lax.axis_index("seq")
    bits = [1 << bit for bit in reversed(range(layout.seq_bits))]

    def block(mask):
        start = jnp.bitwise_xor(me, mask) * width
        return out_ref.at[:, pl.ds(pl.multiple_of(start, 128), width)]

    copies = {}

    def push(mask, bit):
        copy = pltpu.make_async_remote_copy(
            src_ref=block(mask),
            dst_ref=block(mask),
            send_sem=send.at[mask ^ bit],
            recv_sem=recv.at[mask ^ bit],
            device_id=offset(bit, 0),
            device_id_type=MESH,
        )
        copy.start()
        copies[mask ^ bit] = copy

    for bit in bits:
        push(0, bit)
    yield
    held = [0]
    for bit in bits:
        for mask in held[1:]:
            push(mask, bit)
        new = [mask ^ bit for mask in held]
        if bit != bits[-1]:
            for mask in new:
                copies[mask].wait_recv()
        held = held + new
    yield
    for mask in held[len(held) // 2 :]:
        copies[mask].wait_recv()
    for copy in copies.values():
        copy.wait_send()
    yield


def back_kernel(
    layout,
    sizes,
    tok_ref,
    cot_ref,
    h1_ref,
    h2_ref,
    g_ref,
    in_ref,
    down_ref,
    wa_ref,
    qkv_ref,
    att_ref,
    mid_ref,
    gains_ref,
    ids_ref,
    mixed,
    grad_tok,
    gain_sum,
    gate_out,
    up_out,
    down_out,
    attn_out,
    gate_recv,
    up_recv,
    down_recv,
    attn_recv,
    g_all,
    h_all,
    w_in,
    w_down,
    wa,
    qkv,
    attended,
    hid,
    grad_in,
    middle,
    total,
    grad_mid,
    tok,
    down_stage,
    gains,
    ids,
    grad_kv,
    terms,
    gain_in,
    gain_seq,
    own_sum,
    stage,
    core_in,
    arrive,
    last_out,
    last_in,
    down_total,
    down_last_out,
    down_last_in,
    a_send,
    a_recv,
    a_relay,
    a_own,
    core_send,
    core_recv,
    s_send,
    s_recv,
    last_send,
    last_recv,
    down_last_send,
    down_last_recv,
    credit,
    grad_send,
    grad_recv,
    join_send,
    join_recv,
    own_sem,
    gain_send,
    gain_recv,
    gs_send,
    gs_recv,
    load_sem,
    pick_sem,
):
    fsdp, depth = layout.fsdp, sizes.depth
    seq_me, fsdp_me = lax.axis_index("seq"), lax.axis_index("fsdp")
    query, hidden, rows = sizes.query, sizes.hidden, sizes.rows
    base = query + 2 * HD
    count, few = sizes.mlp_rows, sizes.attn_rows
    near = pl.ds(0, few)
    spare = few < count

    def piece_at(ref, mask):
        column = pl.ds(mask // 4 * sizes.attn, sizes.attn)
        return ref.at[pl.ds(mask % 4 * depth, depth), column]

    def staged(mask):
        if spare:
            return piece_at(h_all.at[pl.ds(few, few)], mask)
        return w_down.at[block(mask), pl.ds(0, sizes.attn)]

    if spare:
        own_sum = g_all.at[pl.ds(few, depth)]
    scatter = (stage, core_in, arrive)
    sems = (core_send, core_recv, s_send, s_recv)
    scatter_sem = sems + (last_send, last_recv)

    loads = {}
    for name, src, dst in (
        ("in", in_ref, w_in),
        ("h", h2_ref, h_all),
        ("g", g_ref, g_all),
        ("down", down_ref, w_down),
        ("mid", mid_ref, middle),
        ("tok", tok_ref, tok),
        ("cot", cot_ref, down_last_out),
        ("gains", gains_ref, gains),
        ("wa", wa_ref, wa),
        ("qkv", qkv_ref, qkv),
        ("att", att_ref, attended),
        ("ids", ids_ref, ids),
    ):
        loads[name] = pltpu.make_async_copy(src, dst, load_sem.at[len(loads)])
        loads[name].start()
    greet_all(layout)
    for name in ("in", "h", "g", "down"):
        loads[name].wait()

    def hidden_rows(r):
        h = h_all[r]
        gate = dot(h, w_in[:, :hidden])
        upward = dot(h, w_in[:, hidden:])
        grad = (RESIDUAL * g_all[r].astype(jnp.float32)).astype(jnp.bfloat16)
        g_all[r] = grad
        grad_hidden = dot(grad, w_down[...])
        sigma = jax.nn.sigmoid(gate)
        hid[r] = (gate * sigma * upward).astype(jnp.bfloat16)
        grad_in[r, hidden:] = (grad_hidden * gate * sigma).astype(jnp.bfloat16)
        grad_in[r, :hidden] = (
            grad_hidden * upward * sigma * (1.0 + gate * (1.0 - sigma))
        ).astype(jnp.bfloat16)

    loop_rows(count, 256, hidden_rows)

    sends = []
    far = list(reversed(range(1, fsdp))) + [0]

    def owner_columns(mask):
        start = jnp.bitwise_xor(fsdp_me, mask) * depth
        return pl.ds(pl.multiple_of(start, 128), depth)

    def send_grad(mask, src, dst, index):
        if mask == 0:
            return
        copy = pltpu.make_async_remote_copy(
            src_ref=src,
            dst_ref=dst.at[mask],
            send_sem=grad_send.at[index, mask],
            recv_sem=grad_recv.at[index, mask],
            device_id=offset(0, mask),
            device_id_type=MESH,
        )
        copy.start()
        sends.append((index, mask, copy))

    def block(mask):
        return pl.ds(mask * depth, depth)

    def grad_down(mask):
        down_stage[block(mask)] = dot_rows(g_all[:, owner_columns(mask)], hid[...]).astype(
            jnp.bfloat16
        )
        send_grad(mask, down_stage.at[block(mask)], down_recv, 0)

    for mask in far:
        grad_down(mask)

    def hidden_back(pair, ref):
        left = grad_in[rows_at(pair * 2 * rows, 2 * rows)]

        @pl.loop(0, sizes.width // 512)
        def _(i):
            piece = pl.ds(pl.multiple_of(i * 512, 512), 512)
            ref[:, piece] = dot_cols(left, w_in[piece]).astype(jnp.bfloat16)

    steps = scatter_steps(layout.mlp, rows, MLP_SCATTER, hidden_back, total, scatter, (last_out, last_in), scatter_sem)
    next(steps)

    def grad_up(mask):
        w_in[block(mask)] = dot_rows(h_all[:, owner_columns(mask)], grad_in[...]).astype(
            jnp.bfloat16
        )

    for turn in range(3):
        for mask in far[turn * 3 : turn * 3 + 3]:
            grad_up(mask)
        next(steps)
    finish(steps)
    h1_copy = pltpu.make_async_copy(h1_ref, h_all.at[near], load_sem.at[len(loads)])
    h1_copy.start()
    for name in ("mid", "tok", "cot", "gains", "wa", "qkv", "att", "ids"):
        loads[name].wait()
    gain_one = gains[0:1].astype(jnp.float32)
    gain_two = gains[8:9].astype(jnp.float32)
    terms[...] = jnp.zeros_like(terms)

    def norm_two(r):
        values, normed = middle[r], total[r]
        factor = rms_factor(values)
        terms[1:2] += jnp.sum(normed * values * factor, axis=0, keepdims=True)
        grad = down_last_out[r].astype(jnp.float32) + norm_back(normed, values, factor, gain_two)
        grad_mid[r] = grad
        last_out[r] = (RESIDUAL * grad).astype(jnp.bfloat16)

    loop_rows(rows, 32, norm_two)
    a_steps = gather_steps(
        layout.attn, rows, attn_plan(layout.attn), last_out, g_all.at[near], (a_send, a_recv, a_relay, a_own)
    )
    next(a_steps)
    next(a_steps)
    for mask in far:
        send_grad(mask, w_in.at[block(mask), pl.ds(0, hidden)], gate_recv, 1)
    for mask in far:
        send_grad(mask, w_in.at[block(mask), pl.ds(hidden, hidden)], up_recv, 2)
    finish(a_steps)

    def down_rows(pair, ref):
        left = hid[rows_at(pair * 2 * rows, 2 * rows)]

        @pl.loop(0, sizes.width // 512)
        def _(i):
            piece = pl.ds(pl.multiple_of(i * 512, 512), 512)
            ref[:, piece] = dot_cols(left, w_down[piece]).astype(jnp.bfloat16)

    steps_low = scatter_steps(
        layout.mlp, rows, MLP_SCATTER, down_rows, down_total, scatter, (down_last_out, down_last_in),
        sems + (down_last_send, down_last_recv),
    )
    next(steps_low)


    def collect(index, share, src, width, own_piece, landing, combine, out, out_width):
        picks = []
        for number, mask, copy in sends:
            if number == index:
                copy.wait_recv()
                pick = pltpu.make_async_copy(
                    src.at[mask], landing(mask), pick_sem.at[index, mask]
                )
                pick.start()
                picks.append(pick)
        yield
        for pick in picks:
            pick.wait()

        def terms_of(low, start, size):
            cols = pl.ds(start, size)
            value = own_piece[:, cols] if low == 0 else landing(low)[:, cols]
            value = value.astype(jnp.float32)
            for mask in range(low + share, fsdp, share):
                value = value + landing(mask)[:, cols].astype(jnp.float32)
            return value

        combine(terms_of, share, width)
        home = pl.multiple_of(seq_me * out_width, 128)
        local = pltpu.make_async_copy(
            own_sum.at[:, pl.ds(0, out_width)], out.at[:, pl.ds(home, out_width)], own_sem.at[index]
        )
        local.start()
        local.wait()
        yield from seq_gather(layout, out, out_width, (join_send.at[index], join_recv.at[index]))

    def place_columns(terms_of, share, width):
        mine = fsdp_me % share
        for low in range(share):
            start = pl.multiple_of(jnp.bitwise_xor(mine, low) * width, 128)
            own_sum[:, pl.ds(start, width)] = terms_of(low, 0, width).astype(jnp.bfloat16)

    def place_attn(terms_of, share, width):
        mine = fsdp_me % share
        for low in range(share):
            for source, target in ((0, 0), (base, share * query)):
                start = pl.multiple_of(target + jnp.bitwise_xor(mine, low) * query, 128)
                own_sum[:, pl.ds(start, query)] = terms_of(low, source, query).astype(
                    jnp.bfloat16
                )
        both = sizes.kv_columns
        at = 2 * share * query
        for source in (query, query + HD):
            heads = []
            for first in range(0, share, sizes.kv_share):
                value = terms_of(first, source, HD)
                for low in range(first + 1, min(share, first + sizes.kv_share)):
                    value = value + terms_of(low, source, HD)
                heads.append(value)
            value = heads[0]
            if len(heads) == 2:
                upper = mine // sizes.kv_share == 1
                value = jnp.concatenate(
                    [jnp.where(upper, heads[1], heads[0]), jnp.where(upper, heads[0], heads[1])],
                    axis=1,
                )
            own_sum[:, at : at + both] = value.astype(jnp.bfloat16)
            at += both

    mlp_share, attn_share = layout.mlp.share, layout.attn.share
    joined = mlp_share * hidden
    steps_down = collect(
        0, mlp_share, down_recv, hidden, down_stage.at[block(0)], lambda mask: hid.at[block(mask)], place_columns, down_out, joined
    )
    next(steps_down)

    blocks = sizes.length // sizes.span

    def attend_back_block(i):
        seq = i // blocks
        part = i % blocks
        start = pl.multiple_of(part * sizes.span, sizes.span)
        here = rows_at(seq * sizes.length + start, sizes.span)
        grad_out = dot(g_all[here], wa[:, base:]).astype(jnp.bfloat16)
        grads, grad_keys, grad_values = [], 0.0, 0.0
        for head in range(sizes.heads):
            left, keys, values, probs = attention_scores(sizes, qkv, ids, seq, start, head)
            grad = grad_out[:, head * HD : (head + 1) * HD]
            grad_probs = dot_cols(grad, values)
            centre = jnp.sum(probs * grad_probs, axis=1, keepdims=True)
            grad_scores = (probs * (grad_probs - centre)).astype(jnp.bfloat16)
            grads.append(dot(grad_scores, keys) * (1.0 / HD))
            grad_keys = grad_keys + dot_rows(grad_scores, left) * (1.0 / HD)
            grad_values = grad_values + dot_rows(probs.astype(jnp.bfloat16), grad)
        both = jnp.concatenate([grad_keys, grad_values], axis=1)

        @pl.when(part == 0)
        def _():
            grad_kv[...] = both

        @pl.when(part > 0)
        def _():
            grad_kv[...] += both

        qkv[here, :query] = jnp.concatenate(grads, axis=1).astype(jnp.bfloat16)

        @pl.when(part == blocks - 1)
        def _():
            qkv[rows_at(seq * sizes.length, sizes.length), query:] = grad_kv[...].astype(
                jnp.bfloat16
            )

    turns = layout.attn.share * blocks

    @pl.loop(0, turns // 2)
    def _(i):
        attend_back_block(i)

    next(steps_down)
    next(steps_low)

    @pl.loop(turns // 2, turns)
    def _(i):
        attend_back_block(i)

    next(steps_low)
    for bit in range(layout.mlp.bits):
        pl.semaphore_signal(
            credit, inc=1, device_id=layout.mlp.partner(bit), device_id_type=MESH
        )

    next(steps_down)
    pl.semaphore_wait(credit, layout.mlp.bits)

    def qkv_back(pair, ref):
        left = qkv[rows_at(pair * 2 * rows, 2 * rows)]

        @pl.loop(0, sizes.width // 512)
        def _(i):
            piece = pl.ds(pl.multiple_of(i * 512, 512), 512)
            ref[:, piece] = dot_cols(left, wa[piece, :base]).astype(jnp.bfloat16)

    h1_copy.wait()

    def grad_attn(mask):
        cols = owner_columns(mask)
        staged(mask)[:, :base] = dot_rows(h_all[near, cols], qkv[...]).astype(jnp.bfloat16)
        staged(mask)[:, base:] = dot_rows(g_all[near, cols], attended[...]).astype(
            jnp.bfloat16
        )
        send_grad(mask, staged(mask), attn_recv, 3)

    for mask in far[: fsdp // 2]:
        grad_attn(mask)
    steps = scatter_steps(layout.attn, rows, attn_plan(layout.attn), qkv_back, total, scatter, (last_out, last_in), scatter_sem)
    next(steps)
    for mask in far[fsdp // 2 :]:
        grad_attn(mask)
    steps_gate = collect(
        1, mlp_share, gate_recv, hidden, w_in.at[block(0), pl.ds(0, hidden)], lambda mask: grad_in.at[block(mask), pl.ds(0, hidden)],
        place_columns, gate_out, joined,
    )
    next(steps_gate)
    next(steps)
    next(steps_gate)
    next(steps)
    finish(steps)

    def norm_one(r):
        values, normed = tok[r].astype(jnp.float32), total[r]
        factor = rms_factor(values)
        terms[0:1] += jnp.sum(normed * values * factor, axis=0, keepdims=True)
        grad = grad_mid[r] + norm_back(normed, values, factor, gain_one)
        grad_tok[r] = grad.astype(jnp.bfloat16)

    loop_rows(rows, 32, norm_one)
    finish(steps_low)

    def mix(r):
        mixed[r] = (middle[r] + RESIDUAL * down_total[r]).astype(jnp.bfloat16)

    loop_rows(rows, 32, mix)
    gain_copies = []
    for mask in range(1, fsdp):
        copy = pltpu.make_async_remote_copy(
            src_ref=terms.at[:, owner_columns(mask)],
            dst_ref=gain_in.at[mask],
            send_sem=gain_send.at[mask],
            recv_sem=gain_recv.at[mask],
            device_id=offset(0, mask),
            device_id_type=MESH,
        )
        copy.start()
        gain_copies.append(copy)

    steps_up = collect(
        2, mlp_share, up_recv, hidden, w_in.at[block(0), pl.ds(hidden, hidden)], lambda mask: grad_in.at[block(mask), pl.ds(hidden, hidden)],
        place_columns, up_out, joined,
    )
    next(steps_up)
    next(steps_up)
    next(steps_gate)
    steps_attn = collect(
        3, attn_share, attn_recv, sizes.attn, staged(0), functools.partial(piece_at, g_all),
        place_attn, attn_out, sizes.attn_joined,
    )
    next(steps_attn)
    next(steps_attn)
    next(steps_up)

    value = terms[:, owner_columns(0)]
    for copy in gain_copies:
        copy.wait()
    for mask in range(1, fsdp):
        value = value + gain_in[mask]
    for bit in range(layout.seq_bits):
        gain_seq[2 * bit] = value
        copy = pltpu.make_async_remote_copy(
            src_ref=gain_seq.at[2 * bit],
            dst_ref=gain_seq.at[2 * bit + 1],
            send_sem=gs_send.at[bit],
            recv_sem=gs_recv.at[bit],
            device_id=offset(1 << bit, 0),
            device_id_type=MESH,
        )
        copy.start()
        copy.wait()
        value = value + gain_seq[2 * bit + 1]
    gain_sum[...] = value
    for steps in (steps_attn, steps_down, steps_gate, steps_up):
        finish(steps)
    for _, _, copy in sends:
        copy.wait_send()


def back(layout, sizes, *args):
    width, count, few = sizes.width, sizes.mlp_rows, sizes.attn_rows
    hbm, vmem = pl.BlockSpec(memory_space=pl.ANY), pl.BlockSpec(memory_space=pltpu.VMEM)
    share, depth, fsdp = layout.attn.share, sizes.depth, layout.fsdp
    joined = layout.mlp.share * sizes.hidden
    rows, hidden, base = sizes.rows, sizes.hidden, sizes.query + 2 * HD
    bf16, f32 = jnp.bfloat16, jnp.float32
    shapes = [
        ((rows, width), bf16, vmem),
        ((rows, width), bf16, vmem),
        ((8, depth), f32, vmem),
        ((depth, layout.seq * joined), bf16, hbm),
        ((depth, layout.seq * joined), bf16, hbm),
        ((depth, layout.seq * joined), bf16, hbm),
        ((depth, layout.seq * sizes.attn_joined), bf16, hbm),
        ((fsdp, depth, hidden), bf16, hbm),
        ((fsdp, depth, hidden), bf16, hbm),
        ((fsdp, depth, hidden), bf16, hbm),
        ((fsdp, depth, sizes.attn), bf16, hbm),
    ]
    dma = pltpu.SemaphoreType.DMA
    seq = layout.seq
    return pl.pallas_call(
        functools.partial(back_kernel, layout, sizes),
        out_shape=[jax.ShapeDtypeStruct(shape, dtype) for shape, dtype, _ in shapes],
        in_specs=[hbm] * len(args),
        out_specs=[spec for _, _, spec in shapes],
        scratch_shapes=[
            pltpu.VMEM((count, width), bf16),
            pltpu.VMEM((count, width), bf16),
            pltpu.VMEM((width, 2 * hidden), bf16),
            pltpu.VMEM((width, hidden), bf16),
            pltpu.VMEM((width, sizes.attn), bf16),
            pltpu.VMEM((few, base), bf16),
            pltpu.VMEM((few, sizes.query), bf16),
            pltpu.VMEM((count, hidden), bf16),
            pltpu.VMEM((count, 2 * hidden), bf16),
            pltpu.VMEM((rows, width), f32),
            pltpu.VMEM((rows, width), f32),
            pltpu.VMEM((rows, width), f32),
            pltpu.VMEM((rows, width), bf16),
            pltpu.VMEM((width, hidden), bf16),
            pltpu.VMEM((16, width), bf16),
            pltpu.VMEM((share, 8, sizes.length), jnp.int32),
            pltpu.VMEM((sizes.length, 2 * HD), f32),
            pltpu.VMEM((8, width), f32),
            pltpu.VMEM((fsdp, 8, depth), f32),
            pltpu.VMEM((2 * layout.seq_bits, 8, depth), f32),
            pltpu.VMEM((depth, max(joined, sizes.attn_joined) if few == count else 128), bf16),
        ]
        + scatter_scratch(rows, width)
        + [
            pltpu.VMEM((rows, width), f32),
            pltpu.VMEM((rows, width), bf16),
            pltpu.VMEM((rows, width), bf16),
        ]
        + gather_sems()
        + scatter_sems()
        + [dma((PLAN_PIECES,)), dma((PLAN_PIECES,))]
        + [pltpu.SemaphoreType.REGULAR]
        + [dma((4, fsdp)), dma((4, fsdp)), dma((4, seq)), dma((4, seq)), dma((4,))]
        + [dma((fsdp,)), dma((fsdp,)), dma((layout.seq_bits,)), dma((layout.seq_bits,))]
        + [dma((16,)), dma((4, fsdp))],
        compiler_params=pltpu.CompilerParams(
            collective_id=4, has_side_effects=True, vmem_limit_bytes=62 * 1024 * 1024
        ),
        name="back",
    )(*args)


def body(
    tokens,
    block_ids,
    gain_attn,
    w_query,
    w_key,
    w_value,
    w_out,
    gain_mlp,
    w_gate,
    w_up,
    w_down,
    cotangent,
):
    layout = Layout(lax.axis_size("seq"), lax.axis_size("fsdp"))
    depth = w_gate.shape[0]
    sizes = Sizes(layout, tokens, block_ids, w_query, w_gate)
    gains_own = jnp.concatenate(
        [jnp.broadcast_to(gain[None], (8, depth)) for gain in (gain_attn, gain_mlp)], axis=0
    )
    ids_own = jnp.broadcast_to(block_ids, (8, block_ids.shape[1]))
    (
        normed_one,
        normed_two,
        grad_all,
        in_all,
        down_all,
        attn_all,
        qkv,
        attended,
        middle,
        gains_all,
        ids_all,
    ) = front(
        layout,
        sizes,
        tokens[0],
        cotangent[0],
        ids_own,
        gains_own,
        w_query,
        w_key,
        w_value,
        w_out,
        w_gate,
        w_up,
        w_down,
    )
    mixed, grad_tokens, gain_sum, grad_gate, grad_up, grad_down, grad_attn, *_ = back(
        layout,
        sizes,
        tokens[0],
        cotangent[0],
        normed_one,
        normed_two,
        grad_all,
        in_all,
        down_all,
        attn_all,
        qkv,
        attended,
        middle,
        gains_all,
        ids_all,
    )
    parts = grad_attn.reshape(depth, layout.seq, sizes.attn_joined)
    wide, narrow = layout.attn.share * sizes.query, sizes.kv_columns

    def flat(columns):
        return columns.astype(jnp.float32).reshape(depth, -1)

    def heads(columns):
        columns = columns.astype(jnp.float32)
        if layout.seq * narrow > KVH * HD:
            columns = jnp.sum(columns.reshape(depth, KVH, -1, HD), axis=2)
        return columns.reshape(depth, -1)

    return (
        mixed[None],
        grad_tokens[None],
        gain_sum[0],
        flat(parts[:, :, :wide]),
        heads(parts[:, :, 2 * wide : 2 * wide + narrow]),
        heads(parts[:, :, 2 * wide + narrow :]),
        flat(parts[:, :, wide : 2 * wide]),
        gain_sum[1],
        flat(grad_gate),
        flat(grad_up),
        flat(grad_down),
    )


def solution(mesh):
    tokens, rows = P("fsdp", "seq", None), P("fsdp", None)
    return jax.shard_map(
        body,
        mesh=mesh,
        in_specs=(tokens, rows, P("fsdp"), rows, rows, rows, rows, P("fsdp"), rows, rows, rows, tokens),
        out_specs=(tokens, tokens, P("fsdp"), rows, rows, rows, rows, P("fsdp"), rows, rows, rows),
        check_vma=False,
    )
```

```python
import functools

import jax
import jax.numpy as jnp
from jax import lax
from jax.experimental import pallas as pl
from jax.experimental.pallas import tpu as pltpu
from jax.sharding import PartitionSpec as P

H = 32
KVH = 8
HD = 64
EPSILON = 1e-05
RESIDUAL = 0.22
MLP_GROUP = 16
ATTN_GROUP = 8
MESH = pl.DeviceIdType.MESH
EVEN = ((0, 64), (64, 64))
THIRDS = ((0, 48), (48, 48), (96, 32))


def plan_of(pieces, orders):
    return tuple((start, size, order) for (start, size), order in zip(pieces, orders))


MLP_GATHER = plan_of(THIRDS, ((3, 2, 1), (3, 1, 2), (3, 2, 1)))
MLP_SCATTER = plan_of(THIRDS, ((1, 2, 3), (2, 1, 3), (1, 2, 3)))


def attn_plan(group):
    if group.bits == 3:
        return plan_of(EVEN, ((1, 2), (2, 1)))
    return plan_of(THIRDS, ((1, 2, 3), (2, 3, 1), (3, 1, 2)))


PLAN_PIECES = 3
FIRST_STAGES = 3


def dot(left, right):
    return jnp.dot(left, right, preferred_element_type=jnp.float32)


def dot_cols(left, right):
    return lax.dot_general(
        left, right, (((1,), (1,)), ((), ())), preferred_element_type=jnp.float32
    )


def dot_rows(left, right):
    return lax.dot_general(
        left, right, (((0,), (0,)), ((), ())), preferred_element_type=jnp.float32
    )


def rms_factor(values):
    return lax.rsqrt(jnp.mean(values * values, axis=1, keepdims=True) + EPSILON)


def norm_back(grad_normed, values, factor, gain):
    weighted = grad_normed * gain
    centre = jnp.mean(weighted * values, axis=1, keepdims=True)
    return factor * weighted - values * (factor * factor * factor) * centre


class Group:
    def __init__(self, seq, share):
        self.seq = seq
        self.share = share
        self.count = seq * share
        self.bits = self.count.bit_length() - 1

    def member(self):
        return lax.axis_index("seq") + self.seq * (lax.axis_index("fsdp") % self.share)

    def partner(self, bit):
        mask = 1 << bit
        return offset(mask % self.seq, mask // self.seq)


class Layout:
    def __init__(self, seq_count, fsdp_count):
        self.seq = seq_count
        self.fsdp = fsdp_count
        self.seq_bits = seq_count.bit_length() - 1
        self.mlp = Group(seq_count, max(1, MLP_GROUP // seq_count))
        self.attn = Group(seq_count, max(1, ATTN_GROUP // seq_count))


def offset(low, high):
    return {
        "seq": jnp.bitwise_xor(lax.axis_index("seq"), low),
        "fsdp": jnp.bitwise_xor(lax.axis_index("fsdp"), high),
    }


def place_of(order, index):
    return sum(1 << bit for position, bit in enumerate(order) if index >> position & 1)


def softmax(query, keys, query_ids, key_ids):
    scores = dot_cols(query, keys) * (1.0 / HD)
    scores = jnp.where(key_ids <= query_ids, scores, -1e30)
    shifted = jnp.exp(scores - jnp.max(scores, axis=1, keepdims=True))
    return shifted / jnp.sum(shifted, axis=1, keepdims=True)


def rows_at(start, size):
    return pl.ds(pl.multiple_of(start, 16), size)


def greet_all(layout):
    pairs = [(1 << bit, 0) for bit in range(layout.seq_bits)]
    pairs += [(0, mask) for mask in range(1, layout.fsdp)]
    barrier = pltpu.get_barrier_semaphore()
    for low, high in pairs:
        pl.semaphore_signal(
            barrier, inc=1, device_id=offset(low, high), device_id_type=MESH
        )
    pl.semaphore_wait(barrier, len(pairs))


def gather_steps(group, rows, plan, own_ref, dst_ref, sems):
    send, recv, relay_recv, own_sem = sems
    me = group.member()
    depth = group.bits - 1
    pushed, relayed = {}, []

    def place(mask, piece):
        start, size, _ = plan[piece]
        block = jnp.bitwise_xor(me, mask)
        return dst_ref.at[rows_at(block * rows + start, size)]

    def source(mask, piece):
        start, size, _ = plan[piece]
        return own_ref.at[pl.ds(start, size)] if mask == 0 else place(mask, piece)

    def copy_to(mask, piece, recv_sem, bit):
        copy = pltpu.make_async_remote_copy(
            src_ref=source(mask, piece),
            dst_ref=place(mask, piece),
            send_sem=send,
            recv_sem=recv_sem,
            device_id=group.partner(bit),
            device_id_type=MESH,
        )
        copy.start()
        return copy

    def forward(index, piece):
        order = plan[piece][2]
        mask = place_of(order, index)
        for position in range(index.bit_length(), depth):
            number = index | 1 << position
            pushed[piece, number] = copy_to(
                mask, piece, recv.at[piece, number], order[position]
            )
        relayed.append(copy_to(mask, piece, relay_recv.at[piece, index], 0))

    for piece in range(len(plan)):
        forward(0, piece)
    local = pltpu.make_async_copy(own_ref, dst_ref.at[rows_at(me * rows, rows)], own_sem)
    local.start()
    yield
    for index in range(1, 1 << depth):
        for piece in range(len(plan)):
            pushed[piece, index].wait_recv()
            forward(index, piece)
        if index < 4:
            yield
    yield
    for copy in relayed:
        copy.wait_recv()
    local.wait()
    whole = dst_ref.at[pl.ds(0, (group.count - 1) * rows)]
    pltpu.make_async_remote_copy(
        src_ref=whole,
        dst_ref=whole,
        send_sem=send,
        recv_sem=recv.at[0, 0],
        device_id=group.partner(0),
        device_id_type=MESH,
    ).wait_send()
    yield


def gather_sems():
    count = PLAN_PIECES
    return [
        pltpu.SemaphoreType.DMA,
        pltpu.SemaphoreType.DMA((count, 8)),
        pltpu.SemaphoreType.DMA((count, 8)),
        pltpu.SemaphoreType.DMA,
    ]


def finish(steps):
    for _ in steps:
        pass


def scatter_steps(group, rows, plan, produce, total, buffers, tail, sems):
    stage, core_in, arrive = buffers
    last_out, last_in = tail
    core_send, core_recv, send, recv, last_send, last_recv = sems
    me = group.member()
    core = me % 2
    own = pl.multiple_of(core * rows, 16)
    other = pl.multiple_of((1 - core) * rows, 16)
    depth = group.bits - 1
    top = 1 << depth
    copies, pushed = {}, {}

    def chunked(start, size, body):
        @pl.loop(0, size // 16)
        def _(i):
            body(pl.multiple_of(i * 16 + start, 16))

    def slot(position, index):
        return top - (top >> position) + (index >> position + 1)

    def push(piece, position, index):
        start, size, order = plan[piece]
        rest = index ^ 1 << position
        number = slot(position, rest)
        copy = pltpu.make_async_remote_copy(
            src_ref=stage.at[place_of(order, index) // 2, rows_at(own + start, size)],
            dst_ref=arrive.at[number, pl.ds(start, size)],
            send_sem=send.at[piece, number],
            recv_sem=recv.at[piece, number],
            device_id=group.partner(order[position]),
            device_id_type=MESH,
        )
        copy.start()
        pushed[piece, position, rest] = copy

    def summed(pair, r, slots):
        value = stage[pair, rows_at(own + r, 16)].astype(jnp.float32)
        for number in slots:
            value = value + arrive[number, rows_at(r, 16)].astype(jnp.float32)
        return value

    def settle(pair):
        copies[pair].wait_recv()

        def body(r):
            stage[pair, rows_at(own + r, 16)] = (
                stage[pair, rows_at(own + r, 16)].astype(jnp.float32)
                + core_in[pair, rows_at(r, 16)].astype(jnp.float32)
            ).astype(jnp.bfloat16)

        chunked(0, rows, body)
        for piece, (_, _, order) in enumerate(plan):
            for index in range(1, top, 2):
                if place_of(order, index) == 2 * pair:
                    push(piece, 0, index)

    before = None
    for pair in sorted(range(top), key=lambda pair: (-pair.bit_count(), -pair)):
        produce(jnp.bitwise_xor(me // 2, pair), stage.at[pair])
        copies[pair] = pltpu.make_async_remote_copy(
            src_ref=stage.at[pair, rows_at(other, rows)],
            dst_ref=core_in.at[pair],
            send_sem=core_send.at[pair],
            recv_sem=core_recv.at[pair],
            device_id=group.partner(0),
            device_id_type=MESH,
        )
        copies[pair].start()
        if before is not None:
            settle(before)
        before = pair
    settle(before)
    yield
    final = {}
    for position in range(1, depth):
        for index in reversed(range(1 << position, top, 2 << position)):
            for piece, (start, size, order) in enumerate(plan):
                pair = place_of(order, index) // 2
                slots = [slot(p, index) for p in range(position)]
                for p in range(position):
                    pushed[piece, p, index].wait_recv()
                if position < depth - 1:

                    def keep(r):
                        stage[pair, rows_at(own + r, 16)] = summed(pair, r, slots).astype(
                            jnp.bfloat16
                        )

                    chunked(start, size, keep)
                    push(piece, position, index)
                else:

                    def onward(r):
                        last_out[rows_at(r, 16)] = summed(pair, r, slots).astype(jnp.bfloat16)

                    chunked(start, size, onward)
                    final[piece] = pltpu.make_async_remote_copy(
                        src_ref=last_out.at[pl.ds(start, size)],
                        dst_ref=last_in.at[pl.ds(start, size)],
                        send_sem=last_send.at[piece],
                        recv_sem=last_recv.at[piece],
                        device_id=group.partner(order[position]),
                        device_id_type=MESH,
                    )
                    final[piece].start()
        if position < depth - 1:
            yield
    slots = [slot(p, 0) for p in range(depth - 1)]
    for piece, (start, size, _) in enumerate(plan):
        for p in range(depth - 1):
            pushed[piece, p, 0].wait_recv()

        def gathered(r):
            total[rows_at(r, 16)] = summed(0, r, slots)

        chunked(start, size, gathered)
    for some in (copies, pushed):
        for copy in some.values():
            copy.wait_send()
    yield
    for piece, (start, size, _) in enumerate(plan):
        final[piece].wait_recv()

        def finished(r):
            total[rows_at(r, 16)] += last_in[rows_at(r, 16)].astype(jnp.float32)

        chunked(start, size, finished)
    for copy in final.values():
        copy.wait_send()
    yield


def scatter_scratch(rows, width):
    return [
        pltpu.VMEM((8, 2 * rows, width), jnp.bfloat16),
        pltpu.VMEM((8, rows, width), jnp.bfloat16),
        pltpu.VMEM((6, rows, width), jnp.bfloat16),
        pltpu.VMEM((rows, width), jnp.bfloat16),
        pltpu.VMEM((rows, width), jnp.bfloat16),
    ]


def scatter_sems():
    count = PLAN_PIECES
    return [
        pltpu.SemaphoreType.DMA((8,)),
        pltpu.SemaphoreType.DMA((8,)),
        pltpu.SemaphoreType.DMA((count, 6)),
        pltpu.SemaphoreType.DMA((count, 6)),
        pltpu.SemaphoreType.DMA((count,)),
        pltpu.SemaphoreType.DMA((count,)),
    ]


def loop_rows(count, size, body):
    @pl.loop(0, count // size)
    def _(i):
        body(pl.ds(pl.multiple_of(i * size, size), size))


class Sizes:
    def __init__(self, layout, tokens, block_ids, w_query, w_gate):
        self.rows, self.width = tokens.shape[1], tokens.shape[2]
        self.length = block_ids.shape[1]
        self.depth = w_query.shape[0]
        self.hidden = w_gate.shape[1] // layout.mlp.count
        self.heads = H // layout.attn.count
        self.query = self.heads * HD
        self.attn = 2 * self.query + 2 * HD
        self.mlp_rows = layout.mlp.count * self.rows
        self.attn_rows = layout.attn.count * self.rows
        self.span = max(128, min(self.length, 256 * 512 // self.length))
        self.kv_share = max(1, layout.attn.count // KVH)
        self.kv_columns = max(1, layout.attn.share // self.kv_share) * HD
        self.attn_joined = 2 * layout.attn.share * self.query + 2 * self.kv_columns


def kv_half(sizes, target, chunk):
    second = (target // sizes.kv_share) % 2 == 1
    return jnp.where(second, chunk[:, HD:], chunk[:, :HD])


def attention_scores(sizes, qkv, ids, seq, start, head):
    base = sizes.query
    keys_rows = rows_at(seq * sizes.length, sizes.length)
    query_rows = rows_at(seq * sizes.length + start, sizes.span)
    query = qkv[query_rows, head * HD : (head + 1) * HD]
    keys = qkv[keys_rows, base : base + HD]
    values = qkv[keys_rows, base + HD : base + 2 * HD]
    key_ids = ids[seq, 0:1, :]
    query_ids = jnp.transpose(ids[seq, :, pl.ds(start, sizes.span)])[:, :1]
    return query, keys, values, softmax(query, keys, query_ids, key_ids)


def seq_gather(layout, out_ref, width, sems):
    send, recv = sems
    me = lax.axis_index("seq")
    bits = [1 << bit for bit in reversed(range(layout.seq_bits))]

    def block(mask):
        start = jnp.bitwise_xor(me, mask) * width
        return out_ref.at[:, pl.ds(pl.multiple_of(start, 128), width)]

    copies = {}

    def push(mask, bit):
        copy = pltpu.make_async_remote_copy(
            src_ref=block(mask),
            dst_ref=block(mask),
            send_sem=send.at[mask ^ bit],
            recv_sem=recv.at[mask ^ bit],
            device_id=offset(bit, 0),
            device_id_type=MESH,
        )
        copy.start()
        copies[mask ^ bit] = copy

    for bit in bits:
        push(0, bit)
    yield
    held = [0]
    for bit in bits:
        for mask in held[1:]:
            push(mask, bit)
        new = [mask ^ bit for mask in held]
        if bit != bits[-1]:
            for mask in new:
                copies[mask].wait_recv()
        held = held + new
    yield
    for mask in held[len(held) // 2 :]:
        copies[mask].wait_recv()
    for copy in copies.values():
        copy.wait_send()
    yield


def layer_kernel(
    layout,
    sizes,
    tok_ref,
    cot_ref,
    ids_ref,
    gains_ref,
    wq_ref,
    wk_ref,
    wv_ref,
    wo_ref,
    wg_ref,
    wu_ref,
    wd_ref,
    mixed,
    grad_tok,
    gain_sum,
    gate_out,
    up_out,
    down_out,
    attn_out,
    gate_recv,
    up_recv,
    down_recv,
    attn_recv_hbm,
    h1_out,
    g_all,
    h_all,
    w_in,
    w_down,
    wa,
    qkv,
    attended,
    hid,
    grad_in,
    middle,
    total,
    grad_mid,
    tok,
    down_stage,
    gains,
    ids,
    grad_kv,
    terms,
    gain_in,
    gain_seq,
    own_sum,
    stage,
    core_in,
    arrive,
    last_out,
    last_in,
    down_total,
    down_last_out,
    down_last_in,
    x_send,
    x_recv,
    x_relay,
    x_own,
    h_send,
    h_recv,
    h_relay,
    h_own,
    g_send,
    g_recv,
    g_relay,
    g_own,
    core_send,
    core_recv,
    s_send,
    s_recv,
    last_send,
    last_recv,
    down_last_send,
    down_last_recv,
    credit,
    ready,
    attn_send,
    attn_recv,
    gain_send,
    gain_recv,
    id_send,
    id_recv,
    mlp_send,
    mlp_recv,
    load_sem,
    grad_send,
    grad_recv,
    join_send,
    join_recv,
    own_sem,
    sum_send,
    sum_recv,
    gs_send,
    gs_recv,
    pick_sem,
):
    share, fsdp, depth = layout.attn.share, layout.fsdp, sizes.depth
    mlp_share = layout.mlp.share
    seq_me, fsdp_me = lax.axis_index("seq"), lax.axis_index("fsdp")
    query = sizes.query
    rows, hidden = sizes.rows, sizes.hidden

    count, few = sizes.mlp_rows, sizes.attn_rows
    near = pl.ds(0, few)
    wq = grad_in.at[pl.ds(0, depth), pl.ds(0, share * query)]
    wo = grad_in.at[pl.ds(depth, depth), pl.ds(0, share * query)]
    wk = grad_in.at[pl.ds(0, depth), pl.ds(hidden, 128)]
    wv = grad_in.at[pl.ds(depth, depth), pl.ds(hidden, 128)]
    pack = [grad_in.at[pl.ds((2 + j) * depth, depth), pl.ds(0, sizes.attn)] for j in range(share)]

    def tell(sem):
        for bit in range(layout.mlp.bits):
            pl.semaphore_signal(
                sem, inc=1, device_id=layout.mlp.partner(bit), device_id_type=MESH
            )

    loads = []

    def load(src, dst):
        copy = pltpu.make_async_copy(src, dst, load_sem.at[len(loads)])
        copy.start()
        loads.append(copy)
        return copy

    def columns(ref, start, size):
        return ref.at[:, pl.ds(pl.multiple_of(start, 128), size)]

    load(tok_ref, tok)
    own_rows = pl.ds(pl.multiple_of(fsdp_me * depth, 128), depth)
    load(gains_ref, gains.at[:, own_rows])
    load(columns(wq_ref, seq_me * share * query, share * query), wq)
    load(columns(wo_ref, seq_me * share * query, share * query), wo)
    chunk = seq_me * share // (2 * sizes.kv_share) * 128
    load(columns(wk_ref, chunk, 128), wk)
    load(columns(wv_ref, chunk, 128), wv)
    load(ids_ref, ids.at[fsdp_me % share])
    load(cot_ref, down_last_out)
    greet_all(layout)
    small = []
    for mask in range(1, fsdp):
        copy = pltpu.make_async_remote_copy(
            src_ref=gains_ref,
            dst_ref=gains.at[:, own_rows],
            send_sem=gain_send.at[mask],
            recv_sem=gain_recv.at[mask],
            device_id=offset(0, mask),
            device_id_type=MESH,
        )
        copy.start()
        small.append(copy)
    for copy in loads:
        copy.wait()
    for j in range(share):
        target = seq_me * share + j
        pack[j][...] = jnp.concatenate(
            [
                wq[:, j * query : (j + 1) * query],
                kv_half(sizes, target, wk[...]),
                kv_half(sizes, target, wv[...]),
                wo[:, j * query : (j + 1) * query],
            ],
            axis=1,
        )
    def packed(j):
        start = pl.multiple_of((2 + j) * depth, 128)
        return grad_in.at[pl.ds(start, depth), pl.ds(0, sizes.attn)]

    attn = {}

    def send_attn(number, src, place, hop):
        attn[number] = pltpu.make_async_remote_copy(
            src_ref=src,
            dst_ref=wa.at[place],
            send_sem=attn_send.at[number],
            recv_sem=attn_recv.at[number],
            device_id=offset(0, hop),
            device_id_type=MESH,
        )
        attn[number].start()

    for mask in (4, 5, 3, 2, 1):
        send_attn(mask, packed(jnp.bitwise_xor(fsdp_me, mask) % share), own_rows, mask)
    wa[own_rows] = packed(fsdp_me % share)[...]
    for copy in small:
        copy.wait()
    gain_one = gains[0:1].astype(jnp.float32)

    def norm(r):
        values = tok[r].astype(jnp.float32)
        grad_tok[r] = (values * rms_factor(values) * gain_one).astype(jnp.bfloat16)

    loop_rows(rows, 32, norm)
    x_steps = gather_steps(
        layout.attn, rows, attn_plan(layout.attn), grad_tok, h_all.at[near], (x_send, x_recv, x_relay, x_own)
    )
    next(x_steps)
    id_copies = []
    for mask in range(1, share):
        copy = pltpu.make_async_remote_copy(
            src_ref=ids_ref,
            dst_ref=ids.at[fsdp_me % share],
            send_sem=id_send.at[mask],
            recv_sem=id_recv.at[mask],
            device_id=offset(0, mask),
            device_id_type=MESH,
        )
        copy.start()
        id_copies.append(copy)
    g_steps = gather_steps(
        layout.mlp, rows, MLP_GATHER, cot_ref, g_all, (g_send, g_recv, g_relay, g_own)
    )
    next(g_steps)
    for _ in range(FIRST_STAGES):
        next(x_steps)
    for mask in (4, 5):
        attn[mask].wait_recv()
        start = jnp.bitwise_xor(fsdp_me, mask) * depth
        far_rows = pl.ds(pl.multiple_of(start, 128), depth)
        send_attn(mask ^ 2, wa.at[far_rows], far_rows, 2)

    mlp = []

    def send_mlp(ref, out, place, index, masks):
        def at(j):
            return columns(ref, (seq_me * mlp_share + j) * hidden, hidden)

        home = out.at[own_rows, pl.ds(place, hidden)]
        for mask in masks:
            if mask:
                copy = pltpu.make_async_remote_copy(
                    src_ref=at(jnp.bitwise_xor(fsdp_me, mask) % mlp_share),
                    dst_ref=home,
                    send_sem=mlp_send.at[index, mask],
                    recv_sem=mlp_recv.at[index, mask],
                    device_id=offset(0, mask),
                    device_id_type=MESH,
                )
            else:
                copy = pltpu.make_async_copy(at(fsdp_me % mlp_share), home, load_sem.at[1 + index])
            copy.start()
            mlp.append(copy)

    def send_weights(masks):
        masks = list(masks)
        send_mlp(wg_ref, w_in, 0, 0, masks)
        send_mlp(wu_ref, w_in, hidden, 1, masks)
        send_mlp(wd_ref, w_down, 0, 2, masks)

    send_weights(reversed(range(fsdp)))
    finish(x_steps)
    h1_copy = pltpu.make_async_copy(h_all.at[near], h1_out, load_sem.at[0])
    h1_copy.start()
    next(g_steps)
    for mask, copy in attn.items():
        copy.wait_send()
        if mask not in (4, 5):
            copy.wait_recv()

    def project(r):
        qkv[r] = dot(h_all[r], wa[:, : query + 2 * HD]).astype(jnp.bfloat16)

    loop_rows(sizes.attn_rows, 256, project)
    next(g_steps)
    for copy in id_copies:
        copy.wait()

    blocks = sizes.length // sizes.span

    @pl.loop(0, share * blocks)
    def _(i):
        seq = i // blocks
        start = pl.multiple_of((i % blocks) * sizes.span, sizes.span)
        outs = []
        for head in range(sizes.heads):
            _, _, values, probs = attention_scores(sizes, qkv, ids, seq, start, head)
            outs.append(dot(probs.astype(jnp.bfloat16), values))
        attended[rows_at(seq * sizes.length + start, sizes.span)] = jnp.concatenate(
            outs, axis=1
        ).astype(jnp.bfloat16)

    h1_copy.wait()
    tell(ready)

    def out_rows(pair, ref):
        block = attended[rows_at(pair * 2 * rows, 2 * rows)]

        @pl.loop(0, sizes.width // 512)
        def _(i):
            piece = pl.ds(pl.multiple_of(i * 512, 512), 512)
            ref[:, piece] = dot_cols(block, wa[piece, query + 2 * HD :]).astype(jnp.bfloat16)

    next(g_steps)
    next(g_steps)
    steps = scatter_steps(
        layout.attn, rows, attn_plan(layout.attn), out_rows, middle, (stage, core_in, arrive),
        (last_out, last_in), (core_send, core_recv, s_send, s_recv, last_send, last_recv),
    )
    next(steps)
    next(g_steps)
    finish(steps)
    gain_two = gains[8:9].astype(jnp.float32)

    def second(r):
        values = tok[r].astype(jnp.float32) + RESIDUAL * middle[r]
        middle[r] = values
        grad_tok[r] = (values * rms_factor(values) * gain_two).astype(jnp.bfloat16)

    loop_rows(rows, 32, second)
    pl.semaphore_wait(ready, layout.mlp.bits)
    h_steps = gather_steps(
        layout.mlp, rows, MLP_GATHER, grad_tok, h_all, (h_send, h_recv, h_relay, h_own)
    )
    next(h_steps)
    next(h_steps)
    finish(g_steps)
    finish(h_steps)
    for copy in mlp:
        copy.wait()

    base = query + 2 * HD
    scatter = (stage, core_in, arrive)
    sems = (core_send, core_recv, s_send, s_recv)
    scatter_sem = sems + (last_send, last_recv)
    spare = few < count

    def piece_at(ref, mask):
        column = pl.ds(mask // 4 * sizes.attn, sizes.attn)
        return ref.at[pl.ds(mask % 4 * depth, depth), column]

    def staged(mask):
        if spare:
            return piece_at(h_all.at[pl.ds(few, few)], mask)
        return w_down.at[block(mask), pl.ds(0, sizes.attn)]

    if spare:
        own_sum = g_all.at[pl.ds(few, depth)]

    def hidden_rows(r):
        h = h_all[r]
        gate = dot(h, w_in[:, :hidden])
        upward = dot(h, w_in[:, hidden:])
        grad = (RESIDUAL * g_all[r].astype(jnp.float32)).astype(jnp.bfloat16)
        g_all[r] = grad
        grad_hidden = dot(grad, w_down[...])
        sigma = jax.nn.sigmoid(gate)
        hid[r] = (gate * sigma * upward).astype(jnp.bfloat16)
        grad_in[r, hidden:] = (grad_hidden * gate * sigma).astype(jnp.bfloat16)
        grad_in[r, :hidden] = (
            grad_hidden * upward * sigma * (1.0 + gate * (1.0 - sigma))
        ).astype(jnp.bfloat16)

    loop_rows(count, 256, hidden_rows)

    sends = []
    far = list(reversed(range(1, fsdp))) + [0]

    def owner_columns(mask):
        start = jnp.bitwise_xor(fsdp_me, mask) * depth
        return pl.ds(pl.multiple_of(start, 128), depth)

    def send_grad(mask, src, dst, index):
        if mask == 0:
            return
        copy = pltpu.make_async_remote_copy(
            src_ref=src,
            dst_ref=dst.at[mask],
            send_sem=grad_send.at[index, mask],
            recv_sem=grad_recv.at[index, mask],
            device_id=offset(0, mask),
            device_id_type=MESH,
        )
        copy.start()
        sends.append((index, mask, copy))

    def block(mask):
        return pl.ds(mask * depth, depth)

    def grad_down(mask):
        down_stage[block(mask)] = dot_rows(g_all[:, owner_columns(mask)], hid[...]).astype(
            jnp.bfloat16
        )
        send_grad(mask, down_stage.at[block(mask)], down_recv, 0)

    for mask in far:
        grad_down(mask)

    def hidden_back(pair, ref):
        left = grad_in[rows_at(pair * 2 * rows, 2 * rows)]

        @pl.loop(0, sizes.width // 512)
        def _(i):
            piece = pl.ds(pl.multiple_of(i * 512, 512), 512)
            ref[:, piece] = dot_cols(left, w_in[piece]).astype(jnp.bfloat16)

    steps = scatter_steps(layout.mlp, rows, MLP_SCATTER, hidden_back, total, scatter, (last_out, last_in), scatter_sem)
    next(steps)

    def grad_up(mask):
        w_in[block(mask)] = dot_rows(h_all[:, owner_columns(mask)], grad_in[...]).astype(
            jnp.bfloat16
        )

    for turn in range(3):
        for mask in far[turn * 3 : turn * 3 + 3]:
            grad_up(mask)
        next(steps)
    finish(steps)
    h1_copy = pltpu.make_async_copy(h1_out, h_all.at[near], load_sem.at[0])
    h1_copy.start()
    terms[...] = jnp.zeros_like(terms)

    def norm_two(r):
        values, normed = middle[r], total[r]
        factor = rms_factor(values)
        terms[1:2] += jnp.sum(normed * values * factor, axis=0, keepdims=True)
        grad = down_last_out[r].astype(jnp.float32) + norm_back(normed, values, factor, gain_two)
        grad_mid[r] = grad
        last_out[r] = (RESIDUAL * grad).astype(jnp.bfloat16)

    loop_rows(rows, 32, norm_two)
    def collect(index, share, src, width, own_piece, landing, combine, out, out_width):
        picks = []
        for number, mask, copy in sends:
            if number == index:
                copy.wait_recv()
                pick = pltpu.make_async_copy(
                    src.at[mask], landing(mask), pick_sem.at[index, mask]
                )
                pick.start()
                picks.append(pick)
        yield
        for pick in picks:
            pick.wait()

        def terms_of(low, start, size):
            cols = pl.ds(start, size)
            value = own_piece[:, cols] if low == 0 else landing(low)[:, cols]
            value = value.astype(jnp.float32)
            for mask in range(low + share, fsdp, share):
                value = value + landing(mask)[:, cols].astype(jnp.float32)
            return value

        combine(terms_of, share, width)
        home = pl.multiple_of(seq_me * out_width, 128)
        local = pltpu.make_async_copy(
            own_sum.at[:, pl.ds(0, out_width)], out.at[:, pl.ds(home, out_width)], own_sem.at[index]
        )
        local.start()
        local.wait()
        yield from seq_gather(layout, out, out_width, (join_send.at[index], join_recv.at[index]))

    def place_columns(terms_of, share, width):
        mine = fsdp_me % share
        for low in range(share):
            start = pl.multiple_of(jnp.bitwise_xor(mine, low) * width, 128)
            own_sum[:, pl.ds(start, width)] = terms_of(low, 0, width).astype(jnp.bfloat16)

    def place_attn(terms_of, share, width):
        mine = fsdp_me % share
        for low in range(share):
            for source, target in ((0, 0), (base, share * query)):
                start = pl.multiple_of(target + jnp.bitwise_xor(mine, low) * query, 128)
                own_sum[:, pl.ds(start, query)] = terms_of(low, source, query).astype(
                    jnp.bfloat16
                )
        both = sizes.kv_columns
        at = 2 * share * query
        for source in (query, query + HD):
            heads = []
            for first in range(0, share, sizes.kv_share):
                value = terms_of(first, source, HD)
                for low in range(first + 1, min(share, first + sizes.kv_share)):
                    value = value + terms_of(low, source, HD)
                heads.append(value)
            value = heads[0]
            if len(heads) == 2:
                upper = mine // sizes.kv_share == 1
                value = jnp.concatenate(
                    [jnp.where(upper, heads[1], heads[0]), jnp.where(upper, heads[0], heads[1])],
                    axis=1,
                )
            own_sum[:, at : at + both] = value.astype(jnp.bfloat16)
            at += both

    mlp_share, attn_share = layout.mlp.share, layout.attn.share
    joined = mlp_share * hidden
    steps_down = collect(
        0, mlp_share, down_recv, hidden, down_stage.at[block(0)],
        lambda mask: grad_in.at[block(mask), pl.ds(0, hidden)],
        place_columns, down_out, joined,
    )
    a_steps = gather_steps(
        layout.attn, rows, attn_plan(layout.attn), last_out, g_all.at[near], (x_send, x_recv, x_relay, x_own)
    )
    next(a_steps)
    next(a_steps)
    for mask in far:
        send_grad(mask, w_in.at[block(mask), pl.ds(0, hidden)], gate_recv, 1)
    for mask in far:
        send_grad(mask, w_in.at[block(mask), pl.ds(hidden, hidden)], up_recv, 2)
    next(steps_down)
    finish(a_steps)

    def down_rows(pair, ref):
        left = hid[rows_at(pair * 2 * rows, 2 * rows)]

        @pl.loop(0, sizes.width // 512)
        def _(i):
            piece = pl.ds(pl.multiple_of(i * 512, 512), 512)
            ref[:, piece] = dot_cols(left, w_down[piece]).astype(jnp.bfloat16)

    steps_low = scatter_steps(
        layout.mlp, rows, MLP_SCATTER, down_rows, down_total, scatter, (down_last_out, down_last_in),
        sems + (down_last_send, down_last_recv),
    )
    next(steps_low)


    blocks = sizes.length // sizes.span

    def attend_back_block(i):
        seq = i // blocks
        part = i % blocks
        start = pl.multiple_of(part * sizes.span, sizes.span)
        here = rows_at(seq * sizes.length + start, sizes.span)
        grad_out = dot(g_all[here], wa[:, base:]).astype(jnp.bfloat16)
        grads, grad_keys, grad_values = [], 0.0, 0.0
        for head in range(sizes.heads):
            left, keys, values, probs = attention_scores(sizes, qkv, ids, seq, start, head)
            grad = grad_out[:, head * HD : (head + 1) * HD]
            grad_probs = dot_cols(grad, values)
            centre = jnp.sum(probs * grad_probs, axis=1, keepdims=True)
            grad_scores = (probs * (grad_probs - centre)).astype(jnp.bfloat16)
            grads.append(dot(grad_scores, keys) * (1.0 / HD))
            grad_keys = grad_keys + dot_rows(grad_scores, left) * (1.0 / HD)
            grad_values = grad_values + dot_rows(probs.astype(jnp.bfloat16), grad)
        both = jnp.concatenate([grad_keys, grad_values], axis=1)

        @pl.when(part == 0)
        def _():
            grad_kv[...] = both

        @pl.when(part > 0)
        def _():
            grad_kv[...] += both

        qkv[here, :query] = jnp.concatenate(grads, axis=1).astype(jnp.bfloat16)

        @pl.when(part == blocks - 1)
        def _():
            qkv[rows_at(seq * sizes.length, sizes.length), query:] = grad_kv[...].astype(
                jnp.bfloat16
            )

    turns = layout.attn.share * blocks

    @pl.loop(0, turns // 2)
    def _(i):
        attend_back_block(i)

    next(steps_down)
    next(steps_low)

    @pl.loop(turns // 2, turns)
    def _(i):
        attend_back_block(i)

    next(steps_low)
    tell(credit)
    next(steps_down)
    steps_gate = collect(
        1, mlp_share, gate_recv, hidden, w_in.at[block(0), pl.ds(0, hidden)],
        lambda mask: grad_in.at[block(mask), pl.ds(0, hidden)],
        place_columns, gate_out, joined,
    )
    next(steps_gate)
    next(steps_gate)
    pl.semaphore_wait(credit, layout.mlp.bits)

    def qkv_back(pair, ref):
        left = qkv[rows_at(pair * 2 * rows, 2 * rows)]

        @pl.loop(0, sizes.width // 512)
        def _(i):
            piece = pl.ds(pl.multiple_of(i * 512, 512), 512)
            ref[:, piece] = dot_cols(left, wa[piece, :base]).astype(jnp.bfloat16)

    h1_copy.wait()

    def grad_attn(mask):
        cols = owner_columns(mask)
        staged(mask)[:, :base] = dot_rows(h_all[near, cols], qkv[...]).astype(jnp.bfloat16)
        staged(mask)[:, base:] = dot_rows(g_all[near, cols], attended[...]).astype(
            jnp.bfloat16
        )
        send_grad(mask, staged(mask), attn_recv_hbm, 3)

    for mask in far[: fsdp // 2]:
        grad_attn(mask)
    steps = scatter_steps(layout.attn, rows, attn_plan(layout.attn), qkv_back, total, scatter, (last_out, last_in), scatter_sem)
    next(steps)
    for mask in far[fsdp // 2 :]:
        grad_attn(mask)
    next(steps)
    next(steps_gate)
    finish(steps)

    def norm_one(r):
        values, normed = tok[r].astype(jnp.float32), total[r]
        factor = rms_factor(values)
        terms[0:1] += jnp.sum(normed * values * factor, axis=0, keepdims=True)
        grad = grad_mid[r] + norm_back(normed, values, factor, gain_one)
        grad_tok[r] = grad.astype(jnp.bfloat16)

    loop_rows(rows, 32, norm_one)
    finish(steps_low)

    def mix(r):
        mixed[r] = (middle[r] + RESIDUAL * down_total[r]).astype(jnp.bfloat16)

    loop_rows(rows, 32, mix)
    gain_copies = []
    for mask in range(1, fsdp):
        copy = pltpu.make_async_remote_copy(
            src_ref=terms.at[:, owner_columns(mask)],
            dst_ref=gain_in.at[mask],
            send_sem=sum_send.at[mask],
            recv_sem=sum_recv.at[mask],
            device_id=offset(0, mask),
            device_id_type=MESH,
        )
        copy.start()
        gain_copies.append(copy)

    steps_up = collect(
        2, mlp_share, up_recv, hidden, w_in.at[block(0), pl.ds(hidden, hidden)], lambda mask: grad_in.at[block(mask), pl.ds(hidden, hidden)],
        place_columns, up_out, joined,
    )
    next(steps_up)
    next(steps_up)
    steps_attn = collect(
        3, attn_share, attn_recv_hbm, sizes.attn, staged(0), functools.partial(piece_at, g_all),
        place_attn, attn_out, sizes.attn_joined,
    )
    next(steps_attn)
    next(steps_attn)
    next(steps_up)

    value = terms[:, owner_columns(0)]
    for copy in gain_copies:
        copy.wait()
    for mask in range(1, fsdp):
        value = value + gain_in[mask]
    for bit in range(layout.seq_bits):
        gain_seq[2 * bit] = value
        copy = pltpu.make_async_remote_copy(
            src_ref=gain_seq.at[2 * bit],
            dst_ref=gain_seq.at[2 * bit + 1],
            send_sem=gs_send.at[bit],
            recv_sem=gs_recv.at[bit],
            device_id=offset(1 << bit, 0),
            device_id_type=MESH,
        )
        copy.start()
        copy.wait()
        value = value + gain_seq[2 * bit + 1]
    gain_sum[...] = value
    for steps in (steps_attn, steps_down, steps_gate, steps_up):
        finish(steps)
    for _, _, copy in sends:
        copy.wait_send()


def layer(layout, sizes, *args):
    width, count, few = sizes.width, sizes.mlp_rows, sizes.attn_rows
    hbm, vmem = pl.BlockSpec(memory_space=pl.ANY), pl.BlockSpec(memory_space=pltpu.VMEM)
    share, depth, fsdp = layout.attn.share, sizes.depth, layout.fsdp
    joined = layout.mlp.share * sizes.hidden
    rows, hidden, base = sizes.rows, sizes.hidden, sizes.query + 2 * HD
    bf16, f32 = jnp.bfloat16, jnp.float32
    shapes = [
        ((rows, width), bf16, vmem),
        ((rows, width), bf16, vmem),
        ((8, depth), f32, vmem),
        ((depth, layout.seq * joined), bf16, hbm),
        ((depth, layout.seq * joined), bf16, hbm),
        ((depth, layout.seq * joined), bf16, hbm),
        ((depth, layout.seq * sizes.attn_joined), bf16, hbm),
        ((fsdp, depth, hidden), bf16, hbm),
        ((fsdp, depth, hidden), bf16, hbm),
        ((fsdp, depth, hidden), bf16, hbm),
        ((fsdp, depth, sizes.attn), bf16, hbm),
        ((few, width), bf16, hbm),
    ]
    dma = pltpu.SemaphoreType.DMA
    seq = layout.seq
    return pl.pallas_call(
        functools.partial(layer_kernel, layout, sizes),
        out_shape=[jax.ShapeDtypeStruct(shape, dtype) for shape, dtype, _ in shapes],
        in_specs=[hbm] * len(args),
        out_specs=[spec for _, _, spec in shapes],
        scratch_shapes=[
            pltpu.VMEM((count, width), bf16),
            pltpu.VMEM((count, width), bf16),
            pltpu.VMEM((width, 2 * hidden), bf16),
            pltpu.VMEM((width, hidden), bf16),
            pltpu.VMEM((width, sizes.attn), bf16),
            pltpu.VMEM((few, base), bf16),
            pltpu.VMEM((few, sizes.query), bf16),
            pltpu.VMEM((count, hidden), bf16),
            pltpu.VMEM((count, 2 * hidden), bf16),
            pltpu.VMEM((rows, width), f32),
            pltpu.VMEM((rows, width), f32),
            pltpu.VMEM((rows, width), f32),
            pltpu.VMEM((rows, width), bf16),
            pltpu.VMEM((width, hidden), bf16),
            pltpu.VMEM((16, width), bf16),
            pltpu.VMEM((share, 8, sizes.length), jnp.int32),
            pltpu.VMEM((sizes.length, 2 * HD), f32),
            pltpu.VMEM((8, width), f32),
            pltpu.VMEM((fsdp, 8, depth), f32),
            pltpu.VMEM((2 * layout.seq_bits, 8, depth), f32),
            pltpu.VMEM((depth, max(joined, sizes.attn_joined) if few == count else 128), bf16),
        ]
        + scatter_scratch(rows, width)
        + [
            pltpu.VMEM((rows, width), f32),
            pltpu.VMEM((rows, width), bf16),
            pltpu.VMEM((rows, width), bf16),
        ]
        + gather_sems() * 3
        + scatter_sems()
        + [dma((PLAN_PIECES,)), dma((PLAN_PIECES,))]
        + [pltpu.SemaphoreType.REGULAR, pltpu.SemaphoreType.REGULAR]
        + [dma((fsdp,)), dma((fsdp,)), dma((fsdp,)), dma((fsdp,))]
        + [dma((share,)), dma((share,)), dma((3, fsdp)), dma((3, fsdp)), dma((8,))]
        + [dma((4, fsdp)), dma((4, fsdp)), dma((4, seq)), dma((4, seq)), dma((4,))]
        + [dma((fsdp,)), dma((fsdp,)), dma((layout.seq_bits,)), dma((layout.seq_bits,))]
        + [dma((4, fsdp))],
        compiler_params=pltpu.CompilerParams(
            collective_id=1, has_side_effects=True, vmem_limit_bytes=125 * 512 * 1024
        ),
        name="layer",
    )(*args)


def body(
    tokens,
    block_ids,
    gain_attn,
    w_query,
    w_key,
    w_value,
    w_out,
    gain_mlp,
    w_gate,
    w_up,
    w_down,
    cotangent,
):
    layout = Layout(lax.axis_size("seq"), lax.axis_size("fsdp"))
    depth = w_gate.shape[0]
    sizes = Sizes(layout, tokens, block_ids, w_query, w_gate)
    gains_own = jnp.concatenate(
        [jnp.broadcast_to(gain[None], (8, depth)) for gain in (gain_attn, gain_mlp)], axis=0
    )
    ids_own = jnp.broadcast_to(block_ids, (8, block_ids.shape[1]))
    mixed, grad_tokens, gain_sum, grad_gate, grad_up, grad_down, grad_attn, *_ = layer(
        layout,
        sizes,
        tokens[0],
        cotangent[0],
        ids_own,
        gains_own,
        w_query,
        w_key,
        w_value,
        w_out,
        w_gate,
        w_up,
        w_down,
    )
    wide, narrow = layout.attn.share * sizes.query, sizes.kv_columns

    def joined(start, size):
        columns = [
            grad_attn[:, i * sizes.attn_joined + start : i * sizes.attn_joined + start + size]
            for i in range(layout.seq)
        ]
        return jnp.concatenate(columns, axis=1).astype(jnp.float32)

    def heads(start):
        columns = joined(start, narrow)
        if layout.seq * narrow > KVH * HD:
            columns = jnp.sum(columns.reshape(depth, KVH, -1, HD), axis=2).reshape(depth, -1)
        return columns

    return (
        mixed[None],
        grad_tokens[None],
        gain_sum[0],
        joined(0, wide),
        heads(2 * wide),
        heads(2 * wide + narrow),
        joined(wide, wide),
        gain_sum[1],
        grad_gate.astype(jnp.float32),
        grad_up.astype(jnp.float32),
        grad_down.astype(jnp.float32),
    )


def solution(mesh):
    tokens, rows = P("fsdp", "seq", None), P("fsdp", None)
    return jax.shard_map(
        body,
        mesh=mesh,
        in_specs=(tokens, rows, P("fsdp"), rows, rows, rows, rows, P("fsdp"), rows, rows, rows, tokens),
        out_specs=(tokens, tokens, P("fsdp"), rows, rows, rows, rows, P("fsdp"), rows, rows, rows),
        check_vma=False,
    )
```

```python
import functools

import jax
import jax.numpy as jnp
from jax import lax
from jax.experimental import pallas as pl
from jax.experimental.pallas import tpu as pltpu
from jax.sharding import PartitionSpec as P

H = 32
KVH = 8
HD = 64
EPSILON = 1e-05
RESIDUAL = 0.22
MLP_GROUP = 16
ATTN_GROUP = 8
MESH = pl.DeviceIdType.MESH
EVEN = ((0, 64), (64, 64))
THIRDS = ((0, 48), (48, 48), (96, 32))


def plan_of(pieces, orders):
    return tuple((start, size, order) for (start, size), order in zip(pieces, orders))


MLP_GATHER = plan_of(THIRDS, ((3, 2, 1), (3, 1, 2), (3, 2, 1)))
MLP_SCATTER = plan_of(THIRDS, ((1, 2, 3), (2, 1, 3), (1, 2, 3)))


def attn_plan(group, orders=((1, 2), (2, 1))):
    if group.bits == 3:
        return plan_of(EVEN, orders)
    return plan_of(THIRDS, ((1, 2, 3), (2, 3, 1), (3, 1, 2)))


PLAN_PIECES = 3
FIRST_STAGES = 3


def dot(left, right):
    return jnp.dot(left, right, preferred_element_type=jnp.float32)


def dot_cols(left, right):
    return lax.dot_general(
        left, right, (((1,), (1,)), ((), ())), preferred_element_type=jnp.float32
    )


def dot_rows(left, right):
    return lax.dot_general(
        left, right, (((0,), (0,)), ((), ())), preferred_element_type=jnp.float32
    )


def rms_factor(values):
    return lax.rsqrt(jnp.mean(values * values, axis=1, keepdims=True) + EPSILON)


def norm_back(grad_normed, values, factor, gain):
    weighted = grad_normed * gain
    centre = jnp.mean(weighted * values, axis=1, keepdims=True)
    return factor * weighted - values * (factor * factor * factor) * centre


class Group:
    def __init__(self, seq, share):
        self.seq = seq
        self.share = share
        self.count = seq * share
        self.bits = self.count.bit_length() - 1

    def member(self):
        return lax.axis_index("seq") + self.seq * (lax.axis_index("fsdp") % self.share)

    def partner(self, bit):
        mask = 1 << bit
        return offset(mask % self.seq, mask // self.seq)


class Layout:
    def __init__(self, seq_count, fsdp_count):
        self.seq = seq_count
        self.fsdp = fsdp_count
        self.seq_bits = seq_count.bit_length() - 1
        self.mlp = Group(seq_count, max(1, MLP_GROUP // seq_count))
        self.attn = Group(seq_count, max(1, ATTN_GROUP // seq_count))


def offset(low, high):
    return {
        "seq": jnp.bitwise_xor(lax.axis_index("seq"), low),
        "fsdp": jnp.bitwise_xor(lax.axis_index("fsdp"), high),
    }


def place_of(order, index):
    return sum(1 << bit for position, bit in enumerate(order) if index >> position & 1)


def softmax(query, keys, query_ids, key_ids):
    scores = dot_cols(query, keys) * (1.0 / HD)
    scores = jnp.where(key_ids <= query_ids, scores, -1e30)
    shifted = jnp.exp(scores - jnp.max(scores, axis=1, keepdims=True))
    return shifted / jnp.sum(shifted, axis=1, keepdims=True)


def rows_at(start, size):
    return pl.ds(pl.multiple_of(start, 16), size)


def greet_all(layout):
    pairs = [(1 << bit, 0) for bit in range(layout.seq_bits)]
    pairs += [(0, mask) for mask in range(1, layout.fsdp)]
    barrier = pltpu.get_barrier_semaphore()
    for low, high in pairs:
        pl.semaphore_signal(
            barrier, inc=1, device_id=offset(low, high), device_id_type=MESH
        )
    pl.semaphore_wait(barrier, len(pairs))


def gather_steps(group, rows, plan, own_ref, dst_ref, sems):
    send, recv, relay_recv, own_sem = sems
    me = group.member()
    depth = group.bits - 1
    pushed, relayed = {}, []

    def place(mask, piece):
        start, size, _ = plan[piece]
        block = jnp.bitwise_xor(me, mask)
        return dst_ref.at[rows_at(block * rows + start, size)]

    def source(mask, piece):
        start, size, _ = plan[piece]
        return own_ref.at[pl.ds(start, size)] if mask == 0 else place(mask, piece)

    def copy_to(mask, piece, recv_sem, bit):
        copy = pltpu.make_async_remote_copy(
            src_ref=source(mask, piece),
            dst_ref=place(mask, piece),
            send_sem=send,
            recv_sem=recv_sem,
            device_id=group.partner(bit),
            device_id_type=MESH,
        )
        copy.start()
        return copy

    def forward(index, piece):
        order = plan[piece][2]
        mask = place_of(order, index)
        for position in range(index.bit_length(), depth):
            number = index | 1 << position
            pushed[piece, number] = copy_to(
                mask, piece, recv.at[piece, number], order[position]
            )
        relayed.append(copy_to(mask, piece, relay_recv.at[piece, index], 0))

    for piece in range(len(plan)):
        forward(0, piece)
    local = pltpu.make_async_copy(own_ref, dst_ref.at[rows_at(me * rows, rows)], own_sem)
    local.start()
    yield
    for index in range(1, 1 << depth):
        for piece in range(len(plan)):
            pushed[piece, index].wait_recv()
            forward(index, piece)
        if index < 4:
            yield
    yield
    for copy in relayed:
        copy.wait_recv()
    local.wait()
    whole = dst_ref.at[pl.ds(0, (group.count - 1) * rows)]
    pltpu.make_async_remote_copy(
        src_ref=whole,
        dst_ref=whole,
        send_sem=send,
        recv_sem=recv.at[0, 0],
        device_id=group.partner(0),
        device_id_type=MESH,
    ).wait_send()
    yield


def gather_sems():
    count = PLAN_PIECES
    return [
        pltpu.SemaphoreType.DMA,
        pltpu.SemaphoreType.DMA((count, 8)),
        pltpu.SemaphoreType.DMA((count, 8)),
        pltpu.SemaphoreType.DMA,
    ]


def finish(steps):
    for _ in steps:
        pass


def scatter_steps(group, rows, plan, produce, total, buffers, tail, sems):
    stage, core_in, arrive = buffers
    last_out, last_in = tail
    core_send, core_recv, send, recv, last_send, last_recv = sems
    me = group.member()
    core = me % 2
    own = pl.multiple_of(core * rows, 16)
    other = pl.multiple_of((1 - core) * rows, 16)
    depth = group.bits - 1
    top = 1 << depth
    copies, pushed = {}, {}

    def chunked(start, size, body):
        @pl.loop(0, size // 16)
        def _(i):
            body(pl.multiple_of(i * 16 + start, 16))

    def slot(position, index):
        return top - (top >> position) + (index >> position + 1)

    def push(piece, position, index):
        start, size, order = plan[piece]
        rest = index ^ 1 << position
        number = slot(position, rest)
        copy = pltpu.make_async_remote_copy(
            src_ref=stage.at[place_of(order, index) // 2, rows_at(own + start, size)],
            dst_ref=arrive.at[number, pl.ds(start, size)],
            send_sem=send.at[piece, number],
            recv_sem=recv.at[piece, number],
            device_id=group.partner(order[position]),
            device_id_type=MESH,
        )
        copy.start()
        pushed[piece, position, rest] = copy

    def summed(pair, r, slots):
        value = stage[pair, rows_at(own + r, 16)].astype(jnp.float32)
        for number in slots:
            value = value + arrive[number, rows_at(r, 16)].astype(jnp.float32)
        return value

    def settle(pair):
        copies[pair].wait_recv()

        def body(r):
            stage[pair, rows_at(own + r, 16)] = (
                stage[pair, rows_at(own + r, 16)].astype(jnp.float32)
                + core_in[pair, rows_at(r, 16)].astype(jnp.float32)
            ).astype(jnp.bfloat16)

        chunked(0, rows, body)
        for piece, (_, _, order) in enumerate(plan):
            for index in range(1, top, 2):
                if place_of(order, index) == 2 * pair:
                    push(piece, 0, index)

    before = None
    for pair in sorted(range(top), key=lambda pair: (-pair.bit_count(), -pair)):
        produce(jnp.bitwise_xor(me // 2, pair), stage.at[pair])
        copies[pair] = pltpu.make_async_remote_copy(
            src_ref=stage.at[pair, rows_at(other, rows)],
            dst_ref=core_in.at[pair],
            send_sem=core_send.at[pair],
            recv_sem=core_recv.at[pair],
            device_id=group.partner(0),
            device_id_type=MESH,
        )
        copies[pair].start()
        if before is not None:
            settle(before)
        before = pair
    settle(before)
    yield
    final = {}
    for position in range(1, depth):
        for index in reversed(range(1 << position, top, 2 << position)):
            for piece, (start, size, order) in enumerate(plan):
                pair = place_of(order, index) // 2
                slots = [slot(p, index) for p in range(position)]
                for p in range(position):
                    pushed[piece, p, index].wait_recv()
                if position < depth - 1:

                    def keep(r):
                        stage[pair, rows_at(own + r, 16)] = summed(pair, r, slots).astype(
                            jnp.bfloat16
                        )

                    chunked(start, size, keep)
                    push(piece, position, index)
                else:

                    def onward(r):
                        last_out[rows_at(r, 16)] = summed(pair, r, slots).astype(jnp.bfloat16)

                    chunked(start, size, onward)
                    final[piece] = pltpu.make_async_remote_copy(
                        src_ref=last_out.at[pl.ds(start, size)],
                        dst_ref=last_in.at[pl.ds(start, size)],
                        send_sem=last_send.at[piece],
                        recv_sem=last_recv.at[piece],
                        device_id=group.partner(order[position]),
                        device_id_type=MESH,
                    )
                    final[piece].start()
        if position < depth - 1:
            yield
    slots = [slot(p, 0) for p in range(depth - 1)]
    for piece, (start, size, _) in enumerate(plan):
        for p in range(depth - 1):
            pushed[piece, p, 0].wait_recv()

        def gathered(r):
            total[rows_at(r, 16)] = summed(0, r, slots)

        chunked(start, size, gathered)
    for some in (copies, pushed):
        for copy in some.values():
            copy.wait_send()
    yield
    for piece, (start, size, _) in enumerate(plan):
        final[piece].wait_recv()

        def finished(r):
            total[rows_at(r, 16)] += last_in[rows_at(r, 16)].astype(jnp.float32)

        chunked(start, size, finished)
    for copy in final.values():
        copy.wait_send()
    yield


def scatter_scratch(rows, width):
    return [
        pltpu.VMEM((8, 2 * rows, width), jnp.bfloat16),
        pltpu.VMEM((8, rows, width), jnp.bfloat16),
        pltpu.VMEM((6, rows, width), jnp.bfloat16),
        pltpu.VMEM((rows, width), jnp.bfloat16),
        pltpu.VMEM((rows, width), jnp.bfloat16),
    ]


def scatter_sems():
    count = PLAN_PIECES
    return [
        pltpu.SemaphoreType.DMA((8,)),
        pltpu.SemaphoreType.DMA((8,)),
        pltpu.SemaphoreType.DMA((count, 6)),
        pltpu.SemaphoreType.DMA((count, 6)),
        pltpu.SemaphoreType.DMA((count,)),
        pltpu.SemaphoreType.DMA((count,)),
    ]


def loop_rows(count, size, body):
    @pl.loop(0, count // size)
    def _(i):
        body(pl.ds(pl.multiple_of(i * size, size), size))


class Sizes:
    def __init__(self, layout, tokens, block_ids, w_query, w_gate):
        self.rows, self.width = tokens.shape[1], tokens.shape[2]
        self.length = block_ids.shape[1]
        self.depth = w_query.shape[0]
        self.hidden = w_gate.shape[1] // layout.mlp.count
        self.heads = H // layout.attn.count
        self.query = self.heads * HD
        self.attn = 2 * self.query + 2 * HD
        self.mlp_rows = layout.mlp.count * self.rows
        self.attn_rows = layout.attn.count * self.rows
        self.span = max(128, min(self.length, 256 * 512 // self.length))
        self.kv_share = max(1, layout.attn.count // KVH)
        self.kv_columns = max(1, layout.attn.share // self.kv_share) * HD
        self.attn_joined = 2 * layout.attn.share * self.query + 2 * self.kv_columns


def kv_half(sizes, target, chunk):
    second = (target // sizes.kv_share) % 2 == 1
    return jnp.where(second, chunk[:, HD:], chunk[:, :HD])


def attention_scores(sizes, qkv, ids, seq, start, head):
    base = sizes.query
    keys_rows = rows_at(seq * sizes.length, sizes.length)
    query_rows = rows_at(seq * sizes.length + start, sizes.span)
    query = qkv[query_rows, head * HD : (head + 1) * HD]
    keys = qkv[keys_rows, base : base + HD]
    values = qkv[keys_rows, base + HD : base + 2 * HD]
    key_ids = ids[seq, 0:1, :]
    query_ids = jnp.transpose(ids[seq, :, pl.ds(start, sizes.span)])[:, :1]
    return query, keys, values, softmax(query, keys, query_ids, key_ids)


def seq_gather(layout, out_ref, width, sems):
    send, recv = sems
    me = lax.axis_index("seq")
    bits = [1 << bit for bit in reversed(range(layout.seq_bits))]

    def block(mask):
        start = jnp.bitwise_xor(me, mask) * width
        return out_ref.at[:, pl.ds(pl.multiple_of(start, 128), width)]

    copies = {}

    def push(mask, bit):
        copy = pltpu.make_async_remote_copy(
            src_ref=block(mask),
            dst_ref=block(mask),
            send_sem=send.at[mask ^ bit],
            recv_sem=recv.at[mask ^ bit],
            device_id=offset(bit, 0),
            device_id_type=MESH,
        )
        copy.start()
        copies[mask ^ bit] = copy

    for bit in bits:
        push(0, bit)
    yield
    held = [0]
    for bit in bits:
        for mask in held[1:]:
            push(mask, bit)
        new = [mask ^ bit for mask in held]
        if bit != bits[-1]:
            for mask in new:
                copies[mask].wait_recv()
        held = held + new
    yield
    for mask in held[len(held) // 2 :]:
        copies[mask].wait_recv()
    for copy in copies.values():
        copy.wait_send()
    yield


def layer_kernel(
    layout,
    sizes,
    tok_ref,
    cot_ref,
    ids_ref,
    gains_ref,
    wq_ref,
    wk_ref,
    wv_ref,
    wo_ref,
    wg_ref,
    wu_ref,
    wd_ref,
    mixed,
    grad_tok,
    gain_sum,
    gate_out,
    up_out,
    down_out,
    attn_out,
    gate_recv,
    up_recv,
    down_recv,
    attn_recv_hbm,
    h1_out,
    g_all,
    h_all,
    w_in,
    w_down,
    wa,
    qkv,
    attended,
    hid,
    grad_in,
    middle,
    total,
    grad_mid,
    tok,
    down_stage,
    gains,
    ids,
    grad_kv,
    terms,
    gain_in,
    gain_seq,
    own_sum,
    stage,
    core_in,
    arrive,
    last_out,
    last_in,
    down_total,
    down_last_out,
    down_last_in,
    x_send,
    x_recv,
    x_relay,
    x_own,
    h_send,
    h_recv,
    h_relay,
    h_own,
    g_send,
    g_recv,
    g_relay,
    g_own,
    core_send,
    core_recv,
    s_send,
    s_recv,
    last_send,
    last_recv,
    down_last_send,
    down_last_recv,
    credit,
    ready,
    attn_send,
    attn_recv,
    gain_send,
    gain_recv,
    id_send,
    id_recv,
    mlp_send,
    mlp_recv,
    load_sem,
    grad_send,
    grad_recv,
    join_send,
    join_recv,
    own_sem,
    sum_send,
    sum_recv,
    gs_send,
    gs_recv,
    pick_sem,
):
    share, fsdp, depth = layout.attn.share, layout.fsdp, sizes.depth
    mlp_share = layout.mlp.share
    seq_me, fsdp_me = lax.axis_index("seq"), lax.axis_index("fsdp")
    query = sizes.query
    rows, hidden = sizes.rows, sizes.hidden

    count, few = sizes.mlp_rows, sizes.attn_rows
    near = pl.ds(0, few)
    wq = grad_in.at[pl.ds(0, depth), pl.ds(0, share * query)]
    wo = grad_in.at[pl.ds(depth, depth), pl.ds(0, share * query)]
    wk = grad_in.at[pl.ds(0, depth), pl.ds(hidden, 128)]
    wv = grad_in.at[pl.ds(depth, depth), pl.ds(hidden, 128)]
    pack = [grad_in.at[pl.ds((2 + j) * depth, depth), pl.ds(0, sizes.attn)] for j in range(share)]

    def tell(sem):
        for bit in range(layout.mlp.bits):
            pl.semaphore_signal(
                sem, inc=1, device_id=layout.mlp.partner(bit), device_id_type=MESH
            )

    loads = []

    def load(src, dst):
        copy = pltpu.make_async_copy(src, dst, load_sem.at[len(loads)])
        copy.start()
        loads.append(copy)
        return copy

    def columns(ref, start, size):
        return ref.at[:, pl.ds(pl.multiple_of(start, 128), size)]

    load(tok_ref, tok)
    own_rows = pl.ds(pl.multiple_of(fsdp_me * depth, 128), depth)
    load(gains_ref, gains.at[:, own_rows])
    load(columns(wq_ref, seq_me * share * query, share * query), wq)
    load(columns(wo_ref, seq_me * share * query, share * query), wo)
    chunk = seq_me * share // (2 * sizes.kv_share) * 128
    load(columns(wk_ref, chunk, 128), wk)
    load(columns(wv_ref, chunk, 128), wv)
    load(ids_ref, ids.at[fsdp_me % share])
    load(cot_ref, down_last_out)
    greet_all(layout)
    small = []
    for mask in range(1, fsdp):
        copy = pltpu.make_async_remote_copy(
            src_ref=gains_ref,
            dst_ref=gains.at[:, own_rows],
            send_sem=gain_send.at[mask],
            recv_sem=gain_recv.at[mask],
            device_id=offset(0, mask),
            device_id_type=MESH,
        )
        copy.start()
        small.append(copy)
    for copy in loads:
        copy.wait()
    for j in range(share):
        target = seq_me * share + j
        pack[j][...] = jnp.concatenate(
            [
                wq[:, j * query : (j + 1) * query],
                kv_half(sizes, target, wk[...]),
                kv_half(sizes, target, wv[...]),
                wo[:, j * query : (j + 1) * query],
            ],
            axis=1,
        )
    def packed(j):
        start = pl.multiple_of((2 + j) * depth, 128)
        return grad_in.at[pl.ds(start, depth), pl.ds(0, sizes.attn)]

    attn = {}

    def send_attn(number, src, place, hop):
        attn[number] = pltpu.make_async_remote_copy(
            src_ref=src,
            dst_ref=wa.at[place],
            send_sem=attn_send.at[number],
            recv_sem=attn_recv.at[number],
            device_id=offset(0, hop),
            device_id_type=MESH,
        )
        attn[number].start()

    for mask in (4, 5, 3, 2, 1):
        send_attn(mask, packed(jnp.bitwise_xor(fsdp_me, mask) % share), own_rows, mask)
    wa[own_rows] = packed(fsdp_me % share)[...]
    for copy in small:
        copy.wait()
    gain_one = gains[0:1].astype(jnp.float32)

    def norm(r):
        values = tok[r].astype(jnp.float32)
        grad_tok[r] = (values * rms_factor(values) * gain_one).astype(jnp.bfloat16)

    loop_rows(rows, 32, norm)
    x_steps = gather_steps(
        layout.attn, rows, attn_plan(layout.attn, ((2, 1), (2, 1))), grad_tok, h_all.at[near], (x_send, x_recv, x_relay, x_own)
    )
    next(x_steps)
    id_copies = []
    for mask in range(1, share):
        copy = pltpu.make_async_remote_copy(
            src_ref=ids_ref,
            dst_ref=ids.at[fsdp_me % share],
            send_sem=id_send.at[mask],
            recv_sem=id_recv.at[mask],
            device_id=offset(0, mask),
            device_id_type=MESH,
        )
        copy.start()
        id_copies.append(copy)
    g_steps = gather_steps(
        layout.mlp, rows, MLP_GATHER, cot_ref, g_all, (g_send, g_recv, g_relay, g_own)
    )
    next(g_steps)
    for _ in range(FIRST_STAGES):
        next(x_steps)
    for mask in (4, 5):
        attn[mask].wait_recv()
        start = jnp.bitwise_xor(fsdp_me, mask) * depth
        far_rows = pl.ds(pl.multiple_of(start, 128), depth)
        send_attn(mask ^ 2, wa.at[far_rows], far_rows, 2)

    mlp = []

    def send_mlp(ref, out, place, index, masks):
        def at(j):
            return columns(ref, (seq_me * mlp_share + j) * hidden, hidden)

        home = out.at[own_rows, pl.ds(place, hidden)]
        for mask in masks:
            if mask:
                copy = pltpu.make_async_remote_copy(
                    src_ref=at(jnp.bitwise_xor(fsdp_me, mask) % mlp_share),
                    dst_ref=home,
                    send_sem=mlp_send.at[index, mask],
                    recv_sem=mlp_recv.at[index, mask],
                    device_id=offset(0, mask),
                    device_id_type=MESH,
                )
            else:
                copy = pltpu.make_async_copy(at(fsdp_me % mlp_share), home, load_sem.at[1 + index])
            copy.start()
            mlp.append(copy)

    def send_weights(masks):
        masks = list(masks)
        send_mlp(wg_ref, w_in, 0, 0, masks)
        send_mlp(wu_ref, w_in, hidden, 1, masks)
        send_mlp(wd_ref, w_down, 0, 2, masks)

    send_weights(reversed(range(fsdp)))
    finish(x_steps)
    h1_copy = pltpu.make_async_copy(h_all.at[near], h1_out, load_sem.at[0])
    h1_copy.start()
    next(g_steps)
    for mask, copy in attn.items():
        copy.wait_send()
        if mask not in (4, 5):
            copy.wait_recv()

    def project(r):
        qkv[r] = dot(h_all[r], wa[:, : query + 2 * HD]).astype(jnp.bfloat16)

    loop_rows(sizes.attn_rows, 256, project)
    next(g_steps)
    for copy in id_copies:
        copy.wait()

    blocks = sizes.length // sizes.span

    @pl.loop(0, share * blocks)
    def _(i):
        seq = i // blocks
        start = pl.multiple_of((i % blocks) * sizes.span, sizes.span)
        outs = []
        for head in range(sizes.heads):
            _, _, values, probs = attention_scores(sizes, qkv, ids, seq, start, head)
            outs.append(dot(probs.astype(jnp.bfloat16), values))
        attended[rows_at(seq * sizes.length + start, sizes.span)] = jnp.concatenate(
            outs, axis=1
        ).astype(jnp.bfloat16)

    h1_copy.wait()
    tell(ready)

    def out_rows(pair, ref):
        block = attended[rows_at(pair * 2 * rows, 2 * rows)]

        @pl.loop(0, sizes.width // 512)
        def _(i):
            piece = pl.ds(pl.multiple_of(i * 512, 512), 512)
            ref[:, piece] = dot_cols(block, wa[piece, query + 2 * HD :]).astype(jnp.bfloat16)

    next(g_steps)
    next(g_steps)
    steps = scatter_steps(
        layout.attn, rows, attn_plan(layout.attn), out_rows, middle, (stage, core_in, arrive),
        (last_out, last_in), (core_send, core_recv, s_send, s_recv, last_send, last_recv),
    )
    next(steps)
    next(g_steps)
    finish(steps)
    gain_two = gains[8:9].astype(jnp.float32)

    def second(r):
        values = tok[r].astype(jnp.float32) + RESIDUAL * middle[r]
        middle[r] = values
        grad_tok[r] = (values * rms_factor(values) * gain_two).astype(jnp.bfloat16)

    loop_rows(rows, 32, second)
    pl.semaphore_wait(ready, layout.mlp.bits)
    h_steps = gather_steps(
        layout.mlp, rows, MLP_GATHER, grad_tok, h_all, (h_send, h_recv, h_relay, h_own)
    )
    next(h_steps)
    next(h_steps)
    finish(g_steps)
    finish(h_steps)
    for copy in mlp:
        copy.wait()

    base = query + 2 * HD
    scatter = (stage, core_in, arrive)
    sems = (core_send, core_recv, s_send, s_recv)
    scatter_sem = sems + (last_send, last_recv)
    spare = few < count

    def piece_at(ref, mask):
        column = pl.ds(mask // 4 * sizes.attn, sizes.attn)
        return ref.at[pl.ds(mask % 4 * depth, depth), column]

    def staged(mask):
        if spare:
            return piece_at(h_all.at[pl.ds(few, few)], mask)
        return w_down.at[block(mask), pl.ds(0, sizes.attn)]

    if spare:
        own_sum = g_all.at[pl.ds(few, depth)]

    def hidden_rows(r):
        h = h_all[r]
        gate = dot(h, w_in[:, :hidden])
        upward = dot(h, w_in[:, hidden:])
        grad = (RESIDUAL * g_all[r].astype(jnp.float32)).astype(jnp.bfloat16)
        g_all[r] = grad
        grad_hidden = dot(grad, w_down[...])
        sigma = jax.nn.sigmoid(gate)
        hid[r] = (gate * sigma * upward).astype(jnp.bfloat16)
        grad_in[r, hidden:] = (grad_hidden * gate * sigma).astype(jnp.bfloat16)
        grad_in[r, :hidden] = (
            grad_hidden * upward * sigma * (1.0 + gate * (1.0 - sigma))
        ).astype(jnp.bfloat16)

    loop_rows(count, 256, hidden_rows)

    sends = []
    far = list(reversed(range(1, fsdp))) + [0]

    def owner_columns(mask):
        start = jnp.bitwise_xor(fsdp_me, mask) * depth
        return pl.ds(pl.multiple_of(start, 128), depth)

    def send_grad(mask, src, dst, index):
        if mask == 0:
            return
        copy = pltpu.make_async_remote_copy(
            src_ref=src,
            dst_ref=dst.at[mask],
            send_sem=grad_send.at[index, mask],
            recv_sem=grad_recv.at[index, mask],
            device_id=offset(0, mask),
            device_id_type=MESH,
        )
        copy.start()
        sends.append((index, mask, copy))

    def block(mask):
        return pl.ds(mask * depth, depth)

    def grad_down(mask):
        down_stage[block(mask)] = dot_rows(g_all[:, owner_columns(mask)], hid[...]).astype(
            jnp.bfloat16
        )
        send_grad(mask, down_stage.at[block(mask)], down_recv, 0)

    for mask in far:
        grad_down(mask)

    def hidden_back(pair, ref):
        left = grad_in[rows_at(pair * 2 * rows, 2 * rows)]

        @pl.loop(0, sizes.width // 512)
        def _(i):
            piece = pl.ds(pl.multiple_of(i * 512, 512), 512)
            ref[:, piece] = dot_cols(left, w_in[piece]).astype(jnp.bfloat16)

    steps = scatter_steps(layout.mlp, rows, MLP_SCATTER, hidden_back, total, scatter, (last_out, last_in), scatter_sem)
    next(steps)

    def grad_up(mask):
        w_in[block(mask)] = dot_rows(h_all[:, owner_columns(mask)], grad_in[...]).astype(
            jnp.bfloat16
        )

    for turn in range(3):
        for mask in far[turn * 3 : turn * 3 + 3]:
            grad_up(mask)
        next(steps)
    finish(steps)
    h1_copy = pltpu.make_async_copy(h1_out, h_all.at[near], load_sem.at[0])
    h1_copy.start()
    terms[...] = jnp.zeros_like(terms)

    def norm_two(r):
        values, normed = middle[r], total[r]
        factor = rms_factor(values)
        terms[1:2] += jnp.sum(normed * values * factor, axis=0, keepdims=True)
        grad = down_last_out[r].astype(jnp.float32) + norm_back(normed, values, factor, gain_two)
        grad_mid[r] = grad
        last_out[r] = (RESIDUAL * grad).astype(jnp.bfloat16)

    loop_rows(rows, 32, norm_two)
    def collect(index, share, src, width, own_piece, landing, combine, out, out_width):
        picks = []
        for number, mask, copy in sends:
            if number == index:
                copy.wait_recv()
                pick = pltpu.make_async_copy(
                    src.at[mask], landing(mask), pick_sem.at[index, mask]
                )
                pick.start()
                picks.append(pick)
        yield
        for pick in picks:
            pick.wait()

        def terms_of(low, start, size):
            cols = pl.ds(start, size)
            value = own_piece[:, cols] if low == 0 else landing(low)[:, cols]
            value = value.astype(jnp.float32)
            for mask in range(low + share, fsdp, share):
                value = value + landing(mask)[:, cols].astype(jnp.float32)
            return value

        combine(terms_of, share, width)
        home = pl.multiple_of(seq_me * out_width, 128)
        local = pltpu.make_async_copy(
            own_sum.at[:, pl.ds(0, out_width)], out.at[:, pl.ds(home, out_width)], own_sem.at[index]
        )
        local.start()
        local.wait()
        yield from seq_gather(layout, out, out_width, (join_send.at[index], join_recv.at[index]))

    def place_columns(terms_of, share, width):
        mine = fsdp_me % share
        for low in range(share):
            start = pl.multiple_of(jnp.bitwise_xor(mine, low) * width, 128)
            own_sum[:, pl.ds(start, width)] = terms_of(low, 0, width).astype(jnp.bfloat16)

    def place_attn(terms_of, share, width):
        mine = fsdp_me % share
        for low in range(share):
            for source, target in ((0, 0), (base, share * query)):
                start = pl.multiple_of(target + jnp.bitwise_xor(mine, low) * query, 128)
                own_sum[:, pl.ds(start, query)] = terms_of(low, source, query).astype(
                    jnp.bfloat16
                )
        both = sizes.kv_columns
        at = 2 * share * query
        for source in (query, query + HD):
            heads = []
            for first in range(0, share, sizes.kv_share):
                value = terms_of(first, source, HD)
                for low in range(first + 1, min(share, first + sizes.kv_share)):
                    value = value + terms_of(low, source, HD)
                heads.append(value)
            value = heads[0]
            if len(heads) == 2:
                upper = mine // sizes.kv_share == 1
                value = jnp.concatenate(
                    [jnp.where(upper, heads[1], heads[0]), jnp.where(upper, heads[0], heads[1])],
                    axis=1,
                )
            own_sum[:, at : at + both] = value.astype(jnp.bfloat16)
            at += both

    mlp_share, attn_share = layout.mlp.share, layout.attn.share
    joined = mlp_share * hidden
    steps_down = collect(
        0, mlp_share, down_recv, hidden, down_stage.at[block(0)],
        lambda mask: grad_in.at[block(mask), pl.ds(0, hidden)],
        place_columns, down_out, joined,
    )
    a_steps = gather_steps(
        layout.attn, rows, attn_plan(layout.attn, ((2, 1), (2, 1))), last_out, g_all.at[near], (x_send, x_recv, x_relay, x_own)
    )
    next(a_steps)
    next(a_steps)
    for mask in far:
        send_grad(mask, w_in.at[block(mask), pl.ds(0, hidden)], gate_recv, 1)
    for mask in far:
        send_grad(mask, w_in.at[block(mask), pl.ds(hidden, hidden)], up_recv, 2)
    next(steps_down)
    finish(a_steps)

    def down_rows(pair, ref):
        left = hid[rows_at(pair * 2 * rows, 2 * rows)]

        @pl.loop(0, sizes.width // 512)
        def _(i):
            piece = pl.ds(pl.multiple_of(i * 512, 512), 512)
            ref[:, piece] = dot_cols(left, w_down[piece]).astype(jnp.bfloat16)

    steps_low = scatter_steps(
        layout.mlp, rows, MLP_SCATTER, down_rows, down_total, scatter, (down_last_out, down_last_in),
        sems + (down_last_send, down_last_recv),
    )
    next(steps_low)


    blocks = sizes.length // sizes.span

    def attend_back_block(i):
        seq = i // blocks
        part = i % blocks
        start = pl.multiple_of(part * sizes.span, sizes.span)
        here = rows_at(seq * sizes.length + start, sizes.span)
        grad_out = dot(g_all[here], wa[:, base:]).astype(jnp.bfloat16)
        grads, grad_keys, grad_values = [], 0.0, 0.0
        for head in range(sizes.heads):
            left, keys, values, probs = attention_scores(sizes, qkv, ids, seq, start, head)
            grad = grad_out[:, head * HD : (head + 1) * HD]
            grad_probs = dot_cols(grad, values)
            centre = jnp.sum(probs * grad_probs, axis=1, keepdims=True)
            grad_scores = (probs * (grad_probs - centre)).astype(jnp.bfloat16)
            grads.append(dot(grad_scores, keys) * (1.0 / HD))
            grad_keys = grad_keys + dot_rows(grad_scores, left) * (1.0 / HD)
            grad_values = grad_values + dot_rows(probs.astype(jnp.bfloat16), grad)
        both = jnp.concatenate([grad_keys, grad_values], axis=1)

        @pl.when(part == 0)
        def _():
            grad_kv[...] = both

        @pl.when(part > 0)
        def _():
            grad_kv[...] += both

        qkv[here, :query] = jnp.concatenate(grads, axis=1).astype(jnp.bfloat16)

        @pl.when(part == blocks - 1)
        def _():
            qkv[rows_at(seq * sizes.length, sizes.length), query:] = grad_kv[...].astype(
                jnp.bfloat16
            )

    turns = layout.attn.share * blocks

    @pl.loop(0, turns // 2)
    def _(i):
        attend_back_block(i)

    next(steps_down)
    next(steps_low)

    @pl.loop(turns // 2, turns)
    def _(i):
        attend_back_block(i)

    next(steps_low)
    tell(credit)
    next(steps_down)
    steps_gate = collect(
        1, mlp_share, gate_recv, hidden, w_in.at[block(0), pl.ds(0, hidden)],
        lambda mask: grad_in.at[block(mask), pl.ds(0, hidden)],
        place_columns, gate_out, joined,
    )
    next(steps_gate)
    next(steps_gate)
    pl.semaphore_wait(credit, layout.mlp.bits)

    def qkv_back(pair, ref):
        left = qkv[rows_at(pair * 2 * rows, 2 * rows)]

        @pl.loop(0, sizes.width // 512)
        def _(i):
            piece = pl.ds(pl.multiple_of(i * 512, 512), 512)
            ref[:, piece] = dot_cols(left, wa[piece, :base]).astype(jnp.bfloat16)

    h1_copy.wait()

    def grad_attn(mask):
        cols = owner_columns(mask)
        staged(mask)[:, :base] = dot_rows(h_all[near, cols], qkv[...]).astype(jnp.bfloat16)
        staged(mask)[:, base:] = dot_rows(g_all[near, cols], attended[...]).astype(
            jnp.bfloat16
        )
        send_grad(mask, staged(mask), attn_recv_hbm, 3)

    for mask in far[: fsdp // 2]:
        grad_attn(mask)
    steps = scatter_steps(layout.attn, rows, attn_plan(layout.attn), qkv_back, total, scatter, (last_out, last_in), scatter_sem)
    next(steps)
    for mask in far[fsdp // 2 :]:
        grad_attn(mask)
    next(steps)
    next(steps_gate)
    finish(steps)

    def norm_one(r):
        values, normed = tok[r].astype(jnp.float32), total[r]
        factor = rms_factor(values)
        terms[0:1] += jnp.sum(normed * values * factor, axis=0, keepdims=True)
        grad = grad_mid[r] + norm_back(normed, values, factor, gain_one)
        grad_tok[r] = grad.astype(jnp.bfloat16)

    loop_rows(rows, 32, norm_one)
    finish(steps_low)

    def mix(r):
        mixed[r] = (middle[r] + RESIDUAL * down_total[r]).astype(jnp.bfloat16)

    loop_rows(rows, 32, mix)
    gain_copies = []
    for mask in range(1, fsdp):
        copy = pltpu.make_async_remote_copy(
            src_ref=terms.at[:, owner_columns(mask)],
            dst_ref=gain_in.at[mask],
            send_sem=sum_send.at[mask],
            recv_sem=sum_recv.at[mask],
            device_id=offset(0, mask),
            device_id_type=MESH,
        )
        copy.start()
        gain_copies.append(copy)

    steps_up = collect(
        2, mlp_share, up_recv, hidden, w_in.at[block(0), pl.ds(hidden, hidden)], lambda mask: grad_in.at[block(mask), pl.ds(hidden, hidden)],
        place_columns, up_out, joined,
    )
    next(steps_up)
    next(steps_up)
    steps_attn = collect(
        3, attn_share, attn_recv_hbm, sizes.attn, staged(0), functools.partial(piece_at, g_all),
        place_attn, attn_out, sizes.attn_joined,
    )
    next(steps_attn)
    next(steps_attn)
    next(steps_up)

    value = terms[:, owner_columns(0)]
    for copy in gain_copies:
        copy.wait()
    for mask in range(1, fsdp):
        value = value + gain_in[mask]
    for bit in range(layout.seq_bits):
        gain_seq[2 * bit] = value
        copy = pltpu.make_async_remote_copy(
            src_ref=gain_seq.at[2 * bit],
            dst_ref=gain_seq.at[2 * bit + 1],
            send_sem=gs_send.at[bit],
            recv_sem=gs_recv.at[bit],
            device_id=offset(1 << bit, 0),
            device_id_type=MESH,
        )
        copy.start()
        copy.wait()
        value = value + gain_seq[2 * bit + 1]
    gain_sum[...] = value
    for steps in (steps_attn, steps_down, steps_gate, steps_up):
        finish(steps)
    for _, _, copy in sends:
        copy.wait_send()


def layer(layout, sizes, *args):
    width, count, few = sizes.width, sizes.mlp_rows, sizes.attn_rows
    hbm, vmem = pl.BlockSpec(memory_space=pl.ANY), pl.BlockSpec(memory_space=pltpu.VMEM)
    share, depth, fsdp = layout.attn.share, sizes.depth, layout.fsdp
    joined = layout.mlp.share * sizes.hidden
    rows, hidden, base = sizes.rows, sizes.hidden, sizes.query + 2 * HD
    bf16, f32 = jnp.bfloat16, jnp.float32
    shapes = [
        ((rows, width), bf16, vmem),
        ((rows, width), bf16, vmem),
        ((8, depth), f32, vmem),
        ((depth, layout.seq * joined), bf16, hbm),
        ((depth, layout.seq * joined), bf16, hbm),
        ((depth, layout.seq * joined), bf16, hbm),
        ((depth, layout.seq * sizes.attn_joined), bf16, hbm),
        ((fsdp, depth, hidden), bf16, hbm),
        ((fsdp, depth, hidden), bf16, hbm),
        ((fsdp, depth, hidden), bf16, hbm),
        ((fsdp, depth, sizes.attn), bf16, hbm),
        ((few, width), bf16, hbm),
    ]
    dma = pltpu.SemaphoreType.DMA
    seq = layout.seq
    return pl.pallas_call(
        functools.partial(layer_kernel, layout, sizes),
        out_shape=[jax.ShapeDtypeStruct(shape, dtype) for shape, dtype, _ in shapes],
        in_specs=[hbm] * len(args),
        out_specs=[spec for _, _, spec in shapes],
        scratch_shapes=[
            pltpu.VMEM((count, width), bf16),
            pltpu.VMEM((count, width), bf16),
            pltpu.VMEM((width, 2 * hidden), bf16),
            pltpu.VMEM((width, hidden), bf16),
            pltpu.VMEM((width, sizes.attn), bf16),
            pltpu.VMEM((few, base), bf16),
            pltpu.VMEM((few, sizes.query), bf16),
            pltpu.VMEM((count, hidden), bf16),
            pltpu.VMEM((count, 2 * hidden), bf16),
            pltpu.VMEM((rows, width), f32),
            pltpu.VMEM((rows, width), f32),
            pltpu.VMEM((rows, width), f32),
            pltpu.VMEM((rows, width), bf16),
            pltpu.VMEM((width, hidden), bf16),
            pltpu.VMEM((16, width), bf16),
            pltpu.VMEM((share, 8, sizes.length), jnp.int32),
            pltpu.VMEM((sizes.length, 2 * HD), f32),
            pltpu.VMEM((8, width), f32),
            pltpu.VMEM((fsdp, 8, depth), f32),
            pltpu.VMEM((2 * layout.seq_bits, 8, depth), f32),
            pltpu.VMEM((depth, max(joined, sizes.attn_joined) if few == count else 128), bf16),
        ]
        + scatter_scratch(rows, width)
        + [
            pltpu.VMEM((rows, width), f32),
            pltpu.VMEM((rows, width), bf16),
            pltpu.VMEM((rows, width), bf16),
        ]
        + gather_sems() * 3
        + scatter_sems()
        + [dma((PLAN_PIECES,)), dma((PLAN_PIECES,))]
        + [pltpu.SemaphoreType.REGULAR, pltpu.SemaphoreType.REGULAR]
        + [dma((fsdp,)), dma((fsdp,)), dma((fsdp,)), dma((fsdp,))]
        + [dma((share,)), dma((share,)), dma((3, fsdp)), dma((3, fsdp)), dma((8,))]
        + [dma((4, fsdp)), dma((4, fsdp)), dma((4, seq)), dma((4, seq)), dma((4,))]
        + [dma((fsdp,)), dma((fsdp,)), dma((layout.seq_bits,)), dma((layout.seq_bits,))]
        + [dma((4, fsdp))],
        compiler_params=pltpu.CompilerParams(
            collective_id=1, has_side_effects=True, vmem_limit_bytes=125 * 512 * 1024
        ),
        name="layer",
    )(*args)


def body(
    tokens,
    block_ids,
    gain_attn,
    w_query,
    w_key,
    w_value,
    w_out,
    gain_mlp,
    w_gate,
    w_up,
    w_down,
    cotangent,
):
    layout = Layout(lax.axis_size("seq"), lax.axis_size("fsdp"))
    depth = w_gate.shape[0]
    sizes = Sizes(layout, tokens, block_ids, w_query, w_gate)
    gains_own = jnp.concatenate(
        [jnp.broadcast_to(gain[None], (8, depth)) for gain in (gain_attn, gain_mlp)], axis=0
    )
    ids_own = jnp.broadcast_to(block_ids, (8, block_ids.shape[1]))
    mixed, grad_tokens, gain_sum, grad_gate, grad_up, grad_down, grad_attn, *_ = layer(
        layout,
        sizes,
        tokens[0],
        cotangent[0],
        ids_own,
        gains_own,
        w_query,
        w_key,
        w_value,
        w_out,
        w_gate,
        w_up,
        w_down,
    )
    wide, narrow = layout.attn.share * sizes.query, sizes.kv_columns

    def joined(start, size):
        columns = [
            grad_attn[:, i * sizes.attn_joined + start : i * sizes.attn_joined + start + size]
            for i in range(layout.seq)
        ]
        return jnp.concatenate(columns, axis=1).astype(jnp.float32)

    def heads(start):
        columns = joined(start, narrow)
        if layout.seq * narrow > KVH * HD:
            columns = jnp.sum(columns.reshape(depth, KVH, -1, HD), axis=2).reshape(depth, -1)
        return columns

    return (
        mixed[None],
        grad_tokens[None],
        gain_sum[0],
        joined(0, wide),
        heads(2 * wide),
        heads(2 * wide + narrow),
        joined(wide, wide),
        gain_sum[1],
        grad_gate.astype(jnp.float32),
        grad_up.astype(jnp.float32),
        grad_down.astype(jnp.float32),
    )


def solution(mesh):
    tokens, rows = P("fsdp", "seq", None), P("fsdp", None)
    return jax.shard_map(
        body,
        mesh=mesh,
        in_specs=(tokens, rows, P("fsdp"), rows, rows, rows, rows, P("fsdp"), rows, rows, rows, tokens),
        out_specs=(tokens, tokens, P("fsdp"), rows, rows, rows, rows, P("fsdp"), rows, rows, rows),
        check_vma=False,
    )
```
